32 devices in a mesh: section: 4 (over y, x), space: 8 (over z, core).
Axes of the slice: x: 2, y: 2, z: 4, core: 2. Of those that a mesh axis runs over, the one named last changes fastest.
Arguments:
- video_clips: bfloat16 [4, 4, 32, 8, 512], P(None, None, 'space'), may hold values from -48 to 48
- code_bits: int32 [4, 1, 8, 2, 18], P(None, None, 'space'), may hold values 0 or 1
- recon_grad: bfloat16 [4, 4, 32, 8, 512], P(None, None, 'space'), may hold values from -14 to 14
- enc_convs: bfloat16 [2, 13824, 512], P(None, 'space'), may hold values from -0.0546875 to 0.0546875
- enc_gains: bfloat16 [2, 512], P(None, 'space'), may hold values from 0.099609375 to 1.8984375
- enc_shifts: bfloat16 [4, 512], P(None, 'space'), may hold values from -2.390625 to 2.390625
- down_weight: bfloat16 [32768, 512], P('space'), may hold values from -0.03125 to 0.03125
- down_bias: bfloat16 [512], P('space'), may hold values from -3 to 3
- down_proj: bfloat16 [512, 18], P('space'), may hold values from -0.25 to 0.25
- up_proj: bfloat16 [512, 18], P('space'), may hold values from -1.5 to 1.5
- up_bias: bfloat16 [512], P('space'), may hold values from -3 to 3
- up_weight: bfloat16 [32768, 512], P('space'), may hold values from -0.25 to 0.25
- upsample_bias: bfloat16 [32768], P('space'), may hold values from -3 to 3
- dec_convs: bfloat16 [2, 13824, 512], P(None, 'space'), may hold values from -0.0546875 to 0.0546875
- dec_gains: bfloat16 [2, 512], P(None, 'space'), may hold values from 0.099609375 to 1.8984375
- dec_shifts: bfloat16 [4, 512], P(None, 'space'), may hold values from -2.390625 to 2.390625
Outputs:
- reconstruction: bfloat16 [4, 4, 32, 8, 512], P(None, None, 'space', None, 'section')
- video_grad: bfloat16 [4, 4, 32, 8, 512], P(None, None, 'space', None, 'section')
- enc_convs_grad: float32 [2, 13824, 512], P(None, 'space')
- enc_gains_grad: float32 [2, 512], P(None, 'space')
- enc_shifts_grad: float32 [4, 512], P(None, 'space')
- down_weight_grad: float32 [32768, 512], P('space')
- down_bias_grad: float32 [512], P('space')
- down_proj_grad: float32 [512, 18], P('space')
- up_proj_grad: float32 [512, 18], P('space')
- up_bias_grad: float32 [512], P('space')
- up_weight_grad: float32 [32768, 512], P('space')
- upsample_bias_grad: float32 [32768], P('space')
- dec_convs_grad: float32 [2, 13824, 512], P(None, 'space')
- dec_gains_grad: float32 [2, 512], P(None, 'space')
- dec_shifts_grad: float32 [4, 512], P(None, 'space')
The draws below stay inside these ranges and needn't reach their ends.
All inputs are finite; a program needn't handle non-finite values. No bound on the sum of `code_bits` on one device may be relied on, other than what follows from the above.
Results may differ from the reference program's by a relative error of at most 0.014.
Values may be sent and summed in bfloat16 or wider, within the bound.
No kernel may reach another device: no remote copies, remote signals or barrier semaphores. Data moves between devices by JAX's collectives and lax.ppermute only.
A program may use at most 512 MiB of HBM per device.

```python
import jax
import jax.numpy as jnp
from jax import lax

C = 512
GROUPS = 32
BITS = 18
MB = 4
FR = 4
WID = 8
H = 32


def rising_rows(count, stretch):
    return jnp.exp(stretch * jnp.arange(count, dtype=jnp.float32) / (count - 1))


def draw_video_clips(key, part):
    key = jax.random.fold_in(key, 11)
    noise_key, voxel_key, chan_key, mean_key = jax.random.split(key, 4)
    full_shape = (MB, FR, H, WID, C)
    voxel_scale = jnp.exp(jax.random.uniform(voxel_key, (MB, FR, H, WID, 1), minval=0.0, maxval=1.25))
    channel_scale = jnp.exp(jax.random.uniform(chan_key, (1, 1, 1, 1, C), minval=-0.9, maxval=1.4))
    offset = jax.random.uniform(mean_key, (1, 1, 1, 1, C), minval=-0.5, maxval=0.5)
    noise = jax.random.truncated_normal(noise_key, -4.0, 4.0, full_shape)
    row_scale = rising_rows(H, 1.0986)
    values = 0.25 * (noise + offset) * row_scale[None, None, :, None, None] * voxel_scale * channel_scale
    return values.astype(jnp.bfloat16)


def draw_recon_grad(key, part):
    key = jax.random.fold_in(key, 23)
    noise_key, voxel_key, mean_key = jax.random.split(key, 3)
    full_shape = (MB, FR, H, WID, C)
    voxel_scale = jnp.exp(jax.random.uniform(voxel_key, (MB, FR, H, WID, 1), minval=0.0, maxval=0.7))
    offset = jax.random.uniform(mean_key, (1, 1, 1, 1, C), minval=-0.6, maxval=0.6)
    noise = jax.random.truncated_normal(noise_key, -4.0, 4.0, full_shape)
    row_scale = rising_rows(H, 1.0986)
    values = 0.5 * (noise + offset) * row_scale[None, None, :, None, None] * voxel_scale
    return values.astype(jnp.bfloat16)


def set_ends(result, rng, least, top_value):
    spot = [jax.random.randint(jax.random.fold_in(rng, axis), (), 0, length) for axis, length in enumerate(result.shape)]
    widest = result.shape.index(max(result.shape))
    next_to = spot[:widest] + [(spot[widest] + 1) % result.shape[widest]] + spot[widest + 1:]
    return result.at[tuple(spot)].set(least).at[tuple(next_to)].set(top_value)


def levels(stream_key, dims, pieces, least, high):
    level, own = 1.0, jax.random.fold_in(stream_key, 6)
    for position, parts in pieces:
        steps = jnp.exp(jax.random.uniform(jax.random.fold_in(own, position), (parts,), jnp.float32, least / len(pieces), high / len(pieces)))
        level = level * jnp.repeat(steps, dims[position] // parts).reshape([-1 if axis == position else 1 for axis in range(len(dims))])
    return level


def scatter_about(own_key, shape, deviation, most, cuts=(), kind=jnp.bfloat16):
    level = levels(own_key, shape, cuts, -0.22, 0.18) if cuts else 1.0
    values = jax.random.normal(own_key, shape, jnp.float32) * deviation * level
    return jnp.minimum(jnp.maximum(values, -most), most).astype(kind)


def setup_inputs(seed: int = 0) -> dict:
    seeds = jax.random.split(jax.random.key(seed), 17)
    return {
        "video_clips": draw_video_clips(jax.random.fold_in(seeds[16], 71), 0),
        "code_bits": set_ends((jax.random.randint(seeds[1], (MB, FR // 4, H // 4, WID // 4, BITS), 0, 2) < 1).astype(jnp.int32), jax.random.fold_in(seeds[1], 1), 0, 1),
        "recon_grad": draw_recon_grad(jax.random.fold_in(seeds[16], 71), 0),
        "enc_convs": scatter_about(seeds[3], (2, 27 * C, C), (27 * C) ** -0.5, 0.0546875, ((1, 8),)),
        "enc_gains": jnp.clip(1.0 + 0.18 * jax.random.normal(seeds[4], (2, C), jnp.float32), 0.099609375, 1.8984375).astype(jnp.bfloat16),
        "enc_shifts": scatter_about(seeds[5], (4, C), 0.4, 2.390625, ((1, 8),)),
        "down_weight": scatter_about(seeds[6], (64 * C, C), (64 * C) ** -0.5, 0.03125, ((0, 8),)),
        "down_bias": scatter_about(seeds[7], (C,), 0.5, 3.0, ((0, 8),)),
        "down_proj": scatter_about(seeds[8], (C, BITS), C ** -0.5, 0.25, ((0, 8),)),
        "up_proj": scatter_about(seeds[9], (C, BITS), BITS ** -0.5, 1.5, ((0, 8),)),
        "up_bias": scatter_about(seeds[10], (C,), 0.5, 3.0, ((0, 8),)),
        "up_weight": scatter_about(seeds[11], (64 * C, C), C ** -0.5, 0.25, ((0, 8),)),
        "upsample_bias": scatter_about(seeds[12], (64 * C,), 0.5, 3.0, ((0, 8),)),
        "dec_convs": scatter_about(seeds[13], (2, 27 * C, C), (27 * C) ** -0.5, 0.0546875, ((1, 8),)),
        "dec_gains": jnp.clip(1.0 + 0.18 * jax.random.normal(seeds[14], (2, C), jnp.float32), 0.099609375, 1.8984375).astype(jnp.bfloat16),
        "dec_shifts": scatter_about(seeds[15], (4, C), 0.4, 2.390625, ((1, 8),)),
    }


@jax.custom_vjp
def low(v):
    return lax.optimization_barrier(v.astype(jnp.bfloat16)).astype(jnp.float32)

@jax.custom_vjp
def low_back(v):
    return v

def low_keep(v):
    return (low(v), None)

def low_pass(kept, grad):
    return (grad,)

def back_keep(v):
    return (v, None)

def back_low(kept, grad):
    return (low(grad),)
low.defvjp(low_keep, low_pass)
low_back.defvjp(back_keep, back_low)

def swish_of(values):
    return values * jax.nn.sigmoid(values)

def group_norm(values, gain_row, shift_row):
    grouped = values.reshape(values.shape[0], -1, GROUPS, values.shape[-1] // GROUPS)
    average = lax.optimization_barrier(jnp.mean(grouped, axis=(1, 3), keepdims=True))
    square = lax.optimization_barrier(jnp.mean(grouped * grouped, axis=(1, 3), keepdims=True))
    inv_spread = lax.rsqrt(square - average * average + 1e-06)
    return ((grouped - average) * inv_spread).reshape(values.shape) * gain_row + shift_row

@jax.checkpoint
def convolve(values, weight_rows):
    channels = values.shape[-1]
    frames, height, across = (values.shape[1], values.shape[2], values.shape[3])
    padded = jnp.pad(values, ((0, 0), (1, 1), (1, 1), (1, 1), (0, 0)))
    summed = jnp.zeros((values.shape[0] * frames * height * across, weight_rows.shape[1]), jnp.float32)
    for tap_index in range(27):
        frame_step = tap_index // 9
        row_step = tap_index // 3 % 3
        col_step = tap_index % 3
        window = padded[:, frame_step:frame_step + frames, row_step:row_step + height, col_step:col_step + across, :]
        summed = summed + jnp.dot(window.reshape(-1, channels), weight_rows[tap_index * channels:(tap_index + 1) * channels], precision=lax.Precision.HIGHEST)
    return summed.reshape(values.shape[:-1] + (weight_rows.shape[1],))

def residual_block(inputs, conv_weights, gain_rows, shift_rows):
    act_one = low(swish_of(group_norm(inputs, gain_rows[0], shift_rows[0])))
    middle = low_back(convolve(act_one, conv_weights[0]) + shift_rows[2])
    act_two = low(swish_of(group_norm(middle, gain_rows[1], shift_rows[1])))
    branch = low_back(convolve(act_two, conv_weights[1]) + shift_rows[3])
    return inputs + branch

def to_latent(full_field):
    extent = full_field.shape
    cubes = full_field.reshape(extent[0], extent[1] // 4, 4, extent[2] // 4, 4, extent[3] // 4, 4, extent[4])
    return cubes.transpose(0, 1, 3, 5, 2, 4, 6, 7).reshape(-1, 64 * extent[4])

def from_latent(latent_rows, extent):
    cubes = latent_rows.reshape(extent[0], extent[1] // 4, extent[2] // 4, extent[3] // 4, 4, 4, 4, extent[4])
    return cubes.transpose(0, 1, 4, 2, 5, 3, 6, 7).reshape(extent)

def decoder(sign_rows, up_proj, up_bias, up_weight, upsample_bias, dec_convs, dec_gains, dec_shifts):
    sign_rows = low_back(sign_rows)
    hidden = low(low_back(jnp.dot(sign_rows, up_proj.T, precision=lax.Precision.HIGHEST) + up_bias))
    grown = jnp.dot(hidden, up_weight.T, precision=lax.Precision.HIGHEST) + upsample_bias
    decoded_in = low_back(low(from_latent(grown, (MB, FR, H, WID, C))))
    return residual_block(decoded_in, dec_convs, dec_gains, dec_shifts)

def encoder(video, enc_convs, enc_gains, enc_shifts, down_weight, down_bias, down_proj):
    encoded = low_back(low(residual_block(video, enc_convs, enc_gains, enc_shifts)))
    inner = low(low_back(jnp.dot(to_latent(encoded), down_weight, precision=lax.Precision.HIGHEST) + down_bias))
    return jnp.dot(inner, down_proj, precision=lax.Precision.HIGHEST)

def widen(tensor):
    return tensor.astype(jnp.float32)

def reference(video_clips, code_bits, recon_grad, enc_convs, enc_gains, enc_shifts, down_weight, down_bias, down_proj, up_proj, up_bias, up_weight, upsample_bias, dec_convs, dec_gains, dec_shifts):
    sign_rows = (2 * code_bits - 1).astype(jnp.float32).reshape(-1, BITS)
    rebuilt, decoder_back = jax.vjp(decoder, sign_rows, widen(up_proj), widen(up_bias), widen(up_weight), widen(upsample_bias), widen(dec_convs), widen(dec_gains), widen(dec_shifts))
    dec_grads = decoder_back(widen(recon_grad))
    latent, encoder_back = jax.vjp(encoder, widen(video_clips), widen(enc_convs), widen(enc_gains), widen(enc_shifts), widen(down_weight), widen(down_bias), widen(down_proj))
    enc_grads = encoder_back(dec_grads[0])
    return (rebuilt.astype(jnp.bfloat16), enc_grads[0].astype(jnp.bfloat16), enc_grads[1], enc_grads[2], enc_grads[3], enc_grads[4], enc_grads[5], enc_grads[6], dec_grads[1], dec_grads[2], dec_grads[3], dec_grads[4], dec_grads[5], dec_grads[6], dec_grads[7])
```

```python
from functools import partial

import jax
import jax.numpy as jnp
from jax import lax
from jax.experimental import pallas as pl
from jax.experimental.pallas import tpu as pltpu
from jax.sharding import PartitionSpec as P

GROUPS = 32
CUBE = 4
LANES = 128
BF16 = jnp.bfloat16
F32 = jnp.float32


def swish_slope(values, logistic):
    return logistic * (1.0 + values * (1.0 - logistic))


def chips_of():
    return lax.axis_size("space") // 2


def along_chips(value, step):
    chips = chips_of()
    route = [(i, (i // 2 + step) % chips * 2 + i % 2) for i in range(2 * chips)]
    return lax.ppermute(value, "space", route)


def to_twin(value):
    return lax.ppermute(value, "space", [(i, i ^ 1) for i in range(lax.axis_size("space"))])


def here():
    index = lax.axis_index("space")
    return index // 2, index % 2


def ring_is_short():
    return chips_of() <= 4


def picked(value, index, axis=0):
    return lax.dynamic_index_in_dim(value, index, axis, keepdims=False)


def gathered(value):
    chips = chips_of()
    if not ring_is_short():
        return lax.all_gather(value, "space", axis=0).reshape((chips, 2) + value.shape)
    z, core = here()
    pieces = [value] + [along_chips(value, step) for step in range(1, chips)]
    stack = jnp.zeros((chips,) + value.shape, value.dtype)
    for step, piece in enumerate(pieces):
        stack = lax.dynamic_update_index_in_dim(stack, piece, (z - step) % chips, 0)
    other = to_twin(stack)
    first = jnp.where(core == 0, stack, other)
    second = jnp.where(core == 0, other, stack)
    return jnp.stack([first, second], axis=1)


def scattered(parts):
    chips = chips_of()
    if not ring_is_short():
        flat = parts.reshape((2 * chips,) + parts.shape[2:])
        return lax.psum_scatter(flat, "space", scatter_dimension=0, tiled=False)
    z, core = here()
    mine = picked(parts, core, 1)
    mine = mine + to_twin(picked(parts, 1 - core, 1).astype(BF16)).astype(F32)
    total = picked(mine, z)
    for step in range(1, chips):
        sent = picked(mine, (z + step) % chips).astype(BF16)
        total = total + along_chips(sent, step).astype(F32)
    return total


def summed(value):
    if not ring_is_short():
        return lax.psum(value, "space")
    total = value
    for step in range(1, chips_of()):
        total = total + along_chips(value, step)
    return total + to_twin(total)


def pair_summed(value):
    return value + to_twin(value)


def to_blocks(field):
    chips = chips_of()
    cubes, rows, channels = field.shape
    split = field.reshape(2, cubes // 2, rows, chips, channels // chips)
    return split.transpose(3, 0, 1, 2, 4)


def from_blocks(blocks):
    chips, _, half, rows, width = blocks.shape
    return blocks.transpose(1, 2, 3, 0, 4).reshape(2 * half, rows, chips * width)


def own_block(field):
    z, core = here()
    cubes, rows, channels = field.shape
    width = channels // chips_of()
    return lax.dynamic_slice(field, (core * (cubes // 2), 0, z * width), (cubes // 2, rows, width))


def own_lanes(row):
    z, _ = here()
    width = row.shape[-1] // chips_of()
    return lax.dynamic_slice_in_dim(row, z * width, width, row.ndim - 1)


def cubes_of(slab):
    frames, height, across, channels = slab.shape
    split = slab.reshape(frames, height, across // CUBE, CUBE, channels)
    return split.transpose(0, 1, 3, 2, 4).reshape(-1, across // CUBE, channels)


def slab_of(cubes, extent):
    frames, height, across, channels = extent
    split = cubes.reshape(frames, height, CUBE, across // CUBE, channels)
    return split.transpose(0, 1, 3, 2, 4).reshape(extent)


def field_of(slabs):
    chips, _, cubes, across, channels = slabs.shape
    flat = slabs.reshape(2 * chips, cubes, across, channels)
    return flat.transpose(1, 0, 2, 3).reshape(cubes, 2 * chips * across, channels)


def group_means(sums, width, members):
    groups = sums.reshape(sums.shape[:-1] + (-1, width))
    wide = jnp.broadcast_to(jnp.sum(groups, axis=-1, keepdims=True), groups.shape)
    return wide.reshape(sums.shape) / members


def rimmed(field, across):
    cubes, rows, channels = field.shape
    view = field.reshape(CUBE, CUBE, CUBE, rows // across, across, channels)
    none = (0, 0)
    above = jnp.pad(view[:, -1:, :, :-1], (none, none, none, (1, 0), none, none))
    below = jnp.pad(view[:, :1, :, 1:], (none, none, none, (0, 1), none, none))
    view = jnp.concatenate([above, view, below], axis=1)
    left = jnp.pad(view[:, :, -1:, :, :-1], (none, none, none, none, (1, 0), none))
    right = jnp.pad(view[:, :, :1, :, 1:], (none, none, none, none, (0, 1), none))
    view = jnp.concatenate([left, view, right], axis=2)
    view = jnp.pad(view, ((1, 1), none, none, none, none, none))
    return view.reshape(CUBE + 2, CUBE + 2, CUBE + 2, rows, channels)


def rows_here(weights):
    count = weights.shape[-2]
    start = count * lax.axis_index("space")
    return start // LANES, start % LANES


def block_count(count):
    worst = max(count * s % LANES for s in range(lax.axis_size("space")))
    return -(-(worst + count) // LANES)


def aligned(weights):
    _, offset = rows_here(weights)
    total = block_count(weights.shape[-2]) * LANES
    wide = jnp.zeros(weights.shape[:-2] + (total, weights.shape[-1]), weights.dtype)
    return lax.dynamic_update_slice_in_dim(wide, weights, offset, wide.ndim - 2)


def patches(field, first, count, across):
    cubes, rows, channels = field.shape
    wide = rimmed(field, across)
    per_tap = channels // LANES
    pieces = []
    for j in range(count):
        block = first + j
        tap, lane = jnp.minimum(block // per_tap, 26), block % per_tap
        piece = lax.dynamic_slice(
            wide,
            (tap // 9, tap // 3 % 3, tap % 3, 0, lane * LANES),
            (CUBE, CUBE, CUBE, rows, LANES),
        )
        pieces.append(piece.reshape(cubes * rows, LANES))
    return jnp.concatenate(pieces, axis=1)


def conv_part(field, weights, first, across):
    patch = patches(field, first, weights.shape[0] // LANES, across)
    out = jnp.dot(patch, weights, preferred_element_type=F32)
    return out.reshape(field.shape[:2] + (-1,)), patch


def convt_part(field, weights, first, across):
    cubes, rows, channels = field.shape
    spread = lax.dot_general(
        field.reshape(-1, channels),
        weights,
        (((1,), (1,)), ((), ())),
        preferred_element_type=F32,
    )
    count = weights.shape[0] // LANES
    fold = jax.linear_transpose(
        lambda v: patches(v, first, count, across),
        jax.ShapeDtypeStruct((cubes, rows, channels), F32),
    )
    return fold(spread)[0]


def kernel_grad(patch, field):
    return lax.dot_general(
        patch,
        field.reshape(-1, field.shape[-1]),
        (((0,), (0,)), ((), ())),
        preferred_element_type=F32,
    )


VMEM_BYTES = 56 * 1024 * 1024


def kernels_fit(channels):
    return chips_of() * LANES == channels


def shifted(slabs, rows, valid):
    wide = pltpu.roll(slabs.astype(F32), rows % slabs.shape[1], 1)
    return jnp.where(valid, wide, 0.0)


def row_marks(shape, across):
    row = lax.broadcasted_iota(jnp.int32, shape, len(shape) - 2)
    return row, row % across


def fill_rim(field, rim, across):
    rows, channels = field.shape[1:]
    tiles = channels // LANES
    blank = jnp.zeros((CUBE + 2, CUBE + 2, rows, LANES), rim.dtype)
    for q in range(tiles):
        rim[q, 0] = blank
        rim[q, CUBE + 1] = blank

    def frame(f, carry):
        base = f * CUBE * CUBE
        row, column = row_marks((CUBE, rows, LANES), across)
        row6, column6 = row_marks((CUBE + 2, rows, LANES), across)
        for q in range(tiles):
            lanes = slice(q * LANES, (q + 1) * LANES)
            for h in range(CUBE):
                rim[q, f + 1, h + 1, 1 : CUBE + 1] = field[pl.ds(base + CUBE * h, CUBE), :, lanes]
            above = field[pl.ds(base + CUBE * (CUBE - 1), CUBE), :, lanes]
            rim[q, f + 1, 0, 1 : CUBE + 1] = shifted(above, across, row >= across).astype(rim.dtype)
            below = field[pl.ds(base, CUBE), :, lanes]
            rim[q, f + 1, CUBE + 1, 1 : CUBE + 1] = shifted(
                below, -across, row < rows - across
            ).astype(rim.dtype)
            left = rim[q, f + 1, :, CUBE]
            rim[q, f + 1, :, 0] = shifted(left, 1, column6 >= 1).astype(rim.dtype)
            right = rim[q, f + 1, :, 1]
            rim[q, f + 1, :, CUBE + 1] = shifted(right, -1, column6 < across - 1).astype(rim.dtype)
        return carry

    lax.fori_loop(0, CUBE, frame, 0)


def fold_rim(rim, across):
    tiles, rows = rim.shape[0], rim.shape[4]

    def frame(f, carry):
        row, _ = row_marks((CUBE, rows, LANES), across)
        _, column6 = row_marks((CUBE + 2, rows, LANES), across)
        for q in range(tiles):
            left = shifted(rim[q, f + 1, :, 0], -1, column6 < across - 1)
            rim[q, f + 1, :, CUBE] += left
            right = shifted(rim[q, f + 1, :, CUBE + 1], 1, column6 >= 1)
            rim[q, f + 1, :, 1] += right
            above = shifted(rim[q, f + 1, 0, 1 : CUBE + 1], -across, row < rows - across)
            rim[q, f + 1, CUBE, 1 : CUBE + 1] += above
            below = shifted(rim[q, f + 1, CUBE + 1, 1 : CUBE + 1], across, row >= across)
            rim[q, f + 1, 1, 1 : CUBE + 1] += below
        return carry

    lax.fori_loop(0, CUBE, frame, 0)


def tap_of(block, per_tap):
    tap = jnp.minimum(block // per_tap, 26)
    return block % per_tap, tap // 9, tap // 3 % 3, tap % 3


def fill_patch(rim, patch, first, count, start, size):
    rows = rim.shape[4]
    for j in range(count):
        q, f, h, w = tap_of(first + j, rim.shape[0])
        window = rim[
            q,
            pl.ds(f + start[0], size[0]),
            pl.ds(h + start[1], size[1]),
            pl.ds(w, CUBE),
        ]
        patch[:, j * LANES : (j + 1) * LANES] = window.reshape(
            size[0] * size[1] * CUBE * rows, LANES
        )


def conv_kernel(by_cube, across, where, field, weights, keep, send, rim, patch):
    first, core = where[0], where[1]
    rows, channels = field.shape[1:]
    tiles = channels // LANES
    count = weights.shape[0] // LANES
    half = CUBE // 2
    fill_rim(field, rim, across)

    def part(which):
        start, size = ((0, half * which), (CUBE, half)) if by_cube else ((half * which, 0), (half, CUBE))
        fill_patch(rim, patch, first, count, start, size)
        return jnp.dot(patch[...], weights[...], preferred_element_type=F32)

    for target, which in ((send, 1 - core), (keep, core)):
        total = part(which).astype(target.dtype)
        if by_cube:
            target[...] = total.reshape(target.shape)
        else:
            for q in range(tiles):
                target[q] = total[:, q * LANES : (q + 1) * LANES].reshape(target.shape[1:])


def whole_spec():
    return pl.BlockSpec(memory_space=pltpu.VMEM)


def kernel_params():
    return pltpu.CompilerParams(vmem_limit_bytes=VMEM_BYTES)


def here_scalars(first):
    return jnp.stack([first, lax.axis_index("space") % 2]).astype(jnp.int32)


def conv_shares(field, weights, first, across, by_cube):
    cubes, rows, channels = field.shape
    count = weights.shape[0] // LANES
    tiles = channels // LANES
    if by_cube:
        shape = (CUBE, cubes // (2 * CUBE), rows, channels)
    else:
        shape = (tiles, cubes // 2, rows, LANES)
    work = cubes * rows * channels * weights.shape[0]
    return pl.pallas_call(
        partial(conv_kernel, by_cube, across),
        out_shape=(jax.ShapeDtypeStruct(shape, F32), jax.ShapeDtypeStruct(shape, BF16)),
        in_specs=[pl.BlockSpec(memory_space=pltpu.SMEM), whole_spec(), whole_spec()],
        out_specs=(whole_spec(), whole_spec()),
        scratch_shapes=[
            pltpu.VMEM((tiles, CUBE + 2, CUBE + 2, CUBE + 2, rows, LANES), BF16),
            pltpu.VMEM((cubes // 2 * rows, count * LANES), BF16),
        ],
        compiler_params=kernel_params(),
        cost_estimate=pl.CostEstimate(flops=2 * work, bytes_accessed=8 << 20, transcendentals=0),
        name="conv_part",
    )(here_scalars(first), field, weights)


def add_taps(field, weights, rim, first):
    rows, channels = field.shape[1:]
    tiles = channels // LANES
    count = weights.shape[0] // LANES
    blank = jnp.zeros((CUBE + 2, CUBE + 2, rows, LANES), F32)

    def clear(f, carry):
        for q in range(tiles):
            rim[q, f] = blank
        return carry

    lax.fori_loop(0, CUBE + 2, clear, 0)
    spread_rows = CUBE * CUBE * rows

    def frame(f, carry):
        source = field[pl.ds(f * CUBE * CUBE, CUBE * CUBE)].reshape(spread_rows, channels)
        for j in range(0, count, 2):
            wide = min(2, count - j)
            spread = lax.dot_general(
                source,
                weights[j * LANES : (j + wide) * LANES, :],
                (((1,), (1,)), ((), ())),
                preferred_element_type=F32,
            )
            for i in range(wide):
                q, tf, th, tw = tap_of(first + j + i, tiles)
                rim[q, f + tf, pl.ds(th, CUBE), pl.ds(tw, CUBE)] += spread[
                    :, i * LANES : (i + 1) * LANES
                ].reshape(CUBE, CUBE, rows, LANES)
        return carry

    lax.fori_loop(0, CUBE, frame, 0)


def convt_kernel(across, where, field, weights, keep, send, rim):
    first, core = where[0], where[1]
    add_taps(field, weights, rim, first)
    fold_rim(rim, across)
    half = CUBE // 2
    for q in range(rim.shape[0]):
        for target, which in ((send, 1 - core), (keep, core)):
            for f in range(half):
                target[q, pl.ds(f * CUBE * CUBE, CUBE * CUBE)] = (
                    rim[q, half * which + 1 + f, 1 : CUBE + 1, 1 : CUBE + 1]
                    .reshape((CUBE * CUBE,) + target.shape[2:])
                    .astype(target.dtype)
                )


def convt_whole_kernel(across, where, field, weights, out, rim):
    add_taps(field, weights, rim, where[0])
    fold_rim(rim, across)
    for q in range(rim.shape[0]):
        for f in range(CUBE):
            out[pl.ds(f * CUBE * CUBE, CUBE * CUBE), :, q * LANES : (q + 1) * LANES] = rim[
                q, 1 + f, 1 : CUBE + 1, 1 : CUBE + 1
            ].reshape((CUBE * CUBE,) + out.shape[1:2] + (LANES,))


def convt_shares(field, weights, first, across, whole):
    cubes, rows, channels = field.shape
    tiles = channels // LANES
    shape = (tiles, cubes // 2, rows, LANES)
    if whole:
        out_shape = (jax.ShapeDtypeStruct(field.shape, F32),)
    else:
        out_shape = (jax.ShapeDtypeStruct(shape, F32), jax.ShapeDtypeStruct(shape, BF16))
    work = cubes * rows * channels * weights.shape[0]
    return pl.pallas_call(
        partial(convt_whole_kernel if whole else convt_kernel, across),
        out_shape=out_shape,
        in_specs=[pl.BlockSpec(memory_space=pltpu.SMEM), whole_spec(), whole_spec()],
        out_specs=tuple(whole_spec() for _ in out_shape),
        scratch_shapes=[pltpu.VMEM((tiles, CUBE + 2, CUBE + 2, CUBE + 2, rows, LANES), F32)],
        compiler_params=kernel_params(),
        cost_estimate=pl.CostEstimate(flops=2 * work, bytes_accessed=8 << 20, transcendentals=0),
        name="conv_back_part",
    )(here_scalars(first), field, weights)


def grad_kernel(across, where, field, cotangent, out, rim, patch, wide):
    rows, channels = field.shape[1:]
    count = patch.shape[1] // LANES
    fill_rim(field, rim, across)
    fill_patch(rim, patch, where[0], count, (0, 0), (CUBE, CUBE))
    source = cotangent[...].reshape(-1, channels)
    for j in range(0, count, 2):
        lanes = slice(j * LANES, min(j + 2, count) * LANES)
        wide[lanes, :] = lax.dot_general(
            patch[:, lanes], source, (((0,), (0,)), ((), ())), preferred_element_type=F32
        )
    start = pl.multiple_of(where[1], 8)
    out[...] = wide[pl.ds(start, out.shape[0]), :].astype(out.dtype)


def kernel_grad_here(field, cotangent, first, offset, row_count, across):
    cubes, rows, channels = field.shape
    tiles = channels // LANES
    count = block_count(row_count)
    work = cubes * rows * channels * count * LANES
    return pl.pallas_call(
        partial(grad_kernel, across),
        out_shape=jax.ShapeDtypeStruct((row_count, channels), BF16),
        in_specs=[pl.BlockSpec(memory_space=pltpu.SMEM), whole_spec(), whole_spec()],
        out_specs=whole_spec(),
        scratch_shapes=[
            pltpu.VMEM((tiles, CUBE + 2, CUBE + 2, CUBE + 2, rows, LANES), BF16),
            pltpu.VMEM((cubes * rows, count * LANES), BF16),
            pltpu.VMEM((count * LANES, channels), F32),
        ],
        compiler_params=kernel_params(),
        cost_estimate=pl.CostEstimate(flops=2 * work, bytes_accessed=8 << 20, transcendentals=0),
        name="kernel_grad",
    )(jnp.stack([first, offset]).astype(jnp.int32), field, cotangent)


def chips_summed(mine):
    chips = chips_of()
    z, _ = here()
    total = picked(mine, z)
    for step in range(1, chips):
        sent = picked(mine, (z + step) % chips).astype(BF16)
        total = total + along_chips(sent, step).astype(F32)
    return total


def conv_scattered(field, weights, first, across, by_cube=False):
    if kernels_fit(field.shape[-1]):
        keep, send = conv_shares(field, weights, first, across, by_cube)
        return chips_summed(keep + to_twin(send).astype(F32))
    part, _ = conv_part(field, weights, first, across)
    if by_cube:
        cubes, rows, channels = part.shape
        return scattered(part.reshape(chips_of(), 2, -1, rows, channels))
    return scattered(to_blocks(part))


def convt_scattered(field, weights, first, across):
    if kernels_fit(field.shape[-1]):
        keep, send = convt_shares(field, weights, first, across, False)
        return chips_summed(keep + to_twin(send).astype(F32))
    return scattered(to_blocks(convt_part(field, weights, first, across)))


def convt_whole(field, weights, first, across):
    if kernels_fit(field.shape[-1]):
        return convt_shares(field, weights, first, across, True)[0]
    return convt_part(field, weights, first, across)


def kernel_grads(field, cotangent, first, offset, row_count, across):
    if kernels_fit(field.shape[-1]):
        return kernel_grad_here(field, cotangent, first, offset, row_count, across)
    patch = patches(field, first, block_count(row_count), across)
    grad = kernel_grad(patch, cotangent)
    return lax.dynamic_slice_in_dim(grad, offset, row_count, 0).astype(BF16)


def normed(values, sums, squares, width, members):
    average = group_means(sums, width, members)
    square = group_means(squares, width, members)
    spread = lax.rsqrt(square - average * average + 1e-06)
    return (values - average) * spread, spread


def channel_sums(values):
    return jnp.sum(values, axis=tuple(range(values.ndim - 1)))


def body(
    video_clips,
    code_bits,
    recon_grad,
    enc_convs,
    enc_gains,
    enc_shifts,
    down_weight,
    down_bias,
    down_proj,
    up_proj,
    up_bias,
    up_weight,
    upsample_bias,
    dec_convs,
    dec_gains,
    dec_shifts,
):
    section = lax.axis_index("section")
    space = lax.axis_index("space")
    sections = lax.axis_size("section")
    spaces = lax.axis_size("space")
    chips = chips_of()
    clips, frames, height, width, channels = video_clips.shape
    extent = (frames, height, width, channels)
    across = width // CUBE
    bits = code_bits.shape[-1]
    rows = spaces * across
    cubes = CUBE**3
    own_cubes = cubes // spaces
    members = float(cubes * rows * (channels // GROUPS))
    group = channels // GROUPS
    first_space = (space == 0).astype(F32)

    lanes = down_bias.shape[0]
    code = code_bits.reshape(-1).astype(BF16)
    code = jnp.pad(code, (0, -code.shape[0] % lanes)).reshape(-1, lanes)
    small = jnp.concatenate(
        [
            enc_gains,
            dec_gains,
            enc_shifts,
            dec_shifts,
            up_bias[None],
            down_bias[None],
            up_proj.T,
            down_proj.T,
            code,
        ],
        axis=0,
    )
    small = gathered(small).reshape(spaces, small.shape[0], lanes)
    heads = 14 + 2 * bits
    table = small[:, :heads].transpose(1, 0, 2).reshape(heads, channels)
    wide_table = table.astype(F32)
    e_gains, d_gains = wide_table[0:2], wide_table[2:4]
    e_shifts, d_shifts = wide_table[4:8], wide_table[8:12]
    up_row, down_row = wide_table[12], wide_table[13]
    up_cols, down_cols = table[14 : 14 + bits], table[14 + bits :]
    count = clips * across * bits
    code_all = small[:, heads:].reshape(spaces, -1)[:, :count].reshape(spaces, clips, across, bits)
    signs = (2 * code_all - 1).transpose(1, 0, 2, 3).reshape(clips * rows, bits)

    slabs = jnp.stack(
        [cubes_of(picked(video_clips, section)), cubes_of(picked(recon_grad, section))]
    )
    hidden = (jnp.dot(signs, up_cols, preferred_element_type=F32) + up_row).astype(BF16)
    hidden_own = lax.dynamic_slice_in_dim(hidden, section * rows, rows, 0)
    grown = lax.dot_general(
        hidden_own, up_weight, (((1,), (1,)), ((), ())), preferred_element_type=F32
    )
    grown = (grown + upsample_bias.astype(F32)).astype(BF16)
    grown = grown.reshape(rows, own_cubes, channels).transpose(1, 0, 2)
    decoded_in = gathered(grown).reshape(cubes, rows, channels)
    both = gathered(slabs)
    video = field_of(both[:, :, 0])
    recon_cot = field_of(both[:, :, 1])

    maps = jnp.stack(
        [
            lax.dot_general(
                up_cols, up_weight, (((1,), (1,)), ((), ())), preferred_element_type=F32
            ),
            lax.dot_general(
                down_cols, down_weight, (((1,), (1,)), ((), ())), preferred_element_type=F32
            ),
        ]
    ).astype(BF16)
    maps = gathered(maps).reshape(spaces, 2, bits, own_cubes, channels)
    up_map, down_map = maps[:, 0], maps[:, 1]

    first, offset = rows_here(enc_convs)
    enc_w, dec_w = aligned(enc_convs), aligned(dec_convs)
    half_members = members

    def ahead(inputs, weights, gains, shifts, by_cube):
        wide = inputs.astype(F32)
        flat_one, spread_one = normed(
            wide, channel_sums(wide), channel_sums(wide * wide), group, members
        )
        norm_one = flat_one * gains[0] + shifts[0]
        logistic = jax.nn.sigmoid(norm_one)
        act_one = (norm_one * logistic).astype(BF16)
        middle = conv_scattered(act_one, weights[0], first, across) + own_lanes(shifts[2])
        sums = pair_summed(jnp.stack([channel_sums(middle), channel_sums(middle * middle)]))
        flat_two, spread_two = normed(middle, sums[0], sums[1], group, half_members)
        norm_two = flat_two * own_lanes(gains[1]) + own_lanes(shifts[1])
        act_two = (norm_two * jax.nn.sigmoid(norm_two)).astype(BF16)
        act_two = from_blocks(gathered(act_two))
        branch = conv_scattered(act_two, weights[1], first, across, by_cube)
        return (
            branch,
            (flat_one, spread_one, norm_one, act_one),
            (flat_two, spread_two, norm_two, act_two),
        )

    def grads_two(raw, state, gains):
        flat, spread, norm, _ = state
        pre = raw * swish_slope(norm, jax.nn.sigmoid(norm))
        sums = pair_summed(jnp.stack([channel_sums(pre), channel_sums(pre * flat)]))
        gain = own_lanes(gains[1])
        total = group_means(sums[0] * gain, group, members)
        lined = group_means(sums[1] * gain, group, members)
        inner = (spread * (pre * gain - total - flat * lined)).astype(BF16)
        return inner, sums

    z, core = here()

    def spread_lanes(block_row):
        full = jnp.zeros(block_row.shape[:-1] + (channels,), F32)
        placed = lax.dynamic_update_slice_in_dim(
            full, block_row, z * block_row.shape[-1], full.ndim - 1
        )
        return jnp.where(core == 0, placed, 0.0)

    dec_branch, dec_one, dec_two = ahead(decoded_in, dec_w, d_gains, d_shifts, False)
    dec_inner, dec_sums_two = grads_two(
        convt_scattered(recon_cot, dec_w[1], first, across), dec_two, d_gains
    )
    dec_inner = from_blocks(gathered(dec_inner))
    back = convt_whole(dec_inner, dec_w[0], first, across)
    flat_one, spread_one, norm_one, _ = dec_one
    pre = back * swish_slope(norm_one, jax.nn.sigmoid(norm_one))
    dec_sums_one = jnp.stack([channel_sums(pre), channel_sums(pre * flat_one)])
    total = group_means(dec_sums_one[0] * d_gains[0], group, members)
    lined = group_means(dec_sums_one[1] * d_gains[0], group, members)
    grad_part = spread_one * (pre * d_gains[0] - total - flat_one * lined)
    grad_part = grad_part + recon_cot.astype(F32) * first_space
    sign_part = jnp.einsum(
        "sorc,skoc->rk",
        grad_part.reshape(spaces, own_cubes, rows, channels).astype(BF16),
        up_map,
        preferred_element_type=F32,
    )
    sign_grad = summed(sign_part).astype(BF16)
    enc_cot = jnp.einsum("rk,skoc->sorc", sign_grad, down_map, preferred_element_type=F32)
    enc_cot = enc_cot.astype(BF16).reshape(cubes, rows, channels)

    enc_branch, enc_one, enc_two = ahead(video, enc_w, e_gains, e_shifts, True)
    enc_inner, enc_sums_two = grads_two(
        convt_scattered(enc_cot, enc_w[1], first, across), enc_two, e_gains
    )
    enc_inner = from_blocks(gathered(enc_inner))
    back = convt_scattered(enc_inner, enc_w[0], first, across)
    flat, norm = own_block(enc_one[0]), own_block(enc_one[2])
    pre = back * swish_slope(norm, jax.nn.sigmoid(norm))
    enc_sums_one = pair_summed(jnp.stack([channel_sums(pre), channel_sums(pre * flat)]))
    gain = own_lanes(e_gains[0])
    total = group_means(enc_sums_one[0] * gain, group, members)
    lined = group_means(enc_sums_one[1] * gain, group, members)
    video_back = own_lanes(enc_one[1]) * (pre * gain - total - flat * lined)
    video_back = (own_block(enc_cot).astype(F32) + video_back).astype(BF16)
    recon = dec_branch + own_lanes(d_shifts[3])
    recon = (recon + own_block(decoded_in).astype(F32)).astype(BF16)

    def to_output(block):
        half, _, lane_count = block.shape
        pieces = block.reshape(half, spaces, across, lane_count).transpose(1, 0, 2, 3)
        swapped = lax.all_to_all(pieces, "space", 0, 0, tiled=True)
        slab = swapped.reshape(chips, 2, half, across, lane_count).transpose(1, 2, 3, 0, 4)
        slab = slab_of(slab.reshape(cubes, across, channels), extent)
        parted = slab.reshape(frames, height, width, sections, channels // sections)
        return lax.all_to_all(parted.transpose(3, 0, 1, 2, 4), "section", 0, 0, tiled=True)

    row_count = enc_convs.shape[1]
    grads = [
        lax.psum(kernel_grads(act, cot, first, offset, row_count, across), "section").astype(F32)
        for act, cot in (
            (enc_one[3], enc_inner),
            (enc_two[3], enc_cot),
            (dec_one[3], dec_inner),
            (dec_two[3], recon_cot),
        )
    ]

    encoded = enc_branch
    own = lambda v: lax.dynamic_slice_in_dim(v, space * own_cubes, own_cubes, 0).astype(F32)
    encoded = (encoded + e_shifts[3] + own(video)).astype(BF16)
    decoded_grad = scattered(grad_part.reshape(chips, 2, own_cubes, rows, channels)).astype(BF16)
    both = lax.all_gather(jnp.stack([encoded, decoded_grad]), "section", axis=0)
    both = both.transpose(1, 0, 3, 2, 4).reshape(2, clips * rows, own_cubes * channels)
    enc_rows, dec_rows = both[0], both[1]
    sign_all = lax.all_gather(sign_grad, "section", axis=0, tiled=True)
    inner_grad = jnp.dot(sign_all, down_cols, preferred_element_type=F32).astype(BF16)

    def outer(left, right):
        return lax.dot_general(left, right, (((0,), (0,)), ((), ())), preferred_element_type=F32)

    down_weight_grad = outer(enc_rows, inner_grad)
    up_weight_grad = outer(dec_rows, hidden)
    upsample_grad = jnp.sum(dec_rows.astype(F32), axis=0)
    parts = jnp.stack(
        [
            jnp.dot(enc_rows, down_weight, preferred_element_type=F32),
            jnp.dot(dec_rows, up_weight, preferred_element_type=F32),
        ]
    )
    shares = lax.psum_scatter(parts, "space", scatter_dimension=2, tiled=True)
    inner_low = (shares[0] + down_bias.astype(F32)).astype(BF16)
    hidden_grad = shares[1].astype(BF16)
    down_proj_grad = outer(inner_low, sign_all)
    up_proj_grad = outer(hidden_grad, signs)
    up_bias_grad = jnp.sum(hidden_grad.astype(F32), axis=0)
    inner_share = lax.dynamic_slice_in_dim(inner_grad, space * lanes, lanes, 1)
    down_bias_grad = jnp.sum(inner_share.astype(F32), axis=0)

    one = lambda v: channel_sums(v.astype(F32))[None] * first_space
    small_grads = jnp.concatenate(
        [
            spread_lanes(enc_sums_one[1:]),
            spread_lanes(enc_sums_two[1:]),
            spread_lanes(enc_sums_one[:1]),
            spread_lanes(enc_sums_two[:1]),
            one(enc_inner),
            one(enc_cot),
            dec_sums_one[1:],
            spread_lanes(dec_sums_two[1:]),
            dec_sums_one[:1],
            spread_lanes(dec_sums_two[:1]),
            one(dec_inner),
            one(recon_cot),
        ],
        axis=0,
    )
    small_grads = lax.psum(small_grads, ("section", "space"))
    small_grads = lax.dynamic_slice_in_dim(small_grads, space * lanes, lanes, 1)

    return (
        to_output(recon),
        to_output(video_back),
        jnp.stack(grads[:2]),
        small_grads[0:2],
        small_grads[2:6],
        down_weight_grad,
        down_bias_grad,
        down_proj_grad,
        up_proj_grad,
        up_bias_grad,
        up_weight_grad,
        upsample_grad,
        jnp.stack(grads[2:]),
        small_grads[6:8],
        small_grads[8:12],
    )


def solution(mesh):
    lead, second, third = P("space"), P(None, "space"), P(None, None, "space")
    field = P(None, None, "space", None, "section")
    return jax.shard_map(
        body,
        mesh=mesh,
        in_specs=(
            third,
            third,
            third,
            second,
            second,
            second,
            lead,
            lead,
            lead,
            lead,
            lead,
            lead,
            lead,
            second,
            second,
            second,
        ),
        out_specs=(
            field,
            field,
            second,
            second,
            second,
            lead,
            lead,
            lead,
            lead,
            lead,
            lead,
            lead,
            second,
            second,
            second,
        ),
        check_vma=False,
    )
```

```python
from functools import partial

import jax
import jax.numpy as jnp
from jax import lax
from jax.experimental import pallas as pl
from jax.experimental.pallas import tpu as pltpu
from jax.sharding import PartitionSpec as P

GROUPS = 32
CUBE = 4
LANES = 128
BF16 = jnp.bfloat16
F32 = jnp.float32


def swish_slope(values, logistic):
    return logistic * (1.0 + values * (1.0 - logistic))


def chips_of():
    return lax.axis_size("space") // 2


def along_chips(value, step):
    chips = chips_of()
    route = [(i, (i // 2 + step) % chips * 2 + i % 2) for i in range(2 * chips)]
    return lax.ppermute(value, "space", route)


def to_twin(value):
    return lax.ppermute(value, "space", [(i, i ^ 1) for i in range(lax.axis_size("space"))])


def here():
    index = lax.axis_index("space")
    return index // 2, index % 2


def ring_is_short():
    return chips_of() <= 4


def picked(value, index, axis=0):
    return lax.dynamic_index_in_dim(value, index, axis, keepdims=False)


def gathered(value):
    chips = chips_of()
    if not ring_is_short():
        return lax.all_gather(value, "space", axis=0).reshape((chips, 2) + value.shape)
    z, core = here()
    pieces = [value] + [along_chips(value, step) for step in range(1, chips)]
    stack = jnp.zeros((chips,) + value.shape, value.dtype)
    for step, piece in enumerate(pieces):
        stack = lax.dynamic_update_index_in_dim(stack, piece, (z - step) % chips, 0)
    other = to_twin(stack)
    first = jnp.where(core == 0, stack, other)
    second = jnp.where(core == 0, other, stack)
    return jnp.stack([first, second], axis=1)


def scattered(parts):
    chips = chips_of()
    if not ring_is_short():
        flat = parts.reshape((2 * chips,) + parts.shape[2:])
        return lax.psum_scatter(flat, "space", scatter_dimension=0, tiled=False)
    z, core = here()
    mine = picked(parts, core, 1)
    mine = mine + to_twin(picked(parts, 1 - core, 1).astype(BF16)).astype(F32)
    total = picked(mine, z)
    for step in range(1, chips):
        sent = picked(mine, (z + step) % chips).astype(BF16)
        total = total + along_chips(sent, step).astype(F32)
    return total


def summed(value):
    if not ring_is_short():
        return lax.psum(value, "space")
    total = value
    for step in range(1, chips_of()):
        total = total + along_chips(value, step)
    return total + to_twin(total)


def pair_summed(value):
    return value + to_twin(value)


def to_blocks(field):
    chips = chips_of()
    cubes, rows, channels = field.shape
    split = field.reshape(2, cubes // 2, rows, chips, channels // chips)
    return split.transpose(3, 0, 1, 2, 4)


def from_blocks(blocks):
    chips, _, half, rows, width = blocks.shape
    return blocks.transpose(1, 2, 3, 0, 4).reshape(2 * half, rows, chips * width)


def own_block(field):
    z, core = here()
    cubes, rows, channels = field.shape
    width = channels // chips_of()
    return lax.dynamic_slice(field, (core * (cubes // 2), 0, z * width), (cubes // 2, rows, width))


def own_lanes(row):
    z, _ = here()
    width = row.shape[-1] // chips_of()
    return lax.dynamic_slice_in_dim(row, z * width, width, row.ndim - 1)


def cubes_of(slab):
    frames, height, across, channels = slab.shape
    split = slab.reshape(frames, height, across // CUBE, CUBE, channels)
    return split.transpose(0, 1, 3, 2, 4).reshape(-1, across // CUBE, channels)


def slab_of(cubes, extent):
    frames, height, across, channels = extent
    split = cubes.reshape(frames, height, CUBE, across // CUBE, channels)
    return split.transpose(0, 1, 3, 2, 4).reshape(extent)


def field_of(slabs):
    chips, _, cubes, across, channels = slabs.shape
    flat = slabs.reshape(2 * chips, cubes, across, channels)
    return flat.transpose(1, 0, 2, 3).reshape(cubes, 2 * chips * across, channels)


def group_means(sums, width, members):
    groups = sums.reshape(sums.shape[:-1] + (-1, width))
    wide = jnp.broadcast_to(jnp.sum(groups, axis=-1, keepdims=True), groups.shape)
    return wide.reshape(sums.shape) / members


def rimmed(field, across):
    cubes, rows, channels = field.shape
    view = field.reshape(CUBE, CUBE, CUBE, rows // across, across, channels)
    none = (0, 0)
    above = jnp.pad(view[:, -1:, :, :-1], (none, none, none, (1, 0), none, none))
    below = jnp.pad(view[:, :1, :, 1:], (none, none, none, (0, 1), none, none))
    view = jnp.concatenate([above, view, below], axis=1)
    left = jnp.pad(view[:, :, -1:, :, :-1], (none, none, none, none, (1, 0), none))
    right = jnp.pad(view[:, :, :1, :, 1:], (none, none, none, none, (0, 1), none))
    view = jnp.concatenate([left, view, right], axis=2)
    view = jnp.pad(view, ((1, 1), none, none, none, none, none))
    return view.reshape(CUBE + 2, CUBE + 2, CUBE + 2, rows, channels)


def rows_here(weights):
    count = weights.shape[-2]
    start = count * lax.axis_index("space")
    return start // LANES, start % LANES


def block_count(count):
    worst = max(count * s % LANES for s in range(lax.axis_size("space")))
    return -(-(worst + count) // LANES)


def aligned(weights):
    _, offset = rows_here(weights)
    total = block_count(weights.shape[-2]) * LANES
    wide = jnp.zeros(weights.shape[:-2] + (total, weights.shape[-1]), weights.dtype)
    return lax.dynamic_update_slice_in_dim(wide, weights, offset, wide.ndim - 2)


def patches(field, first, count, across):
    cubes, rows, channels = field.shape
    wide = rimmed(field, across)
    per_tap = channels // LANES
    pieces = []
    for j in range(count):
        block = first + j
        tap, lane = jnp.minimum(block // per_tap, 26), block % per_tap
        piece = lax.dynamic_slice(
            wide,
            (tap // 9, tap // 3 % 3, tap % 3, 0, lane * LANES),
            (CUBE, CUBE, CUBE, rows, LANES),
        )
        pieces.append(piece.reshape(cubes * rows, LANES))
    return jnp.concatenate(pieces, axis=1)


def conv_part(field, weights, first, across):
    patch = patches(field, first, weights.shape[0] // LANES, across)
    out = jnp.dot(patch, weights, preferred_element_type=F32)
    return out.reshape(field.shape[:2] + (-1,)), patch


def convt_part(field, weights, first, across):
    cubes, rows, channels = field.shape
    spread = lax.dot_general(
        field.reshape(-1, channels),
        weights,
        (((1,), (1,)), ((), ())),
        preferred_element_type=F32,
    )
    count = weights.shape[0] // LANES
    fold = jax.linear_transpose(
        lambda v: patches(v, first, count, across),
        jax.ShapeDtypeStruct((cubes, rows, channels), F32),
    )
    return fold(spread)[0]


def kernel_grad(patch, field):
    return lax.dot_general(
        patch,
        field.reshape(-1, field.shape[-1]),
        (((0,), (0,)), ((), ())),
        preferred_element_type=F32,
    )


def normed(values, sums, squares, width, members):
    average = group_means(sums, width, members)
    square = group_means(squares, width, members)
    spread = lax.rsqrt(square - average * average + 1e-06)
    return (values - average) * spread, spread


def channel_sums(values):
    return jnp.sum(values, axis=tuple(range(values.ndim - 1)))


VMEM_BYTES = 56 * 1024 * 1024


def kernels_fit(channels):
    return chips_of() * LANES == channels


def kernel_params():
    return pltpu.CompilerParams(vmem_limit_bytes=VMEM_BYTES)


def shifted(slabs, rows, valid):
    wide = pltpu.roll(slabs.astype(F32), rows % slabs.shape[1], 1)
    return jnp.where(valid, wide, 0.0)


def row_marks(shape, across):
    row = lax.broadcasted_iota(jnp.int32, shape, len(shape) - 2)
    return row, row % across


def fill_rim(field, rim, across):
    rows, channels = field.shape[1:]
    tiles = channels // LANES
    blank = jnp.zeros((CUBE + 2, CUBE + 2, rows, LANES), rim.dtype)
    for q in range(tiles):
        rim[q, 0] = blank
        rim[q, CUBE + 1] = blank

    def frame(f, carry):
        base = f * CUBE * CUBE
        row, column = row_marks((CUBE, rows, LANES), across)
        row6, column6 = row_marks((CUBE + 2, rows, LANES), across)
        for q in range(tiles):
            lanes = slice(q * LANES, (q + 1) * LANES)
            for h in range(CUBE):
                rim[q, f + 1, h + 1, 1 : CUBE + 1] = field[pl.ds(base + CUBE * h, CUBE), :, lanes]
            above = field[pl.ds(base + CUBE * (CUBE - 1), CUBE), :, lanes]
            rim[q, f + 1, 0, 1 : CUBE + 1] = shifted(above, across, row >= across).astype(rim.dtype)
            below = field[pl.ds(base, CUBE), :, lanes]
            rim[q, f + 1, CUBE + 1, 1 : CUBE + 1] = shifted(
                below, -across, row < rows - across
            ).astype(rim.dtype)
            left = rim[q, f + 1, :, CUBE]
            rim[q, f + 1, :, 0] = shifted(left, 1, column6 >= 1).astype(rim.dtype)
            right = rim[q, f + 1, :, 1]
            rim[q, f + 1, :, CUBE + 1] = shifted(right, -1, column6 < across - 1).astype(rim.dtype)
        return carry

    lax.fori_loop(0, CUBE, frame, 0)


def fold_rim(rim, across):
    tiles, rows = rim.shape[0], rim.shape[4]

    def frame(f, carry):
        row, _ = row_marks((CUBE, rows, LANES), across)
        _, column6 = row_marks((CUBE + 2, rows, LANES), across)
        for q in range(tiles):
            left = shifted(rim[q, f + 1, :, 0], -1, column6 < across - 1)
            rim[q, f + 1, :, CUBE] += left
            right = shifted(rim[q, f + 1, :, CUBE + 1], 1, column6 >= 1)
            rim[q, f + 1, :, 1] += right
            above = shifted(rim[q, f + 1, 0, 1 : CUBE + 1], -across, row < rows - across)
            rim[q, f + 1, CUBE, 1 : CUBE + 1] += above
            below = shifted(rim[q, f + 1, CUBE + 1, 1 : CUBE + 1], across, row >= across)
            rim[q, f + 1, 1, 1 : CUBE + 1] += below
        return carry

    lax.fori_loop(0, CUBE, frame, 0)


def tap_of(block, per_tap):
    tap = jnp.minimum(block // per_tap, 26)
    return block % per_tap, tap // 9, tap // 3 % 3, tap % 3


def fill_patch(rim, patch, first, count, start, size):
    rows = rim.shape[4]
    for j in range(count):
        q, f, h, w = tap_of(first + j, rim.shape[0])
        window = rim[
            q,
            pl.ds(f + start[0], size[0]),
            pl.ds(h + start[1], size[1]),
            pl.ds(w, CUBE),
        ]
        patch[:, j * LANES : (j + 1) * LANES] = window.reshape(
            size[0] * size[1] * CUBE * rows, LANES
        )


def add_taps(field, weights, rim, first):
    rows, channels = field.shape[1:]
    tiles = channels // LANES
    count = weights.shape[0] // LANES
    blank = jnp.zeros((CUBE + 2, CUBE + 2, rows, LANES), F32)

    def clear(f, carry):
        for q in range(tiles):
            rim[q, f] = blank
        return carry

    lax.fori_loop(0, CUBE + 2, clear, 0)
    spread_rows = CUBE * CUBE * rows

    def frame(f, carry):
        source = field[pl.ds(f * CUBE * CUBE, CUBE * CUBE)].reshape(spread_rows, channels)
        for j in range(0, count, 2):
            wide = min(2, count - j)
            spread = lax.dot_general(
                source,
                weights[j * LANES : (j + wide) * LANES, :],
                (((1,), (1,)), ((), ())),
                preferred_element_type=F32,
            )
            for i in range(wide):
                q, tf, th, tw = tap_of(first + j + i, tiles)
                rim[q, f + tf, pl.ds(th, CUBE), pl.ds(tw, CUBE)] += spread[
                    :, i * LANES : (i + 1) * LANES
                ].reshape(CUBE, CUBE, rows, LANES)
        return carry

    lax.fori_loop(0, CUBE, frame, 0)


def group_totals(row, width):
    lanes = row.shape[1]
    lane = lax.broadcasted_iota(jnp.int32, row.shape, 1)
    step = 1
    while step < width:
        before = pltpu.roll(row, step, 1)
        after = pltpu.roll(row, lanes - step, 1)
        row = row + jnp.where(lane // step % 2 == 1, before, after)
        step *= 2
    return row


def row_sum(values):
    return jnp.sum(values.reshape(-1, values.shape[-1]), axis=0, keepdims=True)


def logistic_of(values):
    return 0.5 + 0.5 * jnp.tanh(0.5 * values)


def both_halves(row):
    return row + pltpu.roll(row, LANES // 2, 1)


def pack_pair(near, far, core):
    axis = near.ndim - 1
    lane = lax.broadcasted_iota(jnp.int32, near.shape, axis)
    low = lane < LANES // 2
    first = jnp.where(low, near, pltpu.roll(far, LANES // 2, axis))
    second = jnp.where(low, pltpu.roll(near, LANES // 2, axis), far)
    lead = lane * 0 + core == 0
    return jnp.where(lead, first, second), jnp.where(lead, second, first)


def unpack_pair(own, other, core):
    axis = own.ndim - 1
    lane = lax.broadcasted_iota(jnp.int32, own.shape, axis)
    low = lane < LANES // 2
    lead = lane * 0 + core == 0
    first, second = jnp.where(lead, own, other), jnp.where(lead, other, own)
    near = jnp.where(low, first, pltpu.roll(second, LANES // 2, axis))
    far = jnp.where(low, pltpu.roll(first, LANES // 2, axis), second)
    return near, far


def own_row(table, index, z, core):
    lanes = pl.ds(pl.multiple_of(z * LANES, LANES), LANES)
    row = table[index : index + 1, lanes]
    mine, _ = pack_pair(row, row, core)
    return mine


def pack_own(field, out, z, core):
    lanes = pl.ds(pl.multiple_of(z * LANES, LANES), LANES)
    half = field.shape[0] // 2

    def some(i, carry):
        near = field[pl.ds(8 * i, 8), :, lanes].astype(F32)
        far = field[pl.ds(half + 8 * i, 8), :, lanes].astype(F32)
        out[pl.ds(8 * i, 8)] = pack_pair(near, far, core)[0].astype(out.dtype)
        return carry

    lax.fori_loop(0, half // 8, some, 0)


def unpack_stacks(own, other, field, z, core, relative):
    chips, half = own.shape[:2]
    for hop in range(chips):
        place = lax.rem(z + chips - hop, chips) if relative else hop
        lanes = pl.ds(pl.multiple_of(place * LANES, LANES), LANES)

        def some(i, carry, hop=hop, lanes=lanes):
            mine = own[hop, pl.ds(8 * i, 8)].astype(F32)
            twin = other[hop, pl.ds(8 * i, 8)].astype(F32)
            near, far = unpack_pair(mine, twin, core)
            field[pl.ds(8 * i, 8), :, lanes] = near.astype(field.dtype)
            field[pl.ds(half + 8 * i, 8), :, lanes] = far.astype(field.dtype)
            return carry

        lax.fori_loop(0, half // 8, some, 0)


class Rows:
    def __init__(self, weights, index, offset, wide, sem):
        count = weights.shape[1]
        slack = wide.shape[0] - count
        blank = jnp.zeros((slack, wide.shape[1]), wide.dtype)
        wide[0:slack, :] = blank
        wide[count : count + slack, :] = blank
        target = wide.at[pl.ds(pl.multiple_of(offset, 64), count), :]
        self.copy = pltpu.make_async_copy(weights.at[index], target, sem)
        self.copy.start()

    def ready(self):
        self.copy.wait()


def norm_in(field, act, table, gain, shift, stats, group, members):
    cubes, rows, channels = field.shape

    def add(i, carry):
        values = field[pl.ds(4 * i, 4)].astype(F32)
        folded = values.reshape(-1, 8, channels)
        return (carry[0] + jnp.sum(folded, 0), carry[1] + jnp.sum(folded * folded, 0))

    blank = jnp.zeros((8, channels), F32)
    totals, squares = lax.fori_loop(0, cubes // 4, add, (blank, blank))
    sums = jnp.concatenate(
        [jnp.sum(totals, 0, keepdims=True), jnp.sum(squares, 0, keepdims=True)], axis=0
    )
    means = group_totals(sums, group) / members
    average = means[0:1]
    spread = lax.rsqrt(means[1:2] - average * average + 1e-06)
    stats[0:1, :] = average
    stats[1:2, :] = spread
    scale, start = table[gain : gain + 1, :], table[shift : shift + 1, :]

    def apply(i, carry):
        values = field[pl.ds(4 * i, 4)].astype(F32)
        flat = (values - average[None]) * spread[None]
        normal = flat * scale[None] + start[None]
        act[pl.ds(4 * i, 4)] = (normal * logistic_of(normal)).astype(act.dtype)
        return carry

    lax.fori_loop(0, cubes // 4, apply, 0)


def multiply(patch, wide, product):
    size = product.shape[1]

    for f in range(product.shape[0]):
        rows = slice(f * size, (f + 1) * size)
        product[f] = jnp.dot(patch[rows, :], wide[...], preferred_element_type=F32)


def share_blocks(frame_block, keep, send, core):
    tiles, cubes = keep.shape[0], CUBE * CUBE

    def pair(i, carry):
        for q in range(tiles):
            mine, twin = pack_pair(frame_block(i, q), frame_block(i + CUBE // 2, q), core)
            keep[q, pl.ds(i * cubes, cubes)] = mine
            send[q, pl.ds(i * cubes, cubes)] = twin.astype(send.dtype)
        return carry

    lax.fori_loop(0, CUBE // 2, pair, 0)


def of_product(product, rows):
    def block(f, q):
        return product[f, :, q * LANES : (q + 1) * LANES].reshape(CUBE * CUBE, rows, LANES)

    return block


def of_rim(rim):
    rows = rim.shape[4]

    def block(f, q):
        inner = rim[q, f + 1, 1 : CUBE + 1, 1 : CUBE + 1]
        return inner.reshape(CUBE * CUBE, rows, LANES)

    return block


def first_conv_kernel(settings, where, *refs):
    stacked, across, group, members, gain, shift, index = settings
    if stacked:
        own, other, table, weights, keep, send, act, stats, mine, field = refs[:10]
        rim, patch, wide, product, sem = refs[10:]
    else:
        field, table, weights, keep, send, act, stats, mine = refs[:8]
        rim, patch, wide, product, sem = refs[8:]
    first, offset, z, core = where[0], where[1], where[2], where[3]
    coming = Rows(weights, index, offset, wide, sem)
    if stacked:
        chips, count = own.shape[:2]
        for hop in range(chips):
            place = lax.rem(z + chips - hop, chips) * 2
            field[pl.ds((place + core) * count, count)] = own[hop]
            field[pl.ds((place + 1 - core) * count, count)] = other[hop]
    rows = field.shape[1]
    norm_in(field, act, table, gain, shift, stats, group, members)
    fill_rim(act, rim, across)
    fill_patch(rim, patch, first, patch.shape[1] // LANES, (0, 0), (CUBE, CUBE))
    coming.ready()
    multiply(patch, wide, product)
    share_blocks(of_product(product, rows), keep, send, core)
    pack_own(field, mine, z, core)


def fill_grad(patch, source, offset, grad, out):
    count = patch.shape[1]
    for j in range(0, count, 2 * LANES):
        lanes = slice(j, min(j + 2 * LANES, count))
        grad[lanes, :] = lax.dot_general(
            patch[:, lanes], source, (((0,), (0,)), ((), ())), preferred_element_type=F32
        )
    start = pl.multiple_of(offset, 64)
    out[...] = grad[pl.ds(start, out.shape[0]), :].astype(out.dtype)


def second_conv_kernel(across, with_grad, index, where, *refs):
    if with_grad:
        own, other, weights, cotangent, keep, send, out, field = refs[:8]
        rim, patch, wide, product, sem, grad = refs[8:]
    else:
        own, other, weights, keep, send, field = refs[:6]
        rim, patch, wide, product, sem = refs[6:]
    first, offset, z, core = where[0], where[1], where[2], where[3]
    rows, channels = field.shape[1:]
    coming = Rows(weights, index, offset, wide, sem)
    unpack_stacks(own, other, field, z, core, False)
    fill_rim(field, rim, across)
    fill_patch(rim, patch, first, patch.shape[1] // LANES, (0, 0), (CUBE, CUBE))
    coming.ready()
    multiply(patch, wide, product)
    if with_grad:
        share_blocks(of_product(product, rows), keep, send, core)
        fill_grad(patch, cotangent[...].reshape(-1, channels), offset, grad, out)
    else:

        def frame(f, carry):
            low = product[f, : CUBE * CUBE * rows // 2]
            high = product[f, CUBE * CUBE * rows // 2 :]
            lead = lax.broadcasted_iota(jnp.int32, low.shape, 1) * 0 + core == 0
            keep[f] = jnp.where(lead, low, high).reshape(keep.shape[1:])
            send[f] = jnp.where(lead, high, low).reshape(send.shape[1:]).astype(send.dtype)
            return carry

        lax.fori_loop(0, CUBE, frame, 0)


def grad_only_kernel(across, where, field, cotangent, out, rim, patch, grad):
    channels = field.shape[2]
    fill_rim(field, rim, across)
    fill_patch(rim, patch, where[0], patch.shape[1] // LANES, (0, 0), (CUBE, CUBE))
    fill_grad(patch, cotangent[...].reshape(-1, channels), where[1], grad, out)


def twin_add_kernel(where, keep, received, own, *sends):
    chips, z = keep.shape[0], where[2]
    own[...] = keep[z] + received[z].astype(F32)
    for hop, send in enumerate(sends):
        target = lax.rem(z + 1 + hop, chips)
        send[...] = (keep[target] + received[target].astype(F32)).astype(send.dtype)


def twin_sums_kernel(count, where, *refs):
    out = refs[2 * count]
    lanes = out.shape[-1]
    for i in range(count):
        keep, received = refs[2 * i], refs[2 * i + 1]
        for target in range(out.shape[0]):
            total = (keep[target] + received[target].astype(F32)).astype(out.dtype)
            if total.shape[-1] == lanes:
                out[target, i] = total
            else:
                parts = total.shape[-1] // lanes
                for cube in range(total.shape[0]):
                    for q in range(parts):
                        out[target, i, cube * parts + q] = total[cube, :, q * lanes : (q + 1) * lanes]


def total_of(pieces):
    if len(pieces) == 1:
        return jnp.sum(pieces[0][...].astype(F32), axis=0)
    total = pieces[0][...]
    for piece in pieces[1:]:
        total = total + piece[...].astype(F32)
    return total


def mid_norm(middle, table, gain, shift, z, core, group, members):
    sums = jnp.concatenate([row_sum(middle), row_sum(middle * middle)], axis=0)
    means = group_totals(both_halves(sums), group) / members
    average = means[0:1]
    spread = lax.rsqrt(means[1:2] - average * average + 1e-06)
    flat = (middle - average[None]) * spread[None]
    scale = own_row(table, gain, z, core)
    normal = flat * scale[None] + own_row(table, shift, z, core)[None]
    return flat, spread, normal, logistic_of(normal), scale


def mid_back(raw, normed_state, group, members):
    flat, spread, normal, logistic, scale = normed_state
    pre = raw * (logistic * (1.0 + normal * (1.0 - logistic)))
    sums = jnp.concatenate([row_sum(pre), row_sum(pre * flat)], axis=0)
    sums = both_halves(sums)
    means = group_totals(sums * scale, group) / members
    back = spread[None] * (pre * scale[None] - means[0:1][None] - flat * means[1:2][None])
    return back, sums


def mid_ahead_kernel(settings, where, *refs):
    group, members, gain, shift, bias, chips = settings
    pieces, table, act, kept = refs[:chips], refs[chips], refs[chips + 1], refs[chips + 2]
    z, core = where[2], where[3]
    middle = total_of(pieces) + own_row(table, bias, z, core)[None]
    kept[...] = middle
    state = mid_norm(middle, table, gain, shift, z, core, group, members)
    act[...] = (state[2] * state[3]).astype(act.dtype)


def mid_back_kernel(settings, where, *refs):
    group, members, gain, shift, chips = settings
    pieces, kept, table, inner, sums = refs[:chips], *refs[chips:]
    z, core = where[2], where[3]
    state = mid_norm(kept[...], table, gain, shift, z, core, group, members)
    back, rows = mid_back(total_of(pieces), state, group, members)
    inner[...] = back.astype(inner.dtype)
    sums[...] = rows


def mid_both_kernel(settings, where, *refs):
    group, members, gain, shift, bias, chips = settings
    ahead, behind = refs[:chips], refs[chips : chips + 1]
    table, act, inner, sums = refs[chips + 1 :]
    z, core = where[2], where[3]
    middle = total_of(ahead) + own_row(table, bias, z, core)[None]
    state = mid_norm(middle, table, gain, shift, z, core, group, members)
    act[...] = (state[2] * state[3]).astype(act.dtype)
    back, rows = mid_back(total_of(behind), state, group, members)
    inner[...] = back.astype(inner.dtype)
    sums[...] = rows


def last_back_kernel(settings, where, *refs):
    group, members, gain, shift, chips = settings
    pieces = refs[:chips]
    inputs, cotangent, stats, table, out, sums = refs[chips:]
    z, core = where[2], where[3]
    average, spread = own_row(stats, 0, z, core), own_row(stats, 1, z, core)
    flat = (inputs[...].astype(F32) - average[None]) * spread[None]
    scale = own_row(table, gain, z, core)
    normal = flat * scale[None] + own_row(table, shift, z, core)[None]
    state = (flat, spread, normal, logistic_of(normal), scale)
    back, rows = mid_back(total_of(pieces), state, group, members)
    out[...] = (cotangent[...].astype(F32) + back).astype(out.dtype)
    sums[...] = rows


def share_rim(field, coming, where, wide, rim, across, keep, send):
    coming.ready()
    add_taps(field, wide, rim, where[0])
    fold_rim(rim, across)
    share_blocks(of_rim(rim), keep, send, where[3])


def back_kernel(across, index, where, field, weights, keep, send, wide, rim, sem):
    coming = Rows(weights, index, where[1], wide, sem)
    share_rim(field, coming, where, wide, rim, across, keep, send)


def back_stacked_kernel(across, index, where, own, other, weights, keep, send, field, *work):
    wide, rim, sem = work
    coming = Rows(weights, index, where[1], wide, sem)
    unpack_stacks(own, other, field, where[2], where[3], True)
    share_rim(field, coming, where, wide, rim, across, keep, send)


def back_signs_kernel(settings, where, tiny, maps, weights, keep, send, field, mine, *work):
    across, bits, index = settings
    wide, rim, sem = work
    coming = Rows(weights, index, where[1], wide, sem)
    rows, channels = field.shape[1:]
    signs = tiny[0:rows, 0:bits].astype(BF16)
    parts, slabs = maps.shape[:2]
    size = field.shape[0] // (slabs * parts)

    def slab(s, carry):
        for p in range(parts):
            wave = jnp.dot(signs, maps[p, s], preferred_element_type=F32)
            for j in range(size):
                cube = (s * parts + p) * size + j
                field[cube] = wave[:, j * channels : (j + 1) * channels].astype(BF16)
        return carry

    lax.fori_loop(0, slabs, slab, 0)
    share_rim(field, coming, where, wide, rim, across, keep, send)
    pack_own(field, mine, where[2], where[3])


def back_whole_kernel(settings, where, *refs):
    across, group, members, gain, shift, bits, index = settings
    own, other, weights, inputs, stats, table, cotangent, maps = refs[:8]
    keep, send, tiny, field = refs[8:12]
    wide, rim, sem, pre_ref, low, sums = refs[12:]
    z, core = where[2], where[3]
    tiles, rows, channels = rim.shape[0], rim.shape[4], field.shape[2]
    size = CUBE * CUBE
    coming = Rows(weights, index, where[1], wide, sem)
    unpack_stacks(own, other, field, z, core, True)
    coming.ready()
    add_taps(field, wide, rim, where[0])
    fold_rim(rim, across)
    sums[...] = jnp.zeros(sums.shape, F32)
    block = of_rim(rim)

    def at(f, q):
        lanes = slice(q * LANES, (q + 1) * LANES)
        values = inputs[pl.ds(f * size, size), :, lanes].astype(F32)
        flat = (values - stats[0:1, lanes][None]) * stats[1:2, lanes][None]
        return flat, lanes

    def ahead(f, carry):
        for q in range(tiles):
            flat, lanes = at(f, q)
            normal = flat * table[gain : gain + 1, lanes][None] + table[shift : shift + 1, lanes][None]
            logistic = logistic_of(normal)
            pre = block(f, q) * (logistic * (1.0 + normal * (1.0 - logistic)))
            pre_ref[q, pl.ds(f * size, size)] = pre
            sums[0:1, lanes] += row_sum(pre)
            sums[1:2, lanes] += row_sum(pre * flat)
        return carry

    lax.fori_loop(0, CUBE, ahead, 0)
    means = group_totals(sums[0:2, :] * table[gain : gain + 1, :], group) / members
    lead_slab = (2 * z + core == 0).astype(F32)
    half = size // 2

    def behind(f, carry):
        for q in range(tiles):
            flat, lanes = at(f, q)
            scaled = pre_ref[q, pl.ds(f * size, size)] * table[gain : gain + 1, lanes][None]
            back = stats[1:2, lanes][None] * (
                scaled - means[0:1, lanes][None] - flat * means[1:2, lanes][None]
            )
            back = back + cotangent[pl.ds(f * size, size), :, lanes].astype(F32) * lead_slab
            low[pl.ds(f * size, size), :, lanes] = back.astype(BF16)
            lead = lax.broadcasted_iota(jnp.int32, (half, rows, LANES), 2) * 0 + core == 0
            keep[f, :, :, lanes] = jnp.where(lead, back[:half], back[half:])
            send[f, :, :, lanes] = jnp.where(lead, back[half:], back[:half]).astype(BF16)
        return carry

    lax.fori_loop(0, CUBE, behind, 0)
    parts, slabs = maps.shape[:2]
    size = field.shape[0] // (slabs * parts)

    def slab(s, total):
        for p in range(parts):
            cube = (s * parts + p) * size
            wave = jnp.concatenate([low[cube + j] for j in range(size)], axis=1)
            total = total + lax.dot_general(
                wave, maps[p, s], (((1,), (1,)), ((), ())), preferred_element_type=F32
            )
        return total

    signs = lax.fori_loop(0, slabs, slab, jnp.zeros((rows, bits), F32))
    tiny[...] = jnp.zeros(tiny.shape, F32)
    tiny[0:rows, 0:bits] = signs
    for q in range(tiles):
        lanes = slice(q * LANES, (q + 1) * LANES)
        tiny[rows + q : rows + q + 1, :] = sums[0:1, lanes]
        tiny[rows + tiles + q : rows + tiles + q + 1, :] = sums[1:2, lanes]


def fast_body(
    video_clips,
    code_bits,
    recon_grad,
    enc_convs,
    enc_gains,
    enc_shifts,
    down_weight,
    down_bias,
    down_proj,
    up_proj,
    up_bias,
    up_weight,
    upsample_bias,
    dec_convs,
    dec_gains,
    dec_shifts,
):
    section = lax.axis_index("section")
    space = lax.axis_index("space")
    z, core = here()
    sections = lax.axis_size("section")
    spaces = lax.axis_size("space")
    chips = chips_of()
    clips, frames, height, width, channels = video_clips.shape
    across = width // CUBE
    bits = code_bits.shape[-1]
    rows = spaces * across
    cubes = CUBE**3
    own_cubes = cubes // spaces
    half = cubes // 2
    group = channels // GROUPS
    members = float(cubes * rows * group)
    lanes = down_bias.shape[0]
    row_count = enc_convs.shape[1]
    total_rows = block_count(row_count) * LANES
    tiles = channels // LANES
    first, offset = rows_here(enc_convs)
    where = jnp.stack([first, offset, z, core]).astype(jnp.int32)

    def arr(shape, dtype):
        return jax.ShapeDtypeStruct(shape, dtype)

    full = arr((cubes, rows, channels), BF16)
    piece_b, piece_f = arr((half, rows, LANES), BF16), arr((half, rows, LANES), F32)
    blocks_f, blocks_b = arr((tiles, half, rows, LANES), F32), arr((tiles, half, rows, LANES), BF16)
    cubes_f = arr((CUBE, half // CUBE, rows, channels), F32)
    cubes_b = arr((CUBE, half // CUBE, rows, channels), BF16)
    stats_f = arr((8, channels), F32)
    sums_f = arr((2, LANES), F32)
    grad_b = arr((row_count, channels), BF16)
    rim_shape = (tiles, CUBE + 2, CUBE + 2, CUBE + 2, rows, LANES)
    rim_b, rim_f = pltpu.VMEM(rim_shape, BF16), pltpu.VMEM(rim_shape, F32)
    patch = pltpu.VMEM((cubes * rows, total_rows), BF16)
    wide = pltpu.VMEM((total_rows, channels), BF16)
    grad_s = pltpu.VMEM((total_rows, channels), F32)
    product = pltpu.VMEM((CUBE, cubes * rows // CUBE, channels), F32)
    spec = pl.BlockSpec(memory_space=pltpu.VMEM)
    conv_flops = 2 * cubes * rows * channels * total_rows

    hbm = pl.BlockSpec(memory_space=pltpu.HBM)
    enc_convs, dec_convs = (
        pltpu.with_memory_space_constraint(w, pltpu.HBM) for w in (enc_convs, dec_convs)
    )
    arrival = pltpu.SemaphoreType.DMA

    def piece_spec(index):
        return pl.BlockSpec((chips, None, half, rows, LANES), lambda i: (0, index, 0, 0, 0))

    order = [where]

    def call(kernel, name, out_shape, scratch, specs, args, flops=conv_flops, mib=28, held=(), after=()):
        place, anywhere = pl.BlockSpec(memory_space=pltpu.SMEM), pl.BlockSpec(memory_space=pl.ANY)
        inner, outer = len(args), len(out_shape)

        def ordered(*refs):
            skip = inner + len(held) + len(after)
            given, handed = refs[0], refs[1 + skip]
            for i in range(given.shape[0]):
                handed[i] = given[i]
            outs = 2 + skip
            scratch_refs = refs[outs + outer + len(held) :]
            kernel(given, *refs[1 : 1 + inner], *refs[outs : outs + outer], *scratch_refs)

        made = pl.pallas_call(
            ordered,
            grid=(1,),
            out_shape=(arr(where.shape, jnp.int32),)
            + tuple(out_shape)
            + tuple(arr(h.shape, h.dtype) for h in held),
            in_specs=[place] + specs + [anywhere] * (len(held) + len(after)),
            out_specs=(place,) + tuple(spec for _ in out_shape) + (anywhere,) * len(held),
            scratch_shapes=scratch,
            input_output_aliases={1 + inner + i: 1 + outer + i for i in range(len(held))},
            compiler_params=pltpu.CompilerParams(vmem_limit_bytes=mib << 20),
            cost_estimate=pl.CostEstimate(flops=flops, bytes_accessed=6 << 20, transcendentals=0),
            name=name,
        )(order[0], *args, *held, *after)
        order[0] = made[0]
        return made[1:]

    def z_hops(value):
        return [along_chips(value, step) for step in range(1, chips)]

    def gather_stacks(piece, hops=None):
        stack = jnp.stack([piece] + (hops or z_hops(piece)))
        return stack, to_twin(stack)

    def scatter_pieces(shares, held=(), after=()):
        keep, received = shares
        shape = keep.shape[1:]
        outs = (arr(shape, F32),) + tuple(arr(shape, BF16) for _ in range(chips - 1))
        made = call(
            twin_add_kernel, "twin_add", outs, [], [spec, spec], shares, 1, 8, held, after
        )
        hops = [along_chips(s, step) for step, s in zip(range(1, chips), made[1:chips])]
        return [made[0]] + hops, made[chips:]

    line = [[2 * chip + c for chip in range(chips)] for c in range(2)]

    def swap_chips(value):
        return lax.all_to_all(value, "space", 0, 0, axis_index_groups=line, tiled=True)

    def scatter_swap(shares, held=(), after=()):
        flat = [v for pair in shares for v in pair]
        out = arr((chips, len(shares), half, rows, LANES), BF16)
        made = call(
            partial(twin_sums_kernel, len(shares)),
            "twin_sums",
            (out,),
            [],
            [spec] * len(flat),
            flat,
            1,
            16,
            held,
            after,
        )
        return swap_chips(made[0]), made[1:]

    def tiny_gather(value):
        chain = z_hops(value)[::-1] + [value]
        stack = jnp.stack(chain)
        twin = to_twin(stack)
        pair = jnp.where(core == 0, jnp.stack([stack, twin], 1), jnp.stack([twin, stack], 1))
        return lax.dynamic_slice_in_dim(jnp.concatenate([pair, pair]), chips - 1 - z, chips, 0)

    def to_output(pieces):
        count, split = pieces.shape[0], LANES // 2
        parts = pieces.reshape(count, half, spaces, across, LANES).transpose(2, 0, 1, 3, 4)
        got = lax.all_to_all(parts, "space", 0, 0, tiled=True)
        got = got.reshape(spaces, count, half, across, 2, split).transpose(1, 4, 2, 3, 0, 5)
        slab = got.reshape(count, cubes, across, channels)
        slab = jax.vmap(lambda v: slab_of(v, (frames, height, width, channels)))(slab)
        slab = slab.reshape(count, frames, height, width, sections, channels // sections)
        slab = lax.all_to_all(slab.transpose(4, 0, 1, 2, 3, 5), "section", 0, 0, tiled=True)
        return tuple(slab[:, i] for i in range(count))

    def own_channels(row):
        return lax.dynamic_slice_in_dim(row, space * lanes, lanes, row.ndim - 1)

    code = code_bits.reshape(-1).astype(BF16)
    code = jnp.pad(code, (0, -code.shape[0] % lanes)).reshape(-1, lanes)
    small = jnp.concatenate(
        [enc_gains, dec_gains, enc_shifts, dec_shifts, up_bias[None], down_bias[None]]
        + [up_proj.T, down_proj.T, code],
        axis=0,
    )
    recon_slab = cubes_of(picked(recon_grad, section))
    (small,) = call(lambda where: None, "first", (), [], [], (), 1, 8, (small,), (recon_slab,))
    small = tiny_gather(small).reshape(spaces, small.shape[0], lanes)
    heads = 14 + 2 * bits
    heading = small[:, :heads].transpose(1, 0, 2).reshape(heads, channels)
    table = jnp.pad(heading[:14].astype(F32), ((0, 2), (0, 0)))
    up_cols, down_cols = heading[14 : 14 + bits], heading[14 + bits :]
    count = clips * across * bits
    code_all = small[:, heads:].reshape(spaces, -1)[:, :count].reshape(spaces, clips, across, bits)
    signs = (2 * code_all - 1).transpose(1, 0, 2, 3).reshape(clips * rows, bits)

    def cube_map(columns, weight):
        size = weight.shape[0] // sections
        part = lax.dynamic_slice_in_dim(weight, section * size, size, 0)
        made = lax.dot_general(
            columns, part, (((1,), (1,)), ((), ())), preferred_element_type=F32
        )
        return made.astype(BF16).reshape(bits, -1, channels)

    def field_from(every):
        return every.transpose(1, 0, 2, 3).reshape(cubes, rows, channels)

    recon_cot = field_from(lax.all_gather(recon_slab, "space", axis=0))
    hidden = (jnp.dot(signs, up_cols, preferred_element_type=F32) + table[12]).astype(BF16)
    hidden_own = lax.dynamic_slice_in_dim(hidden, section * rows, rows, 0)
    grown = lax.dot_general(
        hidden_own, up_weight, (((1,), (1,)), ((), ())), preferred_element_type=F32
    )
    grown = (grown + upsample_bias.astype(F32)).astype(BF16)
    grown = grown.reshape(rows, own_cubes, channels).transpose(1, 0, 2)
    grown_own, grown_twin = gather_stacks(grown)

    def map_spec(index):
        shape = (sections, spaces, None, bits, own_cubes * channels // sections)
        return pl.BlockSpec(shape, lambda i: (0, 0, index, 0, 0))

    def with_twin(keep, send, *rest):
        return ((keep, to_twin(send)),) + rest

    slabs = cubes_of(picked(video_clips, section))
    slabs, up_cols, down_cols = call(
        lambda where: None,
        "begin",
        (),
        [],
        [],
        (),
        1,
        8,
        (slabs, up_cols, down_cols),
        (grown_own, recon_cot),
    )
    slabs = jnp.concatenate([slabs, cube_map(up_cols, up_weight), cube_map(down_cols, down_weight)])
    slabs = lax.all_gather(slabs, "space", axis=0)
    video = field_from(slabs[:, :cubes])
    maps = slabs[:, cubes:]
    (shares,) = with_twin(
        *call(
            partial(back_kernel, across, 1),
            "dec_back_two",
            (blocks_f, blocks_b),
            [wide, rim_f, arrival],
            [spec, hbm],
            (recon_cot, dec_convs),
        )
    )
    behind, _ = scatter_swap([shares])
    shares, dec_act, dec_stats, dec_mine, decoded_in = with_twin(
        *call(
            partial(first_conv_kernel, (True, across, group, members, 2, 8, 0)),
            "dec_conv_one",
            (blocks_f, blocks_b, full, stats_f, piece_b, full),
            [rim_b, patch, wide, product, arrival],
            [spec, spec, spec, hbm],
            (grown_own, grown_twin, table, dec_convs),
        )
    )
    ahead, (maps,) = scatter_pieces(shares, (maps,))
    maps = lax.all_gather(maps.reshape(spaces, 2, bits, -1), "section", axis=0)
    enc_keep, enc_send, enc_act, enc_stats, enc_mine = call(
        partial(first_conv_kernel, (False, across, group, members, 0, 4, 0)),
        "enc_conv_one",
        (blocks_f, blocks_b, full, stats_f, piece_b),
        [rim_b, patch, wide, product, arrival],
        [spec, spec, hbm],
        (video, table, enc_convs),
    )
    dec_act_two, dec_inner, dec_sums_two, enc_send = call(
        partial(mid_both_kernel, (group, members, 3, 9, 10, chips)),
        "dec_mid",
        (piece_b, piece_b, sums_f),
        [],
        [spec] * (chips + 2),
        (*ahead, behind[:, 0], table),
        1,
        8,
        (enc_send,),
    )
    inner_hops = z_hops(dec_inner)
    enc_pieces, _ = scatter_swap([(enc_keep, to_twin(enc_send))])
    enc_act_two, enc_kept, dec_inner = call(
        partial(mid_ahead_kernel, (group, members, 1, 5, 6, 1)),
        "enc_mid",
        (piece_b, piece_f),
        [],
        [spec] * 2,
        (enc_pieces[:, 0], table),
        1,
        8,
        (dec_inner,),
    )
    inner_own, inner_twin = gather_stacks(dec_inner, inner_hops)
    acts = jnp.broadcast_to(jnp.stack([dec_act_two, enc_act_two])[None], (chips, 2) + piece_b.shape)
    acts = swap_chips(acts)
    tiny_f = arr((rows + 2 * tiles, LANES), F32)
    grad_shares, tiny, dec_inner_full = with_twin(
        *call(
            partial(back_whole_kernel, (across, group, members, 2, 8, bits, 0)),
            "dec_back_one",
            (cubes_f, cubes_b, tiny_f, full),
            [
                wide,
                rim_f,
                arrival,
                pltpu.VMEM((tiles, cubes, rows, LANES), F32),
                pltpu.VMEM((cubes, rows, channels), BF16),
                pltpu.VMEM((8, channels), F32),
            ],
            [spec, spec, hbm, spec, spec, spec, spec, map_spec(0)],
            (inner_own, inner_twin, dec_convs, decoded_in, dec_stats, table, recon_cot, maps),
            mib=34,
        )
    )
    for hop in z_hops(tiny):
        tiny = tiny + hop
    tiny = tiny + to_twin(tiny)
    sign_grad = tiny[:rows, :bits].astype(BF16)

    def kernel_grad_of(act, cot, name, held=(), after=()):
        return call(
            partial(grad_only_kernel, across),
            name,
            (grad_b,),
            [rim_b, patch, grad_s],
            [spec, spec],
            (act, cot),
            held=held,
            after=after,
        )

    (dec_grad_one,) = kernel_grad_of(dec_act, dec_inner_full, "dec_grad_one")

    def parts_of(grad):
        parts = grad.reshape(sections, row_count // sections, channels)
        parts = lax.all_to_all(parts, "section", 0, 0, tiled=True)
        return jnp.sum(parts.astype(F32), axis=0).astype(BF16)

    shares, enc_cot, cot_mine, acts, dec_grad_one = with_twin(
        *call(
            partial(back_signs_kernel, (across, bits, 1)),
            "enc_back_two",
            (blocks_f, blocks_b, full, piece_b),
            [wide, rim_f, arrival],
            [spec, map_spec(1), hbm],
            (tiny, maps, enc_convs),
            held=(acts, dec_grad_one),
        )
    )
    acts_twin = to_twin(acts)
    enc_pieces, (dec_grad_one,) = scatter_pieces(shares, (dec_grad_one,))
    dec_one = parts_of(dec_grad_one)
    recon_keep, recon_send, dec_grad_two, _ = call(
        partial(second_conv_kernel, across, True, 1),
        "dec_conv_two",
        (blocks_f, blocks_b, grad_b, full),
        [rim_b, patch, wide, product, arrival, grad_s],
        [piece_spec(0), piece_spec(0), hbm, spec],
        (acts, acts_twin, dec_convs, recon_cot),
        mib=36,
    )
    enc_inner, enc_sums_two, recon_send, dec_grad_two = call(
        partial(mid_back_kernel, (group, members, 1, 5, chips)),
        "enc_mid_back",
        (piece_b, sums_f),
        [],
        [spec] * (chips + 2),
        (*enc_pieces, enc_kept, table),
        1,
        8,
        (recon_send, dec_grad_two),
    )
    einner_hops = z_hops(enc_inner)

    recon_shares = (recon_keep, to_twin(recon_send))
    encoded_keep, encoded_send, enc_act_two_full, enc_inner, dec_grad_two, dec_one = call(
        partial(second_conv_kernel, across, False, 1),
        "enc_conv_two",
        (cubes_f, cubes_b, full),
        [rim_b, patch, wide, product, arrival],
        [piece_spec(1), piece_spec(1), hbm],
        (acts, acts_twin, enc_convs),
        held=(enc_inner, dec_grad_two, dec_one),
    )
    dec_one = lax.all_gather(dec_one, "section", axis=0, tiled=True)
    dec_two = parts_of(dec_grad_two)
    einner_own, einner_twin = gather_stacks(enc_inner, einner_hops)
    encoded_shares = (encoded_keep, to_twin(encoded_send))
    shares, enc_inner_full = with_twin(
        *call(
            partial(back_stacked_kernel, across, 0),
            "enc_back_one",
            (blocks_f, blocks_b, full),
            [wide, rim_f, arrival],
            [spec, spec, hbm],
            (einner_own, einner_twin, enc_convs),
        )
    )
    enc_pieces, _ = scatter_pieces(shares)
    (enc_grad_two,) = kernel_grad_of(enc_act_two_full, enc_cot, "enc_grad_two")
    (enc_grad_one,) = kernel_grad_of(enc_act, enc_inner_full, "enc_grad_one")
    video_back, enc_sums_one, enc_grad_one = call(
        partial(last_back_kernel, (group, members, 0, 4, chips)),
        "enc_last",
        (piece_b, sums_f),
        [],
        [spec] * (chips + 4),
        (*enc_pieces, enc_mine, cot_mine, enc_stats, table),
        1,
        8,
        (enc_grad_one,),
        (dec_two,),
    )
    dec_two = lax.all_gather(dec_two, "section", axis=0, tiled=True)
    enc_two = lax.psum(enc_grad_two, "section")
    swapped, _ = scatter_swap([grad_shares, recon_shares, encoded_shares])
    totals = jnp.sum(swapped.astype(F32), axis=0)
    own_bias = own_channels(table[11])
    recon = totals[1] + jnp.concatenate([own_bias, own_bias]) + dec_mine.astype(F32)
    pieces = jnp.stack([recon.astype(BF16), video_back])

    def as_cubes(part):
        split = part.reshape(own_cubes, tiles, rows, LANES).transpose(0, 2, 1, 3)
        return split.reshape(own_cubes, rows, channels)

    swaps = range(1, sections)

    def section_swap(value, step):
        return lax.ppermute(value, "section", [(i, i ^ step) for i in range(sections)])

    def quarter_sum(grad):
        size = row_count // sections

        def part(step):
            return lax.dynamic_slice_in_dim(grad, (section ^ step) * size, size, 0)

        got = [section_swap(part(step), step) for step in swaps]
        total = part(0).astype(F32)
        for value in got:
            total = total + value.astype(F32)
        return total.astype(BF16)

    def by_section(value):
        every = jnp.stack([value] + [section_swap(value, step) for step in swaps])
        every = every.reshape((sections // 2, 2) + value.shape)
        every = jnp.where(section % 2 == 1, every[:, ::-1], every)
        every = jnp.where(section // 2 == 1, every[::-1], every)
        return every.reshape((sections,) + value.shape)

    enc_one_sum = quarter_sum(enc_grad_one)
    enc_one = by_section(enc_one_sum).reshape(row_count, channels)

    own = lax.dynamic_slice_in_dim(video, space * own_cubes, own_cubes, 0).astype(F32)
    encoded = as_cubes(totals[2]) + table[7] + own
    decoded_grad = as_cubes(totals[0])
    sign_wide = jnp.pad(sign_grad, ((0, 0), (0, channels - bits)))[None]
    encoded, decoded_grad = encoded.astype(BF16), decoded_grad.astype(BF16)
    both = jnp.concatenate([encoded, decoded_grad, sign_wide])

    signs_own = lax.dynamic_slice_in_dim(signs, section * rows, rows, 0)
    signs_own = jnp.concatenate([signs_own, jnp.ones((rows, 1), BF16)], axis=1)

    def through(bit_rows, field, weight):
        wave = jnp.einsum("rk,orc->koc", bit_rows, field, preferred_element_type=F32)
        wave = wave.astype(BF16).reshape(wave.shape[0], -1)
        return jnp.dot(wave, weight, preferred_element_type=F32)

    projected = jnp.concatenate(
        [through(sign_grad, encoded, down_weight), through(signs_own, decoded_grad, up_weight)]
    )
    both, projected, pieces = call(
        lambda where: None,
        "latent",
        (),
        [],
        [],
        (),
        1,
        8,
        (both, projected, pieces),
        (enc_one_sum,),
    )
    both = by_section(both)
    recon_out, video_out = to_output(pieces)
    for hop in z_hops(projected):
        projected = projected + hop
    projected = own_channels(projected + to_twin(projected))
    sign_total = jnp.sum(sign_grad.astype(F32), axis=0)
    biased = sign_total[:, None] * down_bias.astype(F32)[None]
    projected = jnp.concatenate([projected[:bits] + biased, projected[bits:]])
    sign_all = both[:, 2 * own_cubes, :, :bits].reshape(clips * rows, bits)

    def latent_rows(part):
        return part.transpose(0, 2, 1, 3).reshape(clips * rows, own_cubes * channels)

    enc_rows = latent_rows(both[:, :own_cubes])
    dec_rows = latent_rows(both[:, own_cubes : 2 * own_cubes])
    inner_grad = jnp.dot(sign_all, down_cols, preferred_element_type=F32).astype(BF16)

    def outer(left, right):
        return lax.dot_general(left, right, (((0,), (0,)), ((), ())), preferred_element_type=F32)

    down_weight_grad = outer(enc_rows, inner_grad)
    up_weight_grad = outer(dec_rows, hidden)
    upsample_grad = jnp.sum(dec_rows.astype(F32), axis=0)
    down_bias_grad = jnp.sum(own_channels(inner_grad).astype(F32), axis=0)

    def own_sum(field):
        return own_channels(channel_sums(field.astype(F32)))[None]

    dec_sums_one = own_channels(tiny[rows:].reshape(2, channels))
    enc_sums_one, enc_sums_two, dec_sums_two = (
        s[:, :lanes] for s in (enc_sums_one, enc_sums_two, dec_sums_two)
    )
    small_grads = jnp.concatenate(
        [
            enc_sums_one[1:],
            enc_sums_two[1:],
            enc_sums_one[:1],
            enc_sums_two[:1],
            own_sum(enc_inner_full),
            own_sum(enc_cot),
            dec_sums_one[1:],
            dec_sums_two[1:],
            dec_sums_one[:1],
            dec_sums_two[:1],
            own_sum(dec_inner_full),
            own_sum(recon_cot),
            projected,
        ]
    )
    step = 1
    while step < sections:
        route = [(i, i ^ step) for i in range(sections)]
        small_grads = small_grads + lax.ppermute(small_grads, "section", route)
        step *= 2

    return (
        recon_out,
        video_out,
        jnp.stack([enc_one, enc_two]).astype(F32),
        small_grads[0:2],
        small_grads[2:6],
        down_weight_grad,
        down_bias_grad,
        small_grads[12 : 12 + bits].T,
        small_grads[12 + bits : 12 + 2 * bits].T,
        small_grads[12 + 2 * bits],
        up_weight_grad,
        upsample_grad,
        jnp.stack([dec_one, dec_two]).astype(F32),
        small_grads[6:8],
        small_grads[8:12],
    )


def general_body(
    video_clips,
    code_bits,
    recon_grad,
    enc_convs,
    enc_gains,
    enc_shifts,
    down_weight,
    down_bias,
    down_proj,
    up_proj,
    up_bias,
    up_weight,
    upsample_bias,
    dec_convs,
    dec_gains,
    dec_shifts,
):
    section = lax.axis_index("section")
    space = lax.axis_index("space")
    sections = lax.axis_size("section")
    spaces = lax.axis_size("space")
    chips = chips_of()
    clips, frames, height, width, channels = video_clips.shape
    extent = (frames, height, width, channels)
    across = width // CUBE
    bits = code_bits.shape[-1]
    rows = spaces * across
    cubes = CUBE**3
    own_cubes = cubes // spaces
    members = float(cubes * rows * (channels // GROUPS))
    group = channels // GROUPS
    first_space = (space == 0).astype(F32)

    lanes = down_bias.shape[0]
    code = code_bits.reshape(-1).astype(BF16)
    code = jnp.pad(code, (0, -code.shape[0] % lanes)).reshape(-1, lanes)
    small = jnp.concatenate(
        [
            enc_gains,
            dec_gains,
            enc_shifts,
            dec_shifts,
            up_bias[None],
            down_bias[None],
            up_proj.T,
            down_proj.T,
            code,
        ],
        axis=0,
    )
    small = gathered(small).reshape(spaces, small.shape[0], lanes)
    heads = 14 + 2 * bits
    table = small[:, :heads].transpose(1, 0, 2).reshape(heads, channels)
    wide_table = table.astype(F32)
    e_gains, d_gains = wide_table[0:2], wide_table[2:4]
    e_shifts, d_shifts = wide_table[4:8], wide_table[8:12]
    up_row, down_row = wide_table[12], wide_table[13]
    up_cols, down_cols = table[14 : 14 + bits], table[14 + bits :]
    count = clips * across * bits
    code_all = small[:, heads:].reshape(spaces, -1)[:, :count].reshape(spaces, clips, across, bits)
    signs = (2 * code_all - 1).transpose(1, 0, 2, 3).reshape(clips * rows, bits)

    slabs = jnp.stack(
        [cubes_of(picked(video_clips, section)), cubes_of(picked(recon_grad, section))]
    )
    hidden = (jnp.dot(signs, up_cols, preferred_element_type=F32) + up_row).astype(BF16)
    hidden_own = lax.dynamic_slice_in_dim(hidden, section * rows, rows, 0)
    grown = lax.dot_general(
        hidden_own, up_weight, (((1,), (1,)), ((), ())), preferred_element_type=F32
    )
    grown = (grown + upsample_bias.astype(F32)).astype(BF16)
    grown = grown.reshape(rows, own_cubes, channels).transpose(1, 0, 2)
    decoded_in = gathered(grown).reshape(cubes, rows, channels)
    both = gathered(slabs)
    video = field_of(both[:, :, 0])
    recon_cot = field_of(both[:, :, 1])

    maps = jnp.stack(
        [
            lax.dot_general(
                up_cols, up_weight, (((1,), (1,)), ((), ())), preferred_element_type=F32
            ),
            lax.dot_general(
                down_cols, down_weight, (((1,), (1,)), ((), ())), preferred_element_type=F32
            ),
        ]
    ).astype(BF16)
    maps = gathered(maps).reshape(spaces, 2, bits, own_cubes, channels)
    up_map, down_map = maps[:, 0], maps[:, 1]

    first, offset = rows_here(enc_convs)
    enc_w, dec_w = aligned(enc_convs), aligned(dec_convs)
    half_members = members

    def ahead(inputs, weights, gains, shifts):
        wide = inputs.astype(F32)
        flat_one, spread_one = normed(
            wide, channel_sums(wide), channel_sums(wide * wide), group, members
        )
        norm_one = flat_one * gains[0] + shifts[0]
        logistic = jax.nn.sigmoid(norm_one)
        act_one = (norm_one * logistic).astype(BF16)
        part, patch_one = conv_part(act_one, weights[0], first, across)
        middle = scattered(to_blocks(part)) + own_lanes(shifts[2])
        sums = pair_summed(jnp.stack([channel_sums(middle), channel_sums(middle * middle)]))
        flat_two, spread_two = normed(middle, sums[0], sums[1], group, half_members)
        norm_two = flat_two * own_lanes(gains[1]) + own_lanes(shifts[1])
        act_two = (norm_two * jax.nn.sigmoid(norm_two)).astype(BF16)
        act_two = from_blocks(gathered(act_two))
        branch, patch_two = conv_part(act_two, weights[1], first, across)
        return (
            branch,
            (flat_one, spread_one, norm_one, patch_one),
            (flat_two, spread_two, norm_two, patch_two),
        )

    def grads_two(spread_back, state, gains):
        flat, spread, norm, _ = state
        raw = scattered(to_blocks(spread_back))
        pre = raw * swish_slope(norm, jax.nn.sigmoid(norm))
        sums = pair_summed(jnp.stack([channel_sums(pre), channel_sums(pre * flat)]))
        gain = own_lanes(gains[1])
        total = group_means(sums[0] * gain, group, members)
        lined = group_means(sums[1] * gain, group, members)
        inner = (spread * (pre * gain - total - flat * lined)).astype(BF16)
        return inner, sums

    z, core = here()

    def spread_lanes(block_row):
        full = jnp.zeros(block_row.shape[:-1] + (channels,), F32)
        placed = lax.dynamic_update_slice_in_dim(
            full, block_row, z * block_row.shape[-1], full.ndim - 1
        )
        return jnp.where(core == 0, placed, 0.0)

    dec_branch, dec_one, dec_two = ahead(decoded_in, dec_w, d_gains, d_shifts)
    dec_inner, dec_sums_two = grads_two(
        convt_part(recon_cot, dec_w[1], first, across), dec_two, d_gains
    )
    dec_inner = from_blocks(gathered(dec_inner))
    back = convt_part(dec_inner, dec_w[0], first, across)
    flat_one, spread_one, norm_one, _ = dec_one
    pre = back * swish_slope(norm_one, jax.nn.sigmoid(norm_one))
    dec_sums_one = jnp.stack([channel_sums(pre), channel_sums(pre * flat_one)])
    total = group_means(dec_sums_one[0] * d_gains[0], group, members)
    lined = group_means(dec_sums_one[1] * d_gains[0], group, members)
    grad_part = spread_one * (pre * d_gains[0] - total - flat_one * lined)
    grad_part = grad_part + recon_cot.astype(F32) * first_space
    sign_part = jnp.einsum(
        "sorc,skoc->rk",
        grad_part.reshape(spaces, own_cubes, rows, channels).astype(BF16),
        up_map,
        preferred_element_type=F32,
    )
    sign_grad = summed(sign_part).astype(BF16)
    enc_cot = jnp.einsum("rk,skoc->sorc", sign_grad, down_map, preferred_element_type=F32)
    enc_cot = enc_cot.astype(BF16).reshape(cubes, rows, channels)

    enc_branch, enc_one, enc_two = ahead(video, enc_w, e_gains, e_shifts)
    enc_inner, enc_sums_two = grads_two(
        convt_part(enc_cot, enc_w[1], first, across), enc_two, e_gains
    )
    enc_inner = from_blocks(gathered(enc_inner))
    back = scattered(to_blocks(convt_part(enc_inner, enc_w[0], first, across)))
    flat, norm = own_block(enc_one[0]), own_block(enc_one[2])
    pre = back * swish_slope(norm, jax.nn.sigmoid(norm))
    enc_sums_one = pair_summed(jnp.stack([channel_sums(pre), channel_sums(pre * flat)]))
    gain = own_lanes(e_gains[0])
    total = group_means(enc_sums_one[0] * gain, group, members)
    lined = group_means(enc_sums_one[1] * gain, group, members)
    video_back = own_lanes(enc_one[1]) * (pre * gain - total - flat * lined)
    video_back = (own_block(enc_cot).astype(F32) + video_back).astype(BF16)
    recon = scattered(to_blocks(dec_branch)) + own_lanes(d_shifts[3])
    recon = (recon + own_block(decoded_in).astype(F32)).astype(BF16)

    def to_output(block):
        half, _, lane_count = block.shape
        pieces = block.reshape(half, spaces, across, lane_count).transpose(1, 0, 2, 3)
        swapped = lax.all_to_all(pieces, "space", 0, 0, tiled=True)
        slab = swapped.reshape(chips, 2, half, across, lane_count).transpose(1, 2, 3, 0, 4)
        slab = slab_of(slab.reshape(cubes, across, channels), extent)
        parted = slab.reshape(frames, height, width, sections, channels // sections)
        return lax.all_to_all(parted.transpose(3, 0, 1, 2, 4), "section", 0, 0, tiled=True)

    grads = [
        kernel_grad(enc_one[3], enc_inner),
        kernel_grad(enc_two[3], enc_cot),
        kernel_grad(dec_one[3], dec_inner),
        kernel_grad(dec_two[3], recon_cot),
    ]
    row_count = enc_convs.shape[1]
    grads = [
        lax.psum(lax.dynamic_slice_in_dim(g, offset, row_count, 0).astype(BF16), "section").astype(
            F32
        )
        for g in grads
    ]

    encoded = scattered(enc_branch.reshape(chips, 2, own_cubes, rows, channels))
    own = lambda v: lax.dynamic_slice_in_dim(v, space * own_cubes, own_cubes, 0).astype(F32)
    encoded = (encoded + e_shifts[3] + own(video)).astype(BF16)
    decoded_grad = scattered(grad_part.reshape(chips, 2, own_cubes, rows, channels)).astype(BF16)
    both = lax.all_gather(jnp.stack([encoded, decoded_grad]), "section", axis=0)
    both = both.transpose(1, 0, 3, 2, 4).reshape(2, clips * rows, own_cubes * channels)
    enc_rows, dec_rows = both[0], both[1]
    sign_all = lax.all_gather(sign_grad, "section", axis=0, tiled=True)
    inner_grad = jnp.dot(sign_all, down_cols, preferred_element_type=F32).astype(BF16)

    def outer(left, right):
        return lax.dot_general(left, right, (((0,), (0,)), ((), ())), preferred_element_type=F32)

    down_weight_grad = outer(enc_rows, inner_grad)
    up_weight_grad = outer(dec_rows, hidden)
    upsample_grad = jnp.sum(dec_rows.astype(F32), axis=0)
    parts = jnp.stack(
        [
            jnp.dot(enc_rows, down_weight, preferred_element_type=F32),
            jnp.dot(dec_rows, up_weight, preferred_element_type=F32),
        ]
    )
    shares = lax.psum_scatter(parts, "space", scatter_dimension=2, tiled=True)
    inner_low = (shares[0] + down_bias.astype(F32)).astype(BF16)
    hidden_grad = shares[1].astype(BF16)
    down_proj_grad = outer(inner_low, sign_all)
    up_proj_grad = outer(hidden_grad, signs)
    up_bias_grad = jnp.sum(hidden_grad.astype(F32), axis=0)
    inner_share = lax.dynamic_slice_in_dim(inner_grad, space * lanes, lanes, 1)
    down_bias_grad = jnp.sum(inner_share.astype(F32), axis=0)

    one = lambda v: channel_sums(v.astype(F32))[None] * first_space
    small_grads = jnp.concatenate(
        [
            spread_lanes(enc_sums_one[1:]),
            spread_lanes(enc_sums_two[1:]),
            spread_lanes(enc_sums_one[:1]),
            spread_lanes(enc_sums_two[:1]),
            one(enc_inner),
            one(enc_cot),
            dec_sums_one[1:],
            spread_lanes(dec_sums_two[1:]),
            dec_sums_one[:1],
            spread_lanes(dec_sums_two[:1]),
            one(dec_inner),
            one(recon_cot),
        ],
        axis=0,
    )
    small_grads = lax.psum(small_grads, ("section", "space"))
    small_grads = lax.dynamic_slice_in_dim(small_grads, space * lanes, lanes, 1)

    return (
        to_output(recon),
        to_output(video_back),
        jnp.stack(grads[:2]),
        small_grads[0:2],
        small_grads[2:6],
        down_weight_grad,
        down_bias_grad,
        down_proj_grad,
        up_proj_grad,
        up_bias_grad,
        up_weight_grad,
        upsample_grad,
        jnp.stack(grads[2:]),
        small_grads[6:8],
        small_grads[8:12],
    )


def solution(mesh):
    lead, second, third = P("space"), P(None, "space"), P(None, None, "space")
    field = P(None, None, "space", None, "section")
    short = mesh.shape["space"] == 8 and mesh.shape["section"] == 4
    return jax.shard_map(
        fast_body if short else general_body,
        mesh=mesh,
        in_specs=(
            third,
            third,
            third,
            second,
            second,
            second,
            lead,
            lead,
            lead,
            lead,
            lead,
            lead,
            lead,
            second,
            second,
            second,
        ),
        out_specs=(
            field,
            field,
            second,
            second,
            second,
            lead,
            lead,
            lead,
            lead,
            lead,
            lead,
            lead,
            second,
            second,
            second,
        ),
        check_vma=False,
    )
```

```python
from functools import partial

import jax
import jax.numpy as jnp
from jax import lax
from jax.experimental import pallas as pl
from jax.experimental.pallas import tpu as pltpu
from jax.sharding import PartitionSpec as P

GROUPS = 32
CUBE = 4
LANES = 128
BF16 = jnp.bfloat16
F32 = jnp.float32


def swish_slope(values, logistic):
    return logistic * (1.0 + values * (1.0 - logistic))


def chips_of():
    return lax.axis_size("space") // 2


def along_chips(value, step):
    chips = chips_of()
    route = [(i, (i // 2 + step) % chips * 2 + i % 2) for i in range(2 * chips)]
    return lax.ppermute(value, "space", route)


def to_twin(value):
    return lax.ppermute(value, "space", [(i, i ^ 1) for i in range(lax.axis_size("space"))])


def here():
    index = lax.axis_index("space")
    return index // 2, index % 2


def ring_is_short():
    return chips_of() <= 4


def picked(value, index, axis=0):
    return lax.dynamic_index_in_dim(value, index, axis, keepdims=False)


def gathered(value):
    chips = chips_of()
    if not ring_is_short():
        return lax.all_gather(value, "space", axis=0).reshape((chips, 2) + value.shape)
    z, core = here()
    pieces = [value] + [along_chips(value, step) for step in range(1, chips)]
    stack = jnp.zeros((chips,) + value.shape, value.dtype)
    for step, piece in enumerate(pieces):
        stack = lax.dynamic_update_index_in_dim(stack, piece, (z - step) % chips, 0)
    other = to_twin(stack)
    first = jnp.where(core == 0, stack, other)
    second = jnp.where(core == 0, other, stack)
    return jnp.stack([first, second], axis=1)


def scattered(parts):
    chips = chips_of()
    if not ring_is_short():
        flat = parts.reshape((2 * chips,) + parts.shape[2:])
        return lax.psum_scatter(flat, "space", scatter_dimension=0, tiled=False)
    z, core = here()
    mine = picked(parts, core, 1)
    mine = mine + to_twin(picked(parts, 1 - core, 1).astype(BF16)).astype(F32)
    total = picked(mine, z)
    for step in range(1, chips):
        sent = picked(mine, (z + step) % chips).astype(BF16)
        total = total + along_chips(sent, step).astype(F32)
    return total


def summed(value):
    if not ring_is_short():
        return lax.psum(value, "space")
    total = value
    for step in range(1, chips_of()):
        total = total + along_chips(value, step)
    return total + to_twin(total)


def pair_summed(value):
    return value + to_twin(value)


def to_blocks(field):
    chips = chips_of()
    cubes, rows, channels = field.shape
    split = field.reshape(2, cubes // 2, rows, chips, channels // chips)
    return split.transpose(3, 0, 1, 2, 4)


def from_blocks(blocks):
    chips, _, half, rows, width = blocks.shape
    return blocks.transpose(1, 2, 3, 0, 4).reshape(2 * half, rows, chips * width)


def own_block(field):
    z, core = here()
    cubes, rows, channels = field.shape
    width = channels // chips_of()
    return lax.dynamic_slice(field, (core * (cubes // 2), 0, z * width), (cubes // 2, rows, width))


def own_lanes(row):
    z, _ = here()
    width = row.shape[-1] // chips_of()
    return lax.dynamic_slice_in_dim(row, z * width, width, row.ndim - 1)


def cubes_of(slab):
    frames, height, across, channels = slab.shape
    split = slab.reshape(frames, height, across // CUBE, CUBE, channels)
    return split.transpose(0, 1, 3, 2, 4).reshape(-1, across // CUBE, channels)


def slab_of(cubes, extent):
    frames, height, across, channels = extent
    split = cubes.reshape(frames, height, CUBE, across // CUBE, channels)
    return split.transpose(0, 1, 3, 2, 4).reshape(extent)


def field_of(slabs):
    chips, _, cubes, across, channels = slabs.shape
    flat = slabs.reshape(2 * chips, cubes, across, channels)
    return flat.transpose(1, 0, 2, 3).reshape(cubes, 2 * chips * across, channels)


def group_means(sums, width, members):
    groups = sums.reshape(sums.shape[:-1] + (-1, width))
    wide = jnp.broadcast_to(jnp.sum(groups, axis=-1, keepdims=True), groups.shape)
    return wide.reshape(sums.shape) / members


def rimmed(field, across):
    cubes, rows, channels = field.shape
    view = field.reshape(CUBE, CUBE, CUBE, rows // across, across, channels)
    none = (0, 0)
    above = jnp.pad(view[:, -1:, :, :-1], (none, none, none, (1, 0), none, none))
    below = jnp.pad(view[:, :1, :, 1:], (none, none, none, (0, 1), none, none))
    view = jnp.concatenate([above, view, below], axis=1)
    left = jnp.pad(view[:, :, -1:, :, :-1], (none, none, none, none, (1, 0), none))
    right = jnp.pad(view[:, :, :1, :, 1:], (none, none, none, none, (0, 1), none))
    view = jnp.concatenate([left, view, right], axis=2)
    view = jnp.pad(view, ((1, 1), none, none, none, none, none))
    return view.reshape(CUBE + 2, CUBE + 2, CUBE + 2, rows, channels)


def rows_here(weights):
    count = weights.shape[-2]
    start = count * lax.axis_index("space")
    return start // LANES, start % LANES


def block_count(count):
    worst = max(count * s % LANES for s in range(lax.axis_size("space")))
    return -(-(worst + count) // LANES)


def aligned(weights):
    _, offset = rows_here(weights)
    total = block_count(weights.shape[-2]) * LANES
    wide = jnp.zeros(weights.shape[:-2] + (total, weights.shape[-1]), weights.dtype)
    return lax.dynamic_update_slice_in_dim(wide, weights, offset, wide.ndim - 2)


def patches(field, first, count, across):
    cubes, rows, channels = field.shape
    wide = rimmed(field, across)
    per_tap = channels // LANES
    pieces = []
    for j in range(count):
        block = first + j
        tap, lane = jnp.minimum(block // per_tap, 26), block % per_tap
        piece = lax.dynamic_slice(
            wide,
            (tap // 9, tap // 3 % 3, tap % 3, 0, lane * LANES),
            (CUBE, CUBE, CUBE, rows, LANES),
        )
        pieces.append(piece.reshape(cubes * rows, LANES))
    return jnp.concatenate(pieces, axis=1)


def conv_part(field, weights, first, across):
    patch = patches(field, first, weights.shape[0] // LANES, across)
    out = jnp.dot(patch, weights, preferred_element_type=F32)
    return out.reshape(field.shape[:2] + (-1,)), patch


def convt_part(field, weights, first, across):
    cubes, rows, channels = field.shape
    spread = lax.dot_general(
        field.reshape(-1, channels),
        weights,
        (((1,), (1,)), ((), ())),
        preferred_element_type=F32,
    )
    count = weights.shape[0] // LANES
    fold = jax.linear_transpose(
        lambda v: patches(v, first, count, across),
        jax.ShapeDtypeStruct((cubes, rows, channels), F32),
    )
    return fold(spread)[0]


def kernel_grad(patch, field):
    return lax.dot_general(
        patch,
        field.reshape(-1, field.shape[-1]),
        (((0,), (0,)), ((), ())),
        preferred_element_type=F32,
    )


def normed(values, sums, squares, width, members):
    average = group_means(sums, width, members)
    square = group_means(squares, width, members)
    spread = lax.rsqrt(square - average * average + 1e-06)
    return (values - average) * spread, spread


def channel_sums(values):
    return jnp.sum(values, axis=tuple(range(values.ndim - 1)))


VMEM_BYTES = 56 * 1024 * 1024


def kernels_fit(channels):
    return chips_of() * LANES == channels


def kernel_params():
    return pltpu.CompilerParams(vmem_limit_bytes=VMEM_BYTES)


def shifted(slabs, rows, valid):
    wide = pltpu.roll(slabs.astype(F32), rows % slabs.shape[1], 1)
    return jnp.where(valid, wide, 0.0)


def row_marks(shape, across):
    row = lax.broadcasted_iota(jnp.int32, shape, len(shape) - 2)
    return row, row % across


def fill_rim(field, rim, across):
    rows, channels = field.shape[1:]
    tiles = channels // LANES
    blank = jnp.zeros((CUBE + 2, CUBE + 2, rows, LANES), rim.dtype)
    for q in range(tiles):
        rim[q, 0] = blank
        rim[q, CUBE + 1] = blank

    def frame(f, carry):
        base = f * CUBE * CUBE
        row, column = row_marks((CUBE, rows, LANES), across)
        row6, column6 = row_marks((CUBE + 2, rows, LANES), across)
        for q in range(tiles):
            lanes = slice(q * LANES, (q + 1) * LANES)
            for h in range(CUBE):
                rim[q, f + 1, h + 1, 1 : CUBE + 1] = field[pl.ds(base + CUBE * h, CUBE), :, lanes]
            above = field[pl.ds(base + CUBE * (CUBE - 1), CUBE), :, lanes]
            rim[q, f + 1, 0, 1 : CUBE + 1] = shifted(above, across, row >= across).astype(rim.dtype)
            below = field[pl.ds(base, CUBE), :, lanes]
            rim[q, f + 1, CUBE + 1, 1 : CUBE + 1] = shifted(
                below, -across, row < rows - across
            ).astype(rim.dtype)
            left = rim[q, f + 1, :, CUBE]
            rim[q, f + 1, :, 0] = shifted(left, 1, column6 >= 1).astype(rim.dtype)
            right = rim[q, f + 1, :, 1]
            rim[q, f + 1, :, CUBE + 1] = shifted(right, -1, column6 < across - 1).astype(rim.dtype)
        return carry

    lax.fori_loop(0, CUBE, frame, 0)


def fold_rim(rim, across):
    tiles, rows = rim.shape[0], rim.shape[4]

    def frame(f, carry):
        row, _ = row_marks((CUBE, rows, LANES), across)
        _, column6 = row_marks((CUBE + 2, rows, LANES), across)
        for q in range(tiles):
            left = shifted(rim[q, f + 1, :, 0], -1, column6 < across - 1)
            rim[q, f + 1, :, CUBE] += left
            right = shifted(rim[q, f + 1, :, CUBE + 1], 1, column6 >= 1)
            rim[q, f + 1, :, 1] += right
            above = shifted(rim[q, f + 1, 0, 1 : CUBE + 1], -across, row < rows - across)
            rim[q, f + 1, CUBE, 1 : CUBE + 1] += above
            below = shifted(rim[q, f + 1, CUBE + 1, 1 : CUBE + 1], across, row >= across)
            rim[q, f + 1, 1, 1 : CUBE + 1] += below
        return carry

    lax.fori_loop(0, CUBE, frame, 0)


def tap_of(block, per_tap):
    tap = jnp.minimum(block // per_tap, 26)
    return block % per_tap, tap // 9, tap // 3 % 3, tap % 3


def fill_patch(rim, patch, first, count, start, size):
    rows = rim.shape[4]
    for j in range(count):
        q, f, h, w = tap_of(first + j, rim.shape[0])
        window = rim[
            q,
            pl.ds(f + start[0], size[0]),
            pl.ds(h + start[1], size[1]),
            pl.ds(w, CUBE),
        ]
        patch[:, j * LANES : (j + 1) * LANES] = window.reshape(
            size[0] * size[1] * CUBE * rows, LANES
        )


def add_taps(field, weights, rim, first):
    rows, channels = field.shape[1:]
    tiles = channels // LANES
    count = weights.shape[0] // LANES
    blank = jnp.zeros((CUBE + 2, CUBE + 2, rows, LANES), F32)

    def clear(f, carry):
        for q in range(tiles):
            rim[q, f] = blank
        return carry

    lax.fori_loop(0, CUBE + 2, clear, 0)
    spread_rows = CUBE * CUBE * rows

    def frame(f, carry):
        source = field[pl.ds(f * CUBE * CUBE, CUBE * CUBE)].reshape(spread_rows, channels)
        for j in range(0, count, 2):
            wide = min(2, count - j)
            spread = lax.dot_general(
                source,
                weights[j * LANES : (j + wide) * LANES, :],
                (((1,), (1,)), ((), ())),
                preferred_element_type=F32,
            )
            for i in range(wide):
                q, tf, th, tw = tap_of(first + j + i, tiles)
                rim[q, f + tf, pl.ds(th, CUBE), pl.ds(tw, CUBE)] += spread[
                    :, i * LANES : (i + 1) * LANES
                ].reshape(CUBE, CUBE, rows, LANES)
        return carry

    lax.fori_loop(0, CUBE, frame, 0)


def group_totals(row, width):
    lanes = row.shape[1]
    lane = lax.broadcasted_iota(jnp.int32, row.shape, 1)
    step = 1
    while step < width:
        before = pltpu.roll(row, step, 1)
        after = pltpu.roll(row, lanes - step, 1)
        row = row + jnp.where(lane // step % 2 == 1, before, after)
        step *= 2
    return row


def row_sum(values):
    return jnp.sum(values.reshape(-1, values.shape[-1]), axis=0, keepdims=True)


def logistic_of(values):
    return 0.5 + 0.5 * jnp.tanh(0.5 * values)


def both_halves(row):
    return row + pltpu.roll(row, LANES // 2, 1)


def pack_pair(near, far, core):
    axis = near.ndim - 1
    lane = lax.broadcasted_iota(jnp.int32, near.shape, axis)
    low = lane < LANES // 2
    first = jnp.where(low, near, pltpu.roll(far, LANES // 2, axis))
    second = jnp.where(low, pltpu.roll(near, LANES // 2, axis), far)
    lead = lane * 0 + core == 0
    return jnp.where(lead, first, second), jnp.where(lead, second, first)


def unpack_pair(own, other, core):
    axis = own.ndim - 1
    lane = lax.broadcasted_iota(jnp.int32, own.shape, axis)
    low = lane < LANES // 2
    lead = lane * 0 + core == 0
    first, second = jnp.where(lead, own, other), jnp.where(lead, other, own)
    near = jnp.where(low, first, pltpu.roll(second, LANES // 2, axis))
    far = jnp.where(low, pltpu.roll(first, LANES // 2, axis), second)
    return near, far


def own_row(table, index, z, core):
    lanes = pl.ds(pl.multiple_of(z * LANES, LANES), LANES)
    row = table[index : index + 1, lanes]
    mine, _ = pack_pair(row, row, core)
    return mine


def pack_own(field, out, z, core):
    lanes = pl.ds(pl.multiple_of(z * LANES, LANES), LANES)
    half = field.shape[0] // 2

    def some(i, carry):
        near = field[pl.ds(8 * i, 8), :, lanes].astype(F32)
        far = field[pl.ds(half + 8 * i, 8), :, lanes].astype(F32)
        out[pl.ds(8 * i, 8)] = pack_pair(near, far, core)[0].astype(out.dtype)
        return carry

    lax.fori_loop(0, half // 8, some, 0)


def unpack_stacks(own, other, field, z, core, relative):
    chips, half = own.shape[:2]
    for hop in range(chips):
        place = lax.rem(z + chips - hop, chips) if relative else hop
        lanes = pl.ds(pl.multiple_of(place * LANES, LANES), LANES)

        def some(i, carry, hop=hop, lanes=lanes):
            mine = own[hop, pl.ds(8 * i, 8)].astype(F32)
            twin = other[hop, pl.ds(8 * i, 8)].astype(F32)
            near, far = unpack_pair(mine, twin, core)
            field[pl.ds(8 * i, 8), :, lanes] = near.astype(field.dtype)
            field[pl.ds(half + 8 * i, 8), :, lanes] = far.astype(field.dtype)
            return carry

        lax.fori_loop(0, half // 8, some, 0)


class Rows:
    def __init__(self, weights, index, offset, wide, sem):
        count = weights.shape[1]
        slack = wide.shape[0] - count
        blank = jnp.zeros((slack, wide.shape[1]), wide.dtype)
        wide[0:slack, :] = blank
        wide[count : count + slack, :] = blank
        target = wide.at[pl.ds(pl.multiple_of(offset, 64), count), :]
        self.copy = pltpu.make_async_copy(weights.at[index], target, sem)
        self.copy.start()

    def ready(self):
        self.copy.wait()


def norm_in(field, act, table, gain, shift, stats, group, members):
    cubes, rows, channels = field.shape

    def add(i, carry):
        values = field[pl.ds(4 * i, 4)].astype(F32)
        folded = values.reshape(-1, 8, channels)
        return (carry[0] + jnp.sum(folded, 0), carry[1] + jnp.sum(folded * folded, 0))

    blank = jnp.zeros((8, channels), F32)
    totals, squares = lax.fori_loop(0, cubes // 4, add, (blank, blank))
    sums = jnp.concatenate(
        [jnp.sum(totals, 0, keepdims=True), jnp.sum(squares, 0, keepdims=True)], axis=0
    )
    means = group_totals(sums, group) / members
    average = means[0:1]
    spread = lax.rsqrt(means[1:2] - average * average + 1e-06)
    stats[0:1, :] = average
    stats[1:2, :] = spread
    scale, start = table[gain : gain + 1, :], table[shift : shift + 1, :]

    def apply(i, carry):
        values = field[pl.ds(4 * i, 4)].astype(F32)
        flat = (values - average[None]) * spread[None]
        normal = flat * scale[None] + start[None]
        act[pl.ds(4 * i, 4)] = (normal * logistic_of(normal)).astype(act.dtype)
        return carry

    lax.fori_loop(0, cubes // 4, apply, 0)


def multiply(patch, wide, product):
    size = product.shape[1]

    for f in range(product.shape[0]):
        rows = slice(f * size, (f + 1) * size)
        product[f] = jnp.dot(patch[rows, :], wide[...], preferred_element_type=F32)


def share_blocks(frame_block, keep, send, core):
    tiles, cubes = keep.shape[0], CUBE * CUBE

    def pair(i, carry):
        for q in range(tiles):
            mine, twin = pack_pair(frame_block(i, q), frame_block(i + CUBE // 2, q), core)
            keep[q, pl.ds(i * cubes, cubes)] = mine
            send[q, pl.ds(i * cubes, cubes)] = twin.astype(send.dtype)
        return carry

    lax.fori_loop(0, CUBE // 2, pair, 0)


def of_product(product, rows):
    def block(f, q):
        return product[f, :, q * LANES : (q + 1) * LANES].reshape(CUBE * CUBE, rows, LANES)

    return block


def of_rim(rim):
    rows = rim.shape[4]

    def block(f, q):
        inner = rim[q, f + 1, 1 : CUBE + 1, 1 : CUBE + 1]
        return inner.reshape(CUBE * CUBE, rows, LANES)

    return block


def first_conv_kernel(settings, where, *refs):
    stacked, across, group, members, gain, shift, index = settings
    if stacked:
        own, other, table, weights, keep, send, act, stats, mine, field = refs[:10]
        rim, patch, wide, product, sem = refs[10:]
    else:
        field, table, weights, keep, send, act, stats, mine = refs[:8]
        rim, patch, wide, product, sem = refs[8:]
    first, offset, z, core = where[0], where[1], where[2], where[3]
    coming = Rows(weights, index, offset, wide, sem)
    if stacked:
        chips, count = own.shape[:2]
        for hop in range(chips):
            place = lax.rem(z + chips - hop, chips) * 2
            field[pl.ds((place + core) * count, count)] = own[hop]
            field[pl.ds((place + 1 - core) * count, count)] = other[hop]
    rows = field.shape[1]
    norm_in(field, act, table, gain, shift, stats, group, members)
    fill_rim(act, rim, across)
    fill_patch(rim, patch, first, patch.shape[1] // LANES, (0, 0), (CUBE, CUBE))
    coming.ready()
    multiply(patch, wide, product)
    share_blocks(of_product(product, rows), keep, send, core)
    pack_own(field, mine, z, core)


def fill_grad(patch, source, offset, grad, out):
    count = patch.shape[1]
    for j in range(0, count, 2 * LANES):
        lanes = slice(j, min(j + 2 * LANES, count))
        grad[lanes, :] = lax.dot_general(
            patch[:, lanes], source, (((0,), (0,)), ((), ())), preferred_element_type=F32
        )
    start = pl.multiple_of(offset, 64)
    out[...] = grad[pl.ds(start, out.shape[0]), :].astype(out.dtype)


def second_conv_kernel(across, with_grad, index, where, *refs):
    if with_grad:
        own, other, weights, cotangent, keep, send, out, field = refs[:8]
        rim, patch, wide, product, sem, grad = refs[8:]
    else:
        own, other, weights, keep, send, field = refs[:6]
        rim, patch, wide, product, sem = refs[6:]
    first, offset, z, core = where[0], where[1], where[2], where[3]
    rows, channels = field.shape[1:]
    coming = Rows(weights, index, offset, wide, sem)
    unpack_stacks(own, other, field, z, core, False)
    fill_rim(field, rim, across)
    fill_patch(rim, patch, first, patch.shape[1] // LANES, (0, 0), (CUBE, CUBE))
    coming.ready()
    multiply(patch, wide, product)
    if with_grad:
        share_blocks(of_product(product, rows), keep, send, core)
        fill_grad(patch, cotangent[...].reshape(-1, channels), offset, grad, out)
    else:

        def frame(f, carry):
            low = product[f, : CUBE * CUBE * rows // 2]
            high = product[f, CUBE * CUBE * rows // 2 :]
            lead = lax.broadcasted_iota(jnp.int32, low.shape, 1) * 0 + core == 0
            keep[f] = jnp.where(lead, low, high).reshape(keep.shape[1:])
            send[f] = jnp.where(lead, high, low).reshape(send.shape[1:]).astype(send.dtype)
            return carry

        lax.fori_loop(0, CUBE, frame, 0)


def grad_only_kernel(across, where, field, cotangent, out, rim, patch, grad):
    channels = field.shape[2]
    fill_rim(field, rim, across)
    fill_patch(rim, patch, where[0], patch.shape[1] // LANES, (0, 0), (CUBE, CUBE))
    fill_grad(patch, cotangent[...].reshape(-1, channels), where[1], grad, out)


def twin_add_kernel(where, keep, received, own, *sends):
    chips, z = keep.shape[0], where[2]
    own[...] = keep[z] + received[z].astype(F32)
    for hop, send in enumerate(sends):
        target = lax.rem(z + 1 + hop, chips)
        send[...] = (keep[target] + received[target].astype(F32)).astype(send.dtype)


def twin_sums_kernel(count, where, *refs):
    out = refs[2 * count]
    lanes = out.shape[-1]
    for i in range(count):
        keep, received = refs[2 * i], refs[2 * i + 1]
        for target in range(out.shape[0]):
            total = (keep[target] + received[target].astype(F32)).astype(out.dtype)
            if total.shape[-1] == lanes:
                out[target, i] = total
            else:
                parts = total.shape[-1] // lanes
                for cube in range(total.shape[0]):
                    for q in range(parts):
                        out[target, i, cube * parts + q] = total[cube, :, q * lanes : (q + 1) * lanes]


def total_of(pieces):
    if len(pieces) == 1:
        return jnp.sum(pieces[0][...].astype(F32), axis=0)
    total = pieces[0][...]
    for piece in pieces[1:]:
        total = total + piece[...].astype(F32)
    return total


def mid_norm(middle, table, gain, shift, z, core, group, members):
    sums = jnp.concatenate([row_sum(middle), row_sum(middle * middle)], axis=0)
    means = group_totals(both_halves(sums), group) / members
    average = means[0:1]
    spread = lax.rsqrt(means[1:2] - average * average + 1e-06)
    flat = (middle - average[None]) * spread[None]
    scale = own_row(table, gain, z, core)
    normal = flat * scale[None] + own_row(table, shift, z, core)[None]
    return flat, spread, normal, logistic_of(normal), scale


def mid_back(raw, normed_state, group, members):
    flat, spread, normal, logistic, scale = normed_state
    pre = raw * (logistic * (1.0 + normal * (1.0 - logistic)))
    sums = jnp.concatenate([row_sum(pre), row_sum(pre * flat)], axis=0)
    sums = both_halves(sums)
    means = group_totals(sums * scale, group) / members
    back = spread[None] * (pre * scale[None] - means[0:1][None] - flat * means[1:2][None])
    return back, sums


def mid_ahead_kernel(settings, where, *refs):
    group, members, gain, shift, bias, chips = settings
    pieces, table, act, kept = refs[:chips], refs[chips], refs[chips + 1], refs[chips + 2]
    z, core = where[2], where[3]
    middle = total_of(pieces) + own_row(table, bias, z, core)[None]
    kept[...] = middle
    state = mid_norm(middle, table, gain, shift, z, core, group, members)
    act[...] = (state[2] * state[3]).astype(act.dtype)


def mid_back_kernel(settings, where, *refs):
    group, members, gain, shift, chips = settings
    pieces, kept, table, inner, sums = refs[:chips], *refs[chips:]
    z, core = where[2], where[3]
    state = mid_norm(kept[...], table, gain, shift, z, core, group, members)
    back, rows = mid_back(total_of(pieces), state, group, members)
    inner[...] = back.astype(inner.dtype)
    sums[...] = rows


def mid_both_kernel(settings, where, *refs):
    group, members, gain, shift, bias, chips = settings
    ahead, behind = refs[:chips], refs[chips : chips + 1]
    table, act, inner, sums = refs[chips + 1 :]
    z, core = where[2], where[3]
    middle = total_of(ahead) + own_row(table, bias, z, core)[None]
    state = mid_norm(middle, table, gain, shift, z, core, group, members)
    act[...] = (state[2] * state[3]).astype(act.dtype)
    back, rows = mid_back(total_of(behind), state, group, members)
    inner[...] = back.astype(inner.dtype)
    sums[...] = rows


def last_back_kernel(settings, where, *refs):
    group, members, gain, shift, chips = settings
    pieces = refs[:chips]
    inputs, cotangent, stats, table, out, sums = refs[chips:]
    z, core = where[2], where[3]
    average, spread = own_row(stats, 0, z, core), own_row(stats, 1, z, core)
    flat = (inputs[...].astype(F32) - average[None]) * spread[None]
    scale = own_row(table, gain, z, core)
    normal = flat * scale[None] + own_row(table, shift, z, core)[None]
    state = (flat, spread, normal, logistic_of(normal), scale)
    back, rows = mid_back(total_of(pieces), state, group, members)
    out[...] = (cotangent[...].astype(F32) + back).astype(out.dtype)
    sums[...] = rows


def share_rim(field, coming, where, wide, rim, across, keep, send):
    coming.ready()
    add_taps(field, wide, rim, where[0])
    fold_rim(rim, across)
    share_blocks(of_rim(rim), keep, send, where[3])


def back_kernel(across, index, where, field, weights, keep, send, wide, rim, sem):
    coming = Rows(weights, index, where[1], wide, sem)
    share_rim(field, coming, where, wide, rim, across, keep, send)


def back_stacked_kernel(across, index, where, own, other, weights, keep, send, field, *work):
    wide, rim, sem = work
    coming = Rows(weights, index, where[1], wide, sem)
    unpack_stacks(own, other, field, where[2], where[3], True)
    share_rim(field, coming, where, wide, rim, across, keep, send)


def back_signs_kernel(settings, where, tiny, maps, weights, keep, send, field, mine, *work):
    across, bits, index = settings
    wide, rim, sem = work
    coming = Rows(weights, index, where[1], wide, sem)
    rows, channels = field.shape[1:]
    signs = tiny[0:rows, 0:bits].astype(BF16)
    parts, slabs = maps.shape[:2]
    size = field.shape[0] // (slabs * parts)

    def slab(s, carry):
        for p in range(parts):
            wave = jnp.dot(signs, maps[p, s], preferred_element_type=F32)
            for j in range(size):
                cube = (s * parts + p) * size + j
                field[cube] = wave[:, j * channels : (j + 1) * channels].astype(BF16)
        return carry

    lax.fori_loop(0, slabs, slab, 0)
    share_rim(field, coming, where, wide, rim, across, keep, send)
    pack_own(field, mine, where[2], where[3])


def back_whole_kernel(settings, where, *refs):
    across, group, members, gain, shift, bits, index = settings
    own, other, weights, inputs, stats, table, cotangent, maps = refs[:8]
    keep, send, tiny, field = refs[8:12]
    wide, rim, sem, pre_ref, low, sums = refs[12:]
    z, core = where[2], where[3]
    tiles, rows, channels = rim.shape[0], rim.shape[4], field.shape[2]
    size = CUBE * CUBE
    coming = Rows(weights, index, where[1], wide, sem)
    unpack_stacks(own, other, field, z, core, True)
    coming.ready()
    add_taps(field, wide, rim, where[0])
    fold_rim(rim, across)
    sums[...] = jnp.zeros(sums.shape, F32)
    block = of_rim(rim)

    def at(f, q):
        lanes = slice(q * LANES, (q + 1) * LANES)
        values = inputs[pl.ds(f * size, size), :, lanes].astype(F32)
        flat = (values - stats[0:1, lanes][None]) * stats[1:2, lanes][None]
        return flat, lanes

    def ahead(f, carry):
        for q in range(tiles):
            flat, lanes = at(f, q)
            normal = flat * table[gain : gain + 1, lanes][None] + table[shift : shift + 1, lanes][None]
            logistic = logistic_of(normal)
            pre = block(f, q) * (logistic * (1.0 + normal * (1.0 - logistic)))
            pre_ref[q, pl.ds(f * size, size)] = pre
            sums[0:1, lanes] += row_sum(pre)
            sums[1:2, lanes] += row_sum(pre * flat)
        return carry

    lax.fori_loop(0, CUBE, ahead, 0)
    means = group_totals(sums[0:2, :] * table[gain : gain + 1, :], group) / members
    lead_slab = (2 * z + core == 0).astype(F32)
    half = size // 2

    def behind(f, carry):
        for q in range(tiles):
            flat, lanes = at(f, q)
            scaled = pre_ref[q, pl.ds(f * size, size)] * table[gain : gain + 1, lanes][None]
            back = stats[1:2, lanes][None] * (
                scaled - means[0:1, lanes][None] - flat * means[1:2, lanes][None]
            )
            back = back + cotangent[pl.ds(f * size, size), :, lanes].astype(F32) * lead_slab
            low[pl.ds(f * size, size), :, lanes] = back.astype(BF16)
            lead = lax.broadcasted_iota(jnp.int32, (half, rows, LANES), 2) * 0 + core == 0
            keep[f, :, :, lanes] = jnp.where(lead, back[:half], back[half:])
            send[f, :, :, lanes] = jnp.where(lead, back[half:], back[:half]).astype(BF16)
        return carry

    lax.fori_loop(0, CUBE, behind, 0)
    parts, slabs = maps.shape[:2]
    size = field.shape[0] // (slabs * parts)

    def slab(s, total):
        for p in range(parts):
            cube = (s * parts + p) * size
            wave = jnp.concatenate([low[cube + j] for j in range(size)], axis=1)
            total = total + lax.dot_general(
                wave, maps[p, s], (((1,), (1,)), ((), ())), preferred_element_type=F32
            )
        return total

    signs = lax.fori_loop(0, slabs, slab, jnp.zeros((rows, bits), F32))
    tiny[...] = jnp.zeros(tiny.shape, F32)
    tiny[0:rows, 0:bits] = signs
    for q in range(tiles):
        lanes = slice(q * LANES, (q + 1) * LANES)
        tiny[rows + q : rows + q + 1, :] = sums[0:1, lanes]
        tiny[rows + tiles + q : rows + tiles + q + 1, :] = sums[1:2, lanes]


def fast_body(
    video_clips,
    code_bits,
    recon_grad,
    enc_convs,
    enc_gains,
    enc_shifts,
    down_weight,
    down_bias,
    down_proj,
    up_proj,
    up_bias,
    up_weight,
    upsample_bias,
    dec_convs,
    dec_gains,
    dec_shifts,
):
    section = lax.axis_index("section")
    space = lax.axis_index("space")
    z, core = here()
    sections = lax.axis_size("section")
    spaces = lax.axis_size("space")
    chips = chips_of()
    clips, frames, height, width, channels = video_clips.shape
    across = width // CUBE
    bits = code_bits.shape[-1]
    rows = spaces * across
    cubes = CUBE**3
    own_cubes = cubes // spaces
    half = cubes // 2
    group = channels // GROUPS
    members = float(cubes * rows * group)
    lanes = down_bias.shape[0]
    row_count = enc_convs.shape[1]
    total_rows = block_count(row_count) * LANES
    tiles = channels // LANES
    first, offset = rows_here(enc_convs)
    where = jnp.stack([first, offset, z, core]).astype(jnp.int32)

    def arr(shape, dtype):
        return jax.ShapeDtypeStruct(shape, dtype)

    full = arr((cubes, rows, channels), BF16)
    piece_b, piece_f = arr((half, rows, LANES), BF16), arr((half, rows, LANES), F32)
    blocks_f, blocks_b = arr((tiles, half, rows, LANES), F32), arr((tiles, half, rows, LANES), BF16)
    cubes_f = arr((CUBE, half // CUBE, rows, channels), F32)
    cubes_b = arr((CUBE, half // CUBE, rows, channels), BF16)
    stats_f = arr((8, channels), F32)
    sums_f = arr((2, LANES), F32)
    grad_b = arr((row_count, channels), BF16)
    rim_shape = (tiles, CUBE + 2, CUBE + 2, CUBE + 2, rows, LANES)
    rim_b, rim_f = pltpu.VMEM(rim_shape, BF16), pltpu.VMEM(rim_shape, F32)
    patch = pltpu.VMEM((cubes * rows, total_rows), BF16)
    wide = pltpu.VMEM((total_rows, channels), BF16)
    grad_s = pltpu.VMEM((total_rows, channels), F32)
    product = pltpu.VMEM((CUBE, cubes * rows // CUBE, channels), F32)
    spec = pl.BlockSpec(memory_space=pltpu.VMEM)
    conv_flops = 2 * cubes * rows * channels * total_rows

    hbm = pl.BlockSpec(memory_space=pltpu.HBM)
    enc_convs, dec_convs = (
        pltpu.with_memory_space_constraint(w, pltpu.HBM) for w in (enc_convs, dec_convs)
    )
    arrival = pltpu.SemaphoreType.DMA

    def piece_spec(index):
        return pl.BlockSpec((chips, None, half, rows, LANES), lambda i: (0, index, 0, 0, 0))

    order = [where]

    def call(kernel, name, out_shape, scratch, specs, args, flops=conv_flops, mib=28, held=(), after=()):
        place, anywhere = pl.BlockSpec(memory_space=pltpu.SMEM), pl.BlockSpec(memory_space=pl.ANY)
        inner, outer = len(args), len(out_shape)

        def ordered(*refs):
            skip = inner + len(held) + len(after)
            given, handed = refs[0], refs[1 + skip]
            for i in range(given.shape[0]):
                handed[i] = given[i]
            outs = 2 + skip
            scratch_refs = refs[outs + outer + len(held) :]
            kernel(given, *refs[1 : 1 + inner], *refs[outs : outs + outer], *scratch_refs)

        made = pl.pallas_call(
            ordered,
            grid=(1,),
            out_shape=(arr(where.shape, jnp.int32),)
            + tuple(out_shape)
            + tuple(arr(h.shape, h.dtype) for h in held),
            in_specs=[place] + specs + [anywhere] * (len(held) + len(after)),
            out_specs=(place,) + tuple(spec for _ in out_shape) + (anywhere,) * len(held),
            scratch_shapes=scratch,
            input_output_aliases={1 + inner + i: 1 + outer + i for i in range(len(held))},
            compiler_params=pltpu.CompilerParams(vmem_limit_bytes=mib << 20),
            cost_estimate=pl.CostEstimate(flops=flops, bytes_accessed=6 << 20, transcendentals=0),
            name=name,
        )(order[0], *args, *held, *after)
        order[0] = made[0]
        return made[1:]

    def z_hops(value):
        return [along_chips(value, step) for step in range(1, chips)]

    def gather_stacks(piece, hops=None):
        stack = jnp.stack([piece] + (hops or z_hops(piece)))
        return stack, to_twin(stack)

    def scatter_pieces(shares, held=(), after=()):
        keep, received = shares
        shape = keep.shape[1:]
        outs = (arr(shape, F32),) + tuple(arr(shape, BF16) for _ in range(chips - 1))
        made = call(
            twin_add_kernel, "twin_add", outs, [], [spec, spec], shares, 1, 8, held, after
        )
        hops = [along_chips(s, step) for step, s in zip(range(1, chips), made[1:chips])]
        return [made[0]] + hops, made[chips:]

    line = [[2 * chip + c for chip in range(chips)] for c in range(2)]

    def swap_chips(value):
        return lax.all_to_all(value, "space", 0, 0, axis_index_groups=line, tiled=True)

    def scatter_swap(shares, held=(), after=()):
        flat = [v for pair in shares for v in pair]
        out = arr((chips, len(shares), half, rows, LANES), BF16)
        made = call(
            partial(twin_sums_kernel, len(shares)),
            "twin_sums",
            (out,),
            [],
            [spec] * len(flat),
            flat,
            1,
            16,
            held,
            after,
        )
        return swap_chips(made[0]), made[1:]

    def tiny_gather(value):
        chain = z_hops(value)[::-1] + [value]
        stack = jnp.stack(chain)
        twin = to_twin(stack)
        pair = jnp.where(core == 0, jnp.stack([stack, twin], 1), jnp.stack([twin, stack], 1))
        return lax.dynamic_slice_in_dim(jnp.concatenate([pair, pair]), chips - 1 - z, chips, 0)

    def to_output(pieces):
        count, split = pieces.shape[0], LANES // 2
        parts = pieces.reshape(count, half, spaces, across, LANES).transpose(2, 0, 1, 3, 4)
        got = lax.all_to_all(parts, "space", 0, 0, tiled=True)
        got = got.reshape(spaces, count, half, across, 2, split).transpose(1, 4, 2, 3, 0, 5)
        slab = got.reshape(count, cubes, across, channels)
        slab = jax.vmap(lambda v: slab_of(v, (frames, height, width, channels)))(slab)
        slab = slab.reshape(count, frames, height, width, sections, channels // sections)
        slab = lax.all_to_all(slab.transpose(4, 0, 1, 2, 3, 5), "section", 0, 0, tiled=True)
        return tuple(slab[:, i] for i in range(count))

    def own_channels(row):
        return lax.dynamic_slice_in_dim(row, space * lanes, lanes, row.ndim - 1)

    code = code_bits.reshape(-1).astype(BF16)
    code = jnp.pad(code, (0, -code.shape[0] % lanes)).reshape(-1, lanes)
    small = jnp.concatenate(
        [enc_gains, dec_gains, enc_shifts, dec_shifts, up_bias[None], down_bias[None]]
        + [up_proj.T, down_proj.T, code],
        axis=0,
    )
    recon_slab = cubes_of(picked(recon_grad, section))
    (small,) = call(lambda where: None, "first", (), [], [], (), 1, 8, (small,), (recon_slab,))
    small = tiny_gather(small).reshape(spaces, small.shape[0], lanes)
    heads = 14 + 2 * bits
    heading = small[:, :heads].transpose(1, 0, 2).reshape(heads, channels)
    table = jnp.pad(heading[:14].astype(F32), ((0, 2), (0, 0)))
    up_cols, down_cols = heading[14 : 14 + bits], heading[14 + bits :]
    count = clips * across * bits
    code_all = small[:, heads:].reshape(spaces, -1)[:, :count].reshape(spaces, clips, across, bits)
    signs = (2 * code_all - 1).transpose(1, 0, 2, 3).reshape(clips * rows, bits)

    def cube_map(columns, weight):
        size = weight.shape[0] // sections
        part = lax.dynamic_slice_in_dim(weight, section * size, size, 0)
        made = lax.dot_general(
            columns, part, (((1,), (1,)), ((), ())), preferred_element_type=F32
        )
        return made.astype(BF16).reshape(bits, -1, channels)

    def field_from(every):
        return every.transpose(1, 0, 2, 3).reshape(cubes, rows, channels)

    recon_cot = field_from(lax.all_gather(recon_slab, "space", axis=0))
    hidden = (jnp.dot(signs, up_cols, preferred_element_type=F32) + table[12]).astype(BF16)
    hidden_own = lax.dynamic_slice_in_dim(hidden, section * rows, rows, 0)
    grown = lax.dot_general(
        hidden_own, up_weight, (((1,), (1,)), ((), ())), preferred_element_type=F32
    )
    grown = (grown + upsample_bias.astype(F32)).astype(BF16)
    grown = grown.reshape(rows, own_cubes, channels).transpose(1, 0, 2)
    grown_own, grown_twin = gather_stacks(grown)

    def map_spec(index):
        shape = (sections, spaces, None, bits, own_cubes * channels // sections)
        return pl.BlockSpec(shape, lambda i: (0, 0, index, 0, 0))

    def with_twin(keep, send, *rest):
        return ((keep, to_twin(send)),) + rest

    slabs = cubes_of(picked(video_clips, section))
    slabs, up_cols, down_cols = call(
        lambda where: None,
        "begin",
        (),
        [],
        [],
        (),
        1,
        8,
        (slabs, up_cols, down_cols),
        (grown_own, recon_cot),
    )
    slabs = jnp.concatenate([slabs, cube_map(up_cols, up_weight), cube_map(down_cols, down_weight)])
    slabs = lax.all_gather(slabs, "space", axis=0)
    video = field_from(slabs[:, :cubes])
    maps = slabs[:, cubes:]
    (shares,) = with_twin(
        *call(
            partial(back_kernel, across, 1),
            "dec_back_two",
            (blocks_f, blocks_b),
            [wide, rim_f, arrival],
            [spec, hbm],
            (recon_cot, dec_convs),
        )
    )
    behind, _ = scatter_swap([shares])
    shares, dec_act, dec_stats, dec_mine, decoded_in = with_twin(
        *call(
            partial(first_conv_kernel, (True, across, group, members, 2, 8, 0)),
            "dec_conv_one",
            (blocks_f, blocks_b, full, stats_f, piece_b, full),
            [rim_b, patch, wide, product, arrival],
            [spec, spec, spec, hbm],
            (grown_own, grown_twin, table, dec_convs),
        )
    )
    ahead, _ = scatter_pieces(shares)
    enc_keep, enc_send, enc_act, enc_stats, enc_mine = call(
        partial(first_conv_kernel, (False, across, group, members, 0, 4, 0)),
        "enc_conv_one",
        (blocks_f, blocks_b, full, stats_f, piece_b),
        [rim_b, patch, wide, product, arrival],
        [spec, spec, hbm],
        (video, table, enc_convs),
    )
    dec_act_two, dec_inner, dec_sums_two, enc_send, maps = call(
        partial(mid_both_kernel, (group, members, 3, 9, 10, chips)),
        "dec_mid",
        (piece_b, piece_b, sums_f),
        [],
        [spec] * (chips + 2),
        (*ahead, behind[:, 0], table),
        1,
        8,
        (enc_send, maps),
    )
    maps = lax.all_gather(maps.reshape(spaces, 2, bits, -1), "section", axis=0)
    inner_hops = z_hops(dec_inner)
    enc_pieces, _ = scatter_swap([(enc_keep, to_twin(enc_send))])
    enc_act_two, enc_kept, dec_inner = call(
        partial(mid_ahead_kernel, (group, members, 1, 5, 6, 1)),
        "enc_mid",
        (piece_b, piece_f),
        [],
        [spec] * 2,
        (enc_pieces[:, 0], table),
        1,
        8,
        (dec_inner,),
    )
    inner_own, inner_twin = gather_stacks(dec_inner, inner_hops)
    acts = jnp.broadcast_to(jnp.stack([dec_act_two, enc_act_two])[None], (chips, 2) + piece_b.shape)
    acts = swap_chips(acts)
    tiny_f = arr((rows + 2 * tiles, LANES), F32)
    grad_shares, tiny, dec_inner_full = with_twin(
        *call(
            partial(back_whole_kernel, (across, group, members, 2, 8, bits, 0)),
            "dec_back_one",
            (cubes_f, cubes_b, tiny_f, full),
            [
                wide,
                rim_f,
                arrival,
                pltpu.VMEM((tiles, cubes, rows, LANES), F32),
                pltpu.VMEM((cubes, rows, channels), BF16),
                pltpu.VMEM((8, channels), F32),
            ],
            [spec, spec, hbm, spec, spec, spec, spec, map_spec(0)],
            (inner_own, inner_twin, dec_convs, decoded_in, dec_stats, table, recon_cot, maps),
            mib=34,
        )
    )
    for hop in z_hops(tiny):
        tiny = tiny + hop
    tiny = tiny + to_twin(tiny)
    sign_grad = tiny[:rows, :bits].astype(BF16)

    def kernel_grad_of(act, cot, name, held=(), after=()):
        return call(
            partial(grad_only_kernel, across),
            name,
            (grad_b,),
            [rim_b, patch, grad_s],
            [spec, spec],
            (act, cot),
            held=held,
            after=after,
        )

    (dec_grad_one,) = kernel_grad_of(dec_act, dec_inner_full, "dec_grad_one")

    def parts_of(grad):
        parts = grad.reshape(sections, row_count // sections, channels)
        parts = lax.all_to_all(parts, "section", 0, 0, tiled=True)
        return jnp.sum(parts.astype(F32), axis=0).astype(BF16)

    shares, enc_cot, cot_mine, acts, dec_grad_one = with_twin(
        *call(
            partial(back_signs_kernel, (across, bits, 1)),
            "enc_back_two",
            (blocks_f, blocks_b, full, piece_b),
            [wide, rim_f, arrival],
            [spec, map_spec(1), hbm],
            (tiny, maps, enc_convs),
            held=(acts, dec_grad_one),
        )
    )
    acts_twin = to_twin(acts)
    enc_pieces, (dec_grad_one,) = scatter_pieces(shares, (dec_grad_one,))
    dec_one = parts_of(dec_grad_one)
    recon_keep, recon_send, dec_grad_two, _ = call(
        partial(second_conv_kernel, across, True, 1),
        "dec_conv_two",
        (blocks_f, blocks_b, grad_b, full),
        [rim_b, patch, wide, product, arrival, grad_s],
        [piece_spec(0), piece_spec(0), hbm, spec],
        (acts, acts_twin, dec_convs, recon_cot),
        mib=36,
    )
    enc_inner, enc_sums_two, recon_send, dec_grad_two = call(
        partial(mid_back_kernel, (group, members, 1, 5, chips)),
        "enc_mid_back",
        (piece_b, sums_f),
        [],
        [spec] * (chips + 2),
        (*enc_pieces, enc_kept, table),
        1,
        8,
        (recon_send, dec_grad_two),
    )
    einner_hops = z_hops(enc_inner)

    recon_shares = (recon_keep, to_twin(recon_send))
    encoded_keep, encoded_send, enc_act_two_full, enc_inner, dec_grad_two, dec_one = call(
        partial(second_conv_kernel, across, False, 1),
        "enc_conv_two",
        (cubes_f, cubes_b, full),
        [rim_b, patch, wide, product, arrival],
        [piece_spec(1), piece_spec(1), hbm],
        (acts, acts_twin, enc_convs),
        held=(enc_inner, dec_grad_two, dec_one),
    )
    dec_one = lax.all_gather(dec_one, "section", axis=0, tiled=True)
    dec_two = parts_of(dec_grad_two)
    einner_own, einner_twin = gather_stacks(enc_inner, einner_hops)
    encoded_shares = (encoded_keep, to_twin(encoded_send))
    shares, enc_inner_full = with_twin(
        *call(
            partial(back_stacked_kernel, across, 0),
            "enc_back_one",
            (blocks_f, blocks_b, full),
            [wide, rim_f, arrival],
            [spec, spec, hbm],
            (einner_own, einner_twin, enc_convs),
        )
    )
    enc_pieces, _ = scatter_pieces(shares)
    (enc_grad_two,) = kernel_grad_of(enc_act_two_full, enc_cot, "enc_grad_two")
    (enc_grad_one,) = kernel_grad_of(enc_act, enc_inner_full, "enc_grad_one")
    video_back, enc_sums_one, enc_grad_one, enc_grad_two = call(
        partial(last_back_kernel, (group, members, 0, 4, chips)),
        "enc_last",
        (piece_b, sums_f),
        [],
        [spec] * (chips + 4),
        (*enc_pieces, enc_mine, cot_mine, enc_stats, table),
        1,
        8,
        (enc_grad_one, enc_grad_two),
        (dec_two,),
    )
    dec_two = lax.all_gather(dec_two, "section", axis=0, tiled=True)
    swapped, _ = scatter_swap([grad_shares, recon_shares, encoded_shares])
    totals = jnp.sum(swapped.astype(F32), axis=0)
    own_bias = own_channels(table[11])
    recon = totals[1] + jnp.concatenate([own_bias, own_bias]) + dec_mine.astype(F32)
    pieces = jnp.stack([recon.astype(BF16), video_back])

    def as_cubes(part):
        split = part.reshape(own_cubes, tiles, rows, LANES).transpose(0, 2, 1, 3)
        return split.reshape(own_cubes, rows, channels)

    swaps = range(1, sections)

    def section_swap(value, step):
        return lax.ppermute(value, "section", [(i, i ^ step) for i in range(sections)])

    def quarter_sum(grad):
        size = row_count // sections

        def part(step):
            return lax.dynamic_slice_in_dim(grad, (section ^ step) * size, size, 0)

        got = [section_swap(part(step), step) for step in swaps]
        total = part(0).astype(F32)
        for value in got:
            total = total + value.astype(F32)
        return total.astype(BF16)

    def by_section(value):
        every = jnp.stack([value] + [section_swap(value, step) for step in swaps])
        every = every.reshape((sections // 2, 2) + value.shape)
        every = jnp.where(section % 2 == 1, every[:, ::-1], every)
        every = jnp.where(section // 2 == 1, every[::-1], every)
        return every.reshape((sections,) + value.shape)

    enc_one_sum = quarter_sum(enc_grad_one)
    enc_two = lax.all_gather(parts_of(enc_grad_two), "section", axis=0, tiled=True)

    own = lax.dynamic_slice_in_dim(video, space * own_cubes, own_cubes, 0).astype(F32)
    encoded = as_cubes(totals[2]) + table[7] + own
    decoded_grad = as_cubes(totals[0])
    sign_wide = jnp.pad(sign_grad, ((0, 0), (0, channels - bits)))[None]
    encoded, decoded_grad = encoded.astype(BF16), decoded_grad.astype(BF16)
    both = jnp.concatenate([encoded, decoded_grad, sign_wide])

    signs_own = lax.dynamic_slice_in_dim(signs, section * rows, rows, 0)
    signs_own = jnp.concatenate([signs_own, jnp.ones((rows, 1), BF16)], axis=1)

    def through(bit_rows, field, weight):
        wave = jnp.einsum("rk,orc->koc", bit_rows, field, preferred_element_type=F32)
        wave = wave.astype(BF16).reshape(wave.shape[0], -1)
        return jnp.dot(wave, weight, preferred_element_type=F32)

    projected = jnp.concatenate(
        [through(sign_grad, encoded, down_weight), through(signs_own, decoded_grad, up_weight)]
    )
    both, projected, pieces, enc_one_sum = call(
        lambda where: None,
        "latent",
        (),
        [],
        [],
        (),
        1,
        8,
        (both, projected, pieces, enc_one_sum),
    )
    enc_one = by_section(enc_one_sum).reshape(row_count, channels)
    both = by_section(both)
    recon_out, video_out = to_output(pieces)
    for hop in z_hops(projected):
        projected = projected + hop
    projected = own_channels(projected + to_twin(projected))
    sign_total = jnp.sum(sign_grad.astype(F32), axis=0)
    biased = sign_total[:, None] * down_bias.astype(F32)[None]
    projected = jnp.concatenate([projected[:bits] + biased, projected[bits:]])
    sign_all = both[:, 2 * own_cubes, :, :bits].reshape(clips * rows, bits)

    def latent_rows(part):
        return part.transpose(0, 2, 1, 3).reshape(clips * rows, own_cubes * channels)

    enc_rows = latent_rows(both[:, :own_cubes])
    dec_rows = latent_rows(both[:, own_cubes : 2 * own_cubes])
    inner_grad = jnp.dot(sign_all, down_cols, preferred_element_type=F32).astype(BF16)

    def outer(left, right):
        return lax.dot_general(left, right, (((0,), (0,)), ((), ())), preferred_element_type=F32)

    down_weight_grad = outer(enc_rows, inner_grad)
    up_weight_grad = outer(dec_rows, hidden)
    upsample_grad = jnp.sum(dec_rows.astype(F32), axis=0)
    down_bias_grad = jnp.sum(own_channels(inner_grad).astype(F32), axis=0)

    def own_sum(field):
        return own_channels(channel_sums(field.astype(F32)))[None]

    dec_sums_one = own_channels(tiny[rows:].reshape(2, channels))
    enc_sums_one, enc_sums_two, dec_sums_two = (
        s[:, :lanes] for s in (enc_sums_one, enc_sums_two, dec_sums_two)
    )
    small_grads = jnp.concatenate(
        [
            enc_sums_one[1:],
            enc_sums_two[1:],
            enc_sums_one[:1],
            enc_sums_two[:1],
            own_sum(enc_inner_full),
            own_sum(enc_cot),
            dec_sums_one[1:],
            dec_sums_two[1:],
            dec_sums_one[:1],
            dec_sums_two[:1],
            own_sum(dec_inner_full),
            own_sum(recon_cot),
            projected,
        ]
    )
    step = 1
    while step < sections:
        route = [(i, i ^ step) for i in range(sections)]
        small_grads = small_grads + lax.ppermute(small_grads, "section", route)
        step *= 2

    return (
        recon_out,
        video_out,
        jnp.stack([enc_one, enc_two]).astype(F32),
        small_grads[0:2],
        small_grads[2:6],
        down_weight_grad,
        down_bias_grad,
        small_grads[12 : 12 + bits].T,
        small_grads[12 + bits : 12 + 2 * bits].T,
        small_grads[12 + 2 * bits],
        up_weight_grad,
        upsample_grad,
        jnp.stack([dec_one, dec_two]).astype(F32),
        small_grads[6:8],
        small_grads[8:12],
    )


def general_body(
    video_clips,
    code_bits,
    recon_grad,
    enc_convs,
    enc_gains,
    enc_shifts,
    down_weight,
    down_bias,
    down_proj,
    up_proj,
    up_bias,
    up_weight,
    upsample_bias,
    dec_convs,
    dec_gains,
    dec_shifts,
):
    section = lax.axis_index("section")
    space = lax.axis_index("space")
    sections = lax.axis_size("section")
    spaces = lax.axis_size("space")
    chips = chips_of()
    clips, frames, height, width, channels = video_clips.shape
    extent = (frames, height, width, channels)
    across = width // CUBE
    bits = code_bits.shape[-1]
    rows = spaces * across
    cubes = CUBE**3
    own_cubes = cubes // spaces
    members = float(cubes * rows * (channels // GROUPS))
    group = channels // GROUPS
    first_space = (space == 0).astype(F32)

    lanes = down_bias.shape[0]
    code = code_bits.reshape(-1).astype(BF16)
    code = jnp.pad(code, (0, -code.shape[0] % lanes)).reshape(-1, lanes)
    small = jnp.concatenate(
        [
            enc_gains,
            dec_gains,
            enc_shifts,
            dec_shifts,
            up_bias[None],
            down_bias[None],
            up_proj.T,
            down_proj.T,
            code,
        ],
        axis=0,
    )
    small = gathered(small).reshape(spaces, small.shape[0], lanes)
    heads = 14 + 2 * bits
    table = small[:, :heads].transpose(1, 0, 2).reshape(heads, channels)
    wide_table = table.astype(F32)
    e_gains, d_gains = wide_table[0:2], wide_table[2:4]
    e_shifts, d_shifts = wide_table[4:8], wide_table[8:12]
    up_row, down_row = wide_table[12], wide_table[13]
    up_cols, down_cols = table[14 : 14 + bits], table[14 + bits :]
    count = clips * across * bits
    code_all = small[:, heads:].reshape(spaces, -1)[:, :count].reshape(spaces, clips, across, bits)
    signs = (2 * code_all - 1).transpose(1, 0, 2, 3).reshape(clips * rows, bits)

    slabs = jnp.stack(
        [cubes_of(picked(video_clips, section)), cubes_of(picked(recon_grad, section))]
    )
    hidden = (jnp.dot(signs, up_cols, preferred_element_type=F32) + up_row).astype(BF16)
    hidden_own = lax.dynamic_slice_in_dim(hidden, section * rows, rows, 0)
    grown = lax.dot_general(
        hidden_own, up_weight, (((1,), (1,)), ((), ())), preferred_element_type=F32
    )
    grown = (grown + upsample_bias.astype(F32)).astype(BF16)
    grown = grown.reshape(rows, own_cubes, channels).transpose(1, 0, 2)
    decoded_in = gathered(grown).reshape(cubes, rows, channels)
    both = gathered(slabs)
    video = field_of(both[:, :, 0])
    recon_cot = field_of(both[:, :, 1])

    maps = jnp.stack(
        [
            lax.dot_general(
                up_cols, up_weight, (((1,), (1,)), ((), ())), preferred_element_type=F32
            ),
            lax.dot_general(
                down_cols, down_weight, (((1,), (1,)), ((), ())), preferred_element_type=F32
            ),
        ]
    ).astype(BF16)
    maps = gathered(maps).reshape(spaces, 2, bits, own_cubes, channels)
    up_map, down_map = maps[:, 0], maps[:, 1]

    first, offset = rows_here(enc_convs)
    enc_w, dec_w = aligned(enc_convs), aligned(dec_convs)
    half_members = members

    def ahead(inputs, weights, gains, shifts):
        wide = inputs.astype(F32)
        flat_one, spread_one = normed(
            wide, channel_sums(wide), channel_sums(wide * wide), group, members
        )
        norm_one = flat_one * gains[0] + shifts[0]
        logistic = jax.nn.sigmoid(norm_one)
        act_one = (norm_one * logistic).astype(BF16)
        part, patch_one = conv_part(act_one, weights[0], first, across)
        middle = scattered(to_blocks(part)) + own_lanes(shifts[2])
        sums = pair_summed(jnp.stack([channel_sums(middle), channel_sums(middle * middle)]))
        flat_two, spread_two = normed(middle, sums[0], sums[1], group, half_members)
        norm_two = flat_two * own_lanes(gains[1]) + own_lanes(shifts[1])
        act_two = (norm_two * jax.nn.sigmoid(norm_two)).astype(BF16)
        act_two = from_blocks(gathered(act_two))
        branch, patch_two = conv_part(act_two, weights[1], first, across)
        return (
            branch,
            (flat_one, spread_one, norm_one, patch_one),
            (flat_two, spread_two, norm_two, patch_two),
        )

    def grads_two(spread_back, state, gains):
        flat, spread, norm, _ = state
        raw = scattered(to_blocks(spread_back))
        pre = raw * swish_slope(norm, jax.nn.sigmoid(norm))
        sums = pair_summed(jnp.stack([channel_sums(pre), channel_sums(pre * flat)]))
        gain = own_lanes(gains[1])
        total = group_means(sums[0] * gain, group, members)
        lined = group_means(sums[1] * gain, group, members)
        inner = (spread * (pre * gain - total - flat * lined)).astype(BF16)
        return inner, sums

    z, core = here()

    def spread_lanes(block_row):
        full = jnp.zeros(block_row.shape[:-1] + (channels,), F32)
        placed = lax.dynamic_update_slice_in_dim(
            full, block_row, z * block_row.shape[-1], full.ndim - 1
        )
        return jnp.where(core == 0, placed, 0.0)

    dec_branch, dec_one, dec_two = ahead(decoded_in, dec_w, d_gains, d_shifts)
    dec_inner, dec_sums_two = grads_two(
        convt_part(recon_cot, dec_w[1], first, across), dec_two, d_gains
    )
    dec_inner = from_blocks(gathered(dec_inner))
    back = convt_part(dec_inner, dec_w[0], first, across)
    flat_one, spread_one, norm_one, _ = dec_one
    pre = back * swish_slope(norm_one, jax.nn.sigmoid(norm_one))
    dec_sums_one = jnp.stack([channel_sums(pre), channel_sums(pre * flat_one)])
    total = group_means(dec_sums_one[0] * d_gains[0], group, members)
    lined = group_means(dec_sums_one[1] * d_gains[0], group, members)
    grad_part = spread_one * (pre * d_gains[0] - total - flat_one * lined)
    grad_part = grad_part + recon_cot.astype(F32) * first_space
    sign_part = jnp.einsum(
        "sorc,skoc->rk",
        grad_part.reshape(spaces, own_cubes, rows, channels).astype(BF16),
        up_map,
        preferred_element_type=F32,
    )
    sign_grad = summed(sign_part).astype(BF16)
    enc_cot = jnp.einsum("rk,skoc->sorc", sign_grad, down_map, preferred_element_type=F32)
    enc_cot = enc_cot.astype(BF16).reshape(cubes, rows, channels)

    enc_branch, enc_one, enc_two = ahead(video, enc_w, e_gains, e_shifts)
    enc_inner, enc_sums_two = grads_two(
        convt_part(enc_cot, enc_w[1], first, across), enc_two, e_gains
    )
    enc_inner = from_blocks(gathered(enc_inner))
    back = scattered(to_blocks(convt_part(enc_inner, enc_w[0], first, across)))
    flat, norm = own_block(enc_one[0]), own_block(enc_one[2])
    pre = back * swish_slope(norm, jax.nn.sigmoid(norm))
    enc_sums_one = pair_summed(jnp.stack([channel_sums(pre), channel_sums(pre * flat)]))
    gain = own_lanes(e_gains[0])
    total = group_means(enc_sums_one[0] * gain, group, members)
    lined = group_means(enc_sums_one[1] * gain, group, members)
    video_back = own_lanes(enc_one[1]) * (pre * gain - total - flat * lined)
    video_back = (own_block(enc_cot).astype(F32) + video_back).astype(BF16)
    recon = scattered(to_blocks(dec_branch)) + own_lanes(d_shifts[3])
    recon = (recon + own_block(decoded_in).astype(F32)).astype(BF16)

    def to_output(block):
        half, _, lane_count = block.shape
        pieces = block.reshape(half, spaces, across, lane_count).transpose(1, 0, 2, 3)
        swapped = lax.all_to_all(pieces, "space", 0, 0, tiled=True)
        slab = swapped.reshape(chips, 2, half, across, lane_count).transpose(1, 2, 3, 0, 4)
        slab = slab_of(slab.reshape(cubes, across, channels), extent)
        parted = slab.reshape(frames, height, width, sections, channels // sections)
        return lax.all_to_all(parted.transpose(3, 0, 1, 2, 4), "section", 0, 0, tiled=True)

    grads = [
        kernel_grad(enc_one[3], enc_inner),
        kernel_grad(enc_two[3], enc_cot),
        kernel_grad(dec_one[3], dec_inner),
        kernel_grad(dec_two[3], recon_cot),
    ]
    row_count = enc_convs.shape[1]
    grads = [
        lax.psum(lax.dynamic_slice_in_dim(g, offset, row_count, 0).astype(BF16), "section").astype(
            F32
        )
        for g in grads
    ]

    encoded = scattered(enc_branch.reshape(chips, 2, own_cubes, rows, channels))
    own = lambda v: lax.dynamic_slice_in_dim(v, space * own_cubes, own_cubes, 0).astype(F32)
    encoded = (encoded + e_shifts[3] + own(video)).astype(BF16)
    decoded_grad = scattered(grad_part.reshape(chips, 2, own_cubes, rows, channels)).astype(BF16)
    both = lax.all_gather(jnp.stack([encoded, decoded_grad]), "section", axis=0)
    both = both.transpose(1, 0, 3, 2, 4).reshape(2, clips * rows, own_cubes * channels)
    enc_rows, dec_rows = both[0], both[1]
    sign_all = lax.all_gather(sign_grad, "section", axis=0, tiled=True)
    inner_grad = jnp.dot(sign_all, down_cols, preferred_element_type=F32).astype(BF16)

    def outer(left, right):
        return lax.dot_general(left, right, (((0,), (0,)), ((), ())), preferred_element_type=F32)

    down_weight_grad = outer(enc_rows, inner_grad)
    up_weight_grad = outer(dec_rows, hidden)
    upsample_grad = jnp.sum(dec_rows.astype(F32), axis=0)
    parts = jnp.stack(
        [
            jnp.dot(enc_rows, down_weight, preferred_element_type=F32),
            jnp.dot(dec_rows, up_weight, preferred_element_type=F32),
        ]
    )
    shares = lax.psum_scatter(parts, "space", scatter_dimension=2, tiled=True)
    inner_low = (shares[0] + down_bias.astype(F32)).astype(BF16)
    hidden_grad = shares[1].astype(BF16)
    down_proj_grad = outer(inner_low, sign_all)
    up_proj_grad = outer(hidden_grad, signs)
    up_bias_grad = jnp.sum(hidden_grad.astype(F32), axis=0)
    inner_share = lax.dynamic_slice_in_dim(inner_grad, space * lanes, lanes, 1)
    down_bias_grad = jnp.sum(inner_share.astype(F32), axis=0)

    one = lambda v: channel_sums(v.astype(F32))[None] * first_space
    small_grads = jnp.concatenate(
        [
            spread_lanes(enc_sums_one[1:]),
            spread_lanes(enc_sums_two[1:]),
            spread_lanes(enc_sums_one[:1]),
            spread_lanes(enc_sums_two[:1]),
            one(enc_inner),
            one(enc_cot),
            dec_sums_one[1:],
            spread_lanes(dec_sums_two[1:]),
            dec_sums_one[:1],
            spread_lanes(dec_sums_two[:1]),
            one(dec_inner),
            one(recon_cot),
        ],
        axis=0,
    )
    small_grads = lax.psum(small_grads, ("section", "space"))
    small_grads = lax.dynamic_slice_in_dim(small_grads, space * lanes, lanes, 1)

    return (
        to_output(recon),
        to_output(video_back),
        jnp.stack(grads[:2]),
        small_grads[0:2],
        small_grads[2:6],
        down_weight_grad,
        down_bias_grad,
        down_proj_grad,
        up_proj_grad,
        up_bias_grad,
        up_weight_grad,
        upsample_grad,
        jnp.stack(grads[2:]),
        small_grads[6:8],
        small_grads[8:12],
    )


def solution(mesh):
    lead, second, third = P("space"), P(None, "space"), P(None, None, "space")
    field = P(None, None, "space", None, "section")
    short = mesh.shape["space"] == 8 and mesh.shape["section"] == 4
    return jax.shard_map(
        fast_body if short else general_body,
        mesh=mesh,
        in_specs=(
            third,
            third,
            third,
            second,
            second,
            second,
            lead,
            lead,
            lead,
            lead,
            lead,
            lead,
            lead,
            second,
            second,
            second,
        ),
        out_specs=(
            field,
            field,
            second,
            second,
            second,
            lead,
            lead,
            lead,
            lead,
            lead,
            lead,
            lead,
            second,
            second,
            second,
        ),
        check_vma=False,
    )
```

```python
from functools import partial

import jax
import jax.numpy as jnp
from jax import lax
from jax.experimental import pallas as pl
from jax.experimental.pallas import tpu as pltpu
from jax.sharding import PartitionSpec as P

GROUPS = 32
CUBE = 4
LANES = 128
BF16 = jnp.bfloat16
F32 = jnp.float32


def swish_slope(values, logistic):
    return logistic * (1.0 + values * (1.0 - logistic))


def chips_of():
    return lax.axis_size("space") // 2


def along_chips(value, step):
    chips = chips_of()
    route = [(i, (i // 2 + step) % chips * 2 + i % 2) for i in range(2 * chips)]
    return lax.ppermute(value, "space", route)


def to_twin(value):
    return lax.ppermute(value, "space", [(i, i ^ 1) for i in range(lax.axis_size("space"))])


def here():
    index = lax.axis_index("space")
    return index // 2, index % 2


def ring_is_short():
    return chips_of() <= 4


def picked(value, index, axis=0):
    return lax.dynamic_index_in_dim(value, index, axis, keepdims=False)


def gathered(value):
    chips = chips_of()
    if not ring_is_short():
        return lax.all_gather(value, "space", axis=0).reshape((chips, 2) + value.shape)
    z, core = here()
    pieces = [value] + [along_chips(value, step) for step in range(1, chips)]
    stack = jnp.zeros((chips,) + value.shape, value.dtype)
    for step, piece in enumerate(pieces):
        stack = lax.dynamic_update_index_in_dim(stack, piece, (z - step) % chips, 0)
    other = to_twin(stack)
    first = jnp.where(core == 0, stack, other)
    second = jnp.where(core == 0, other, stack)
    return jnp.stack([first, second], axis=1)


def scattered(parts):
    chips = chips_of()
    if not ring_is_short():
        flat = parts.reshape((2 * chips,) + parts.shape[2:])
        return lax.psum_scatter(flat, "space", scatter_dimension=0, tiled=False)
    z, core = here()
    mine = picked(parts, core, 1)
    mine = mine + to_twin(picked(parts, 1 - core, 1).astype(BF16)).astype(F32)
    total = picked(mine, z)
    for step in range(1, chips):
        sent = picked(mine, (z + step) % chips).astype(BF16)
        total = total + along_chips(sent, step).astype(F32)
    return total


def summed(value):
    if not ring_is_short():
        return lax.psum(value, "space")
    total = value
    for step in range(1, chips_of()):
        total = total + along_chips(value, step)
    return total + to_twin(total)


def pair_summed(value):
    return value + to_twin(value)


def to_blocks(field):
    chips = chips_of()
    cubes, rows, channels = field.shape
    split = field.reshape(2, cubes // 2, rows, chips, channels // chips)
    return split.transpose(3, 0, 1, 2, 4)


def from_blocks(blocks):
    chips, _, half, rows, width = blocks.shape
    return blocks.transpose(1, 2, 3, 0, 4).reshape(2 * half, rows, chips * width)


def own_block(field):
    z, core = here()
    cubes, rows, channels = field.shape
    width = channels // chips_of()
    return lax.dynamic_slice(field, (core * (cubes // 2), 0, z * width), (cubes // 2, rows, width))


def own_lanes(row):
    z, _ = here()
    width = row.shape[-1] // chips_of()
    return lax.dynamic_slice_in_dim(row, z * width, width, row.ndim - 1)


def cubes_of(slab):
    frames, height, across, channels = slab.shape
    split = slab.reshape(frames, height, across // CUBE, CUBE, channels)
    return split.transpose(0, 1, 3, 2, 4).reshape(-1, across // CUBE, channels)


def slab_of(cubes, extent):
    frames, height, across, channels = extent
    split = cubes.reshape(frames, height, CUBE, across // CUBE, channels)
    return split.transpose(0, 1, 3, 2, 4).reshape(extent)


def field_of(slabs):
    chips, _, cubes, across, channels = slabs.shape
    flat = slabs.reshape(2 * chips, cubes, across, channels)
    return flat.transpose(1, 0, 2, 3).reshape(cubes, 2 * chips * across, channels)


def group_means(sums, width, members):
    groups = sums.reshape(sums.shape[:-1] + (-1, width))
    wide = jnp.broadcast_to(jnp.sum(groups, axis=-1, keepdims=True), groups.shape)
    return wide.reshape(sums.shape) / members


def rimmed(field, across):
    cubes, rows, channels = field.shape
    view = field.reshape(CUBE, CUBE, CUBE, rows // across, across, channels)
    none = (0, 0)
    above = jnp.pad(view[:, -1:, :, :-1], (none, none, none, (1, 0), none, none))
    below = jnp.pad(view[:, :1, :, 1:], (none, none, none, (0, 1), none, none))
    view = jnp.concatenate([above, view, below], axis=1)
    left = jnp.pad(view[:, :, -1:, :, :-1], (none, none, none, none, (1, 0), none))
    right = jnp.pad(view[:, :, :1, :, 1:], (none, none, none, none, (0, 1), none))
    view = jnp.concatenate([left, view, right], axis=2)
    view = jnp.pad(view, ((1, 1), none, none, none, none, none))
    return view.reshape(CUBE + 2, CUBE + 2, CUBE + 2, rows, channels)


def rows_here(weights):
    count = weights.shape[-2]
    start = count * lax.axis_index("space")
    return start // LANES, start % LANES


def block_count(count):
    worst = max(count * s % LANES for s in range(lax.axis_size("space")))
    return -(-(worst + count) // LANES)


def aligned(weights):
    _, offset = rows_here(weights)
    total = block_count(weights.shape[-2]) * LANES
    wide = jnp.zeros(weights.shape[:-2] + (total, weights.shape[-1]), weights.dtype)
    return lax.dynamic_update_slice_in_dim(wide, weights, offset, wide.ndim - 2)


def patches(field, first, count, across):
    cubes, rows, channels = field.shape
    wide = rimmed(field, across)
    per_tap = channels // LANES
    pieces = []
    for j in range(count):
        block = first + j
        tap, lane = jnp.minimum(block // per_tap, 26), block % per_tap
        piece = lax.dynamic_slice(
            wide,
            (tap // 9, tap // 3 % 3, tap % 3, 0, lane * LANES),
            (CUBE, CUBE, CUBE, rows, LANES),
        )
        pieces.append(piece.reshape(cubes * rows, LANES))
    return jnp.concatenate(pieces, axis=1)


def conv_part(field, weights, first, across):
    patch = patches(field, first, weights.shape[0] // LANES, across)
    out = jnp.dot(patch, weights, preferred_element_type=F32)
    return out.reshape(field.shape[:2] + (-1,)), patch


def convt_part(field, weights, first, across):
    cubes, rows, channels = field.shape
    spread = lax.dot_general(
        field.reshape(-1, channels),
        weights,
        (((1,), (1,)), ((), ())),
        preferred_element_type=F32,
    )
    count = weights.shape[0] // LANES
    fold = jax.linear_transpose(
        lambda v: patches(v, first, count, across),
        jax.ShapeDtypeStruct((cubes, rows, channels), F32),
    )
    return fold(spread)[0]


def kernel_grad(patch, field):
    return lax.dot_general(
        patch,
        field.reshape(-1, field.shape[-1]),
        (((0,), (0,)), ((), ())),
        preferred_element_type=F32,
    )


def normed(values, sums, squares, width, members):
    average = group_means(sums, width, members)
    square = group_means(squares, width, members)
    spread = lax.rsqrt(square - average * average + 1e-06)
    return (values - average) * spread, spread


def channel_sums(values):
    return jnp.sum(values, axis=tuple(range(values.ndim - 1)))


VMEM_BYTES = 56 * 1024 * 1024


def kernels_fit(channels):
    return chips_of() * LANES == channels


def kernel_params():
    return pltpu.CompilerParams(vmem_limit_bytes=VMEM_BYTES)


def shifted(slabs, rows, valid):
    wide = pltpu.roll(slabs.astype(F32), rows % slabs.shape[1], 1)
    return jnp.where(valid, wide, 0.0)


def row_marks(shape, across):
    row = lax.broadcasted_iota(jnp.int32, shape, len(shape) - 2)
    return row, row % across


def fill_rim(field, rim, across):
    rows, channels = field.shape[1:]
    tiles = channels // LANES
    blank = jnp.zeros((CUBE + 2, CUBE + 2, rows, LANES), rim.dtype)
    for q in range(tiles):
        rim[q, 0] = blank
        rim[q, CUBE + 1] = blank

    def frame(f, carry):
        base = f * CUBE * CUBE
        row, column = row_marks((CUBE, rows, LANES), across)
        row6, column6 = row_marks((CUBE + 2, rows, LANES), across)
        for q in range(tiles):
            lanes = slice(q * LANES, (q + 1) * LANES)
            for h in range(CUBE):
                rim[q, f + 1, h + 1, 1 : CUBE + 1] = field[pl.ds(base + CUBE * h, CUBE), :, lanes]
            above = field[pl.ds(base + CUBE * (CUBE - 1), CUBE), :, lanes]
            rim[q, f + 1, 0, 1 : CUBE + 1] = shifted(above, across, row >= across).astype(rim.dtype)
            below = field[pl.ds(base, CUBE), :, lanes]
            rim[q, f + 1, CUBE + 1, 1 : CUBE + 1] = shifted(
                below, -across, row < rows - across
            ).astype(rim.dtype)
            left = rim[q, f + 1, :, CUBE]
            rim[q, f + 1, :, 0] = shifted(left, 1, column6 >= 1).astype(rim.dtype)
            right = rim[q, f + 1, :, 1]
            rim[q, f + 1, :, CUBE + 1] = shifted(right, -1, column6 < across - 1).astype(rim.dtype)
        return carry

    lax.fori_loop(0, CUBE, frame, 0)


def fold_rim(rim, across):
    tiles, rows = rim.shape[0], rim.shape[4]

    def frame(f, carry):
        row, _ = row_marks((CUBE, rows, LANES), across)
        _, column6 = row_marks((CUBE + 2, rows, LANES), across)
        for q in range(tiles):
            left = shifted(rim[q, f + 1, :, 0], -1, column6 < across - 1)
            rim[q, f + 1, :, CUBE] += left
            right = shifted(rim[q, f + 1, :, CUBE + 1], 1, column6 >= 1)
            rim[q, f + 1, :, 1] += right
            above = shifted(rim[q, f + 1, 0, 1 : CUBE + 1], -across, row < rows - across)
            rim[q, f + 1, CUBE, 1 : CUBE + 1] += above
            below = shifted(rim[q, f + 1, CUBE + 1, 1 : CUBE + 1], across, row >= across)
            rim[q, f + 1, 1, 1 : CUBE + 1] += below
        return carry

    lax.fori_loop(0, CUBE, frame, 0)


def tap_of(block, per_tap):
    tap = jnp.minimum(block // per_tap, 26)
    return block % per_tap, tap // 9, tap // 3 % 3, tap % 3


def fill_patch(rim, patch, first, count, start, size):
    rows = rim.shape[4]
    for j in range(count):
        q, f, h, w = tap_of(first + j, rim.shape[0])
        window = rim[
            q,
            pl.ds(f + start[0], size[0]),
            pl.ds(h + start[1], size[1]),
            pl.ds(w, CUBE),
        ]
        patch[:, j * LANES : (j + 1) * LANES] = window.reshape(
            size[0] * size[1] * CUBE * rows, LANES
        )


def add_taps(field, weights, rim, first):
    rows, channels = field.shape[1:]
    tiles = channels // LANES
    count = weights.shape[0] // LANES
    blank = jnp.zeros((CUBE + 2, CUBE + 2, rows, LANES), F32)

    def clear(f, carry):
        for q in range(tiles):
            rim[q, f] = blank
        return carry

    lax.fori_loop(0, CUBE + 2, clear, 0)
    spread_rows = CUBE * CUBE * rows

    for f in range(CUBE):
        source = field[pl.ds(f * CUBE * CUBE, CUBE * CUBE)].reshape(spread_rows, channels)
        for j in range(0, count, 2):
            wide = min(2, count - j)
            spread = lax.dot_general(
                source,
                weights[j * LANES : (j + wide) * LANES, :],
                (((1,), (1,)), ((), ())),
                preferred_element_type=F32,
            )
            for i in range(wide):
                q, tf, th, tw = tap_of(first + j + i, tiles)
                rim[q, f + tf, pl.ds(th, CUBE), pl.ds(tw, CUBE)] += spread[
                    :, i * LANES : (i + 1) * LANES
                ].reshape(CUBE, CUBE, rows, LANES)


def group_totals(row, width):
    lanes = row.shape[1]
    lane = lax.broadcasted_iota(jnp.int32, row.shape, 1)
    step = 1
    while step < width:
        before = pltpu.roll(row, step, 1)
        after = pltpu.roll(row, lanes - step, 1)
        row = row + jnp.where(lane // step % 2 == 1, before, after)
        step *= 2
    return row


def row_sum(values):
    return jnp.sum(values.reshape(-1, values.shape[-1]), axis=0, keepdims=True)


def logistic_of(values):
    return 0.5 + 0.5 * jnp.tanh(0.5 * values)


def both_halves(row):
    return row + pltpu.roll(row, LANES // 2, 1)


def pack_pair(near, far, core):
    axis = near.ndim - 1
    lane = lax.broadcasted_iota(jnp.int32, near.shape, axis)
    low = lane < LANES // 2
    first = jnp.where(low, near, pltpu.roll(far, LANES // 2, axis))
    second = jnp.where(low, pltpu.roll(near, LANES // 2, axis), far)
    lead = lane * 0 + core == 0
    return jnp.where(lead, first, second), jnp.where(lead, second, first)


def unpack_pair(own, other, core):
    axis = own.ndim - 1
    lane = lax.broadcasted_iota(jnp.int32, own.shape, axis)
    low = lane < LANES // 2
    lead = lane * 0 + core == 0
    first, second = jnp.where(lead, own, other), jnp.where(lead, other, own)
    near = jnp.where(low, first, pltpu.roll(second, LANES // 2, axis))
    far = jnp.where(low, pltpu.roll(first, LANES // 2, axis), second)
    return near, far


def own_row(table, index, z, core):
    lanes = pl.ds(pl.multiple_of(z * LANES, LANES), LANES)
    row = table[index : index + 1, lanes]
    mine, _ = pack_pair(row, row, core)
    return mine


def pack_own(field, out, z, core):
    lanes = pl.ds(pl.multiple_of(z * LANES, LANES), LANES)
    half = field.shape[0] // 2

    def some(i, carry):
        near = field[pl.ds(8 * i, 8), :, lanes].astype(F32)
        far = field[pl.ds(half + 8 * i, 8), :, lanes].astype(F32)
        out[pl.ds(8 * i, 8)] = pack_pair(near, far, core)[0].astype(out.dtype)
        return carry

    lax.fori_loop(0, half // 8, some, 0)


def unpack_stacks(own, other, field, z, core, relative):
    chips, half = own.shape[:2]
    for hop in range(chips):
        place = lax.rem(z + chips - hop, chips) if relative else hop
        lanes = pl.ds(pl.multiple_of(place * LANES, LANES), LANES)

        def some(i, carry, hop=hop, lanes=lanes):
            mine = own[hop, pl.ds(8 * i, 8)].astype(F32)
            twin = other[hop, pl.ds(8 * i, 8)].astype(F32)
            near, far = unpack_pair(mine, twin, core)
            field[pl.ds(8 * i, 8), :, lanes] = near.astype(field.dtype)
            field[pl.ds(half + 8 * i, 8), :, lanes] = far.astype(field.dtype)
            return carry

        lax.fori_loop(0, half // 8, some, 0)


class Rows:
    def __init__(self, weights, index, offset, wide, sem):
        count = weights.shape[1]
        slack = wide.shape[0] - count
        blank = jnp.zeros((slack, wide.shape[1]), wide.dtype)
        wide[0:slack, :] = blank
        wide[count : count + slack, :] = blank
        target = wide.at[pl.ds(pl.multiple_of(offset, 64), count), :]
        self.copy = pltpu.make_async_copy(weights.at[index], target, sem)
        self.copy.start()

    def ready(self):
        self.copy.wait()


def norm_in(field, act, table, gain, shift, stats, group, members):
    cubes, rows, channels = field.shape

    def add(i, carry):
        values = field[pl.ds(4 * i, 4)].astype(F32)
        folded = values.reshape(-1, 8, channels)
        return (carry[0] + jnp.sum(folded, 0), carry[1] + jnp.sum(folded * folded, 0))

    blank = jnp.zeros((8, channels), F32)
    totals, squares = lax.fori_loop(0, cubes // 4, add, (blank, blank))
    sums = jnp.concatenate(
        [jnp.sum(totals, 0, keepdims=True), jnp.sum(squares, 0, keepdims=True)], axis=0
    )
    means = group_totals(sums, group) / members
    average = means[0:1]
    spread = lax.rsqrt(means[1:2] - average * average + 1e-06)
    stats[0:1, :] = average
    stats[1:2, :] = spread
    scale, start = table[gain : gain + 1, :], table[shift : shift + 1, :]

    def apply(i, carry):
        values = field[pl.ds(4 * i, 4)].astype(F32)
        flat = (values - average[None]) * spread[None]
        normal = flat * scale[None] + start[None]
        act[pl.ds(4 * i, 4)] = (normal * logistic_of(normal)).astype(act.dtype)
        return carry

    lax.fori_loop(0, cubes // 4, apply, 0)


def multiply(patch, wide, product):
    size = product.shape[1]

    for f in range(product.shape[0]):
        rows = slice(f * size, (f + 1) * size)
        product[f] = jnp.dot(patch[rows, :], wide[...], preferred_element_type=F32)


def share_blocks(frame_block, keep, send, core):
    tiles, cubes = keep.shape[0], CUBE * CUBE

    def pair(i, carry):
        for q in range(tiles):
            mine, twin = pack_pair(frame_block(i, q), frame_block(i + CUBE // 2, q), core)
            keep[q, pl.ds(i * cubes, cubes)] = mine
            send[q, pl.ds(i * cubes, cubes)] = twin.astype(send.dtype)
        return carry

    lax.fori_loop(0, CUBE // 2, pair, 0)


def of_product(product, rows):
    def block(f, q):
        return product[f, :, q * LANES : (q + 1) * LANES].reshape(CUBE * CUBE, rows, LANES)

    return block


def of_rim(rim):
    rows = rim.shape[4]

    def block(f, q):
        inner = rim[q, f + 1, 1 : CUBE + 1, 1 : CUBE + 1]
        return inner.reshape(CUBE * CUBE, rows, LANES)

    return block


def first_conv_kernel(settings, where, *refs):
    stacked, across, group, members, gain, shift, index = settings
    if stacked:
        own, other, table, weights, keep, send, act, stats, mine, field = refs[:10]
        rim, patch, wide, product, sem = refs[10:]
    else:
        field, table, weights, keep, send, act, stats, mine = refs[:8]
        rim, patch, wide, product, sem = refs[8:]
    first, offset, z, core = where[0], where[1], where[2], where[3]
    coming = Rows(weights, index, offset, wide, sem)
    if stacked:
        chips, count = own.shape[:2]
        for hop in range(chips):
            place = lax.rem(z + chips - hop, chips) * 2
            field[pl.ds((place + core) * count, count)] = own[hop]
            field[pl.ds((place + 1 - core) * count, count)] = other[hop]
    rows = field.shape[1]
    norm_in(field, act, table, gain, shift, stats, group, members)
    fill_rim(act, rim, across)
    fill_patch(rim, patch, first, patch.shape[1] // LANES, (0, 0), (CUBE, CUBE))
    coming.ready()
    multiply(patch, wide, product)
    share_blocks(of_product(product, rows), keep, send, core)
    pack_own(field, mine, z, core)


def fill_grad(patch, source, offset, grad, out):
    count = patch.shape[1]
    for j in range(0, count, 2 * LANES):
        lanes = slice(j, min(j + 2 * LANES, count))
        grad[lanes, :] = lax.dot_general(
            patch[:, lanes], source, (((0,), (0,)), ((), ())), preferred_element_type=F32
        )
    start = pl.multiple_of(offset, 64)
    out[...] = grad[pl.ds(start, out.shape[0]), :].astype(out.dtype)


def second_conv_kernel(across, with_grad, index, where, *refs):
    if with_grad:
        own, other, weights, cotangent, keep, send, out, field = refs[:8]
        rim, patch, wide, product, sem, grad = refs[8:]
    else:
        own, other, weights, keep, send, field = refs[:6]
        rim, patch, wide, product, sem = refs[6:]
    first, offset, z, core = where[0], where[1], where[2], where[3]
    rows, channels = field.shape[1:]
    coming = Rows(weights, index, offset, wide, sem)
    unpack_stacks(own, other, field, z, core, False)
    fill_rim(field, rim, across)
    fill_patch(rim, patch, first, patch.shape[1] // LANES, (0, 0), (CUBE, CUBE))
    coming.ready()
    multiply(patch, wide, product)
    if with_grad:
        share_blocks(of_product(product, rows), keep, send, core)
        fill_grad(patch, cotangent[...].reshape(-1, channels), offset, grad, out)
    else:

        def frame(f, carry):
            low = product[f, : CUBE * CUBE * rows // 2]
            high = product[f, CUBE * CUBE * rows // 2 :]
            lead = lax.broadcasted_iota(jnp.int32, low.shape, 1) * 0 + core == 0
            keep[f] = jnp.where(lead, low, high).reshape(keep.shape[1:])
            send[f] = jnp.where(lead, high, low).reshape(send.shape[1:]).astype(send.dtype)
            return carry

        lax.fori_loop(0, CUBE, frame, 0)


def grad_only_kernel(across, where, field, cotangent, out, rim, patch, grad):
    channels = field.shape[2]
    fill_rim(field, rim, across)
    fill_patch(rim, patch, where[0], patch.shape[1] // LANES, (0, 0), (CUBE, CUBE))
    fill_grad(patch, cotangent[...].reshape(-1, channels), where[1], grad, out)


def twin_add_kernel(where, keep, received, own, *sends):
    chips, z = keep.shape[0], where[2]
    own[...] = keep[z] + received[z].astype(F32)
    for hop, send in enumerate(sends):
        target = lax.rem(z + 1 + hop, chips)
        send[...] = (keep[target] + received[target].astype(F32)).astype(send.dtype)


def twin_sums_kernel(count, where, *refs):
    out = refs[2 * count]
    lanes = out.shape[-1]
    for i in range(count):
        keep, received = refs[2 * i], refs[2 * i + 1]
        for target in range(out.shape[0]):
            total = (keep[target] + received[target].astype(F32)).astype(out.dtype)
            if total.shape[-1] == lanes:
                out[target, i] = total
            else:
                parts = total.shape[-1] // lanes
                for cube in range(total.shape[0]):
                    for q in range(parts):
                        out[target, i, cube * parts + q] = total[cube, :, q * lanes : (q + 1) * lanes]


def total_of(pieces):
    if len(pieces) == 1:
        return jnp.sum(pieces[0][...].astype(F32), axis=0)
    total = pieces[0][...]
    for piece in pieces[1:]:
        total = total + piece[...].astype(F32)
    return total


def mid_norm(middle, table, gain, shift, z, core, group, members):
    sums = jnp.concatenate([row_sum(middle), row_sum(middle * middle)], axis=0)
    means = group_totals(both_halves(sums), group) / members
    average = means[0:1]
    spread = lax.rsqrt(means[1:2] - average * average + 1e-06)
    flat = (middle - average[None]) * spread[None]
    scale = own_row(table, gain, z, core)
    normal = flat * scale[None] + own_row(table, shift, z, core)[None]
    return flat, spread, normal, logistic_of(normal), scale


def mid_back(raw, normed_state, group, members):
    flat, spread, normal, logistic, scale = normed_state
    pre = raw * (logistic * (1.0 + normal * (1.0 - logistic)))
    sums = jnp.concatenate([row_sum(pre), row_sum(pre * flat)], axis=0)
    sums = both_halves(sums)
    means = group_totals(sums * scale, group) / members
    back = spread[None] * (pre * scale[None] - means[0:1][None] - flat * means[1:2][None])
    return back, sums


def mid_ahead_kernel(settings, where, *refs):
    group, members, gain, shift, bias, chips = settings
    pieces, table, act, kept = refs[:chips], refs[chips], refs[chips + 1], refs[chips + 2]
    z, core = where[2], where[3]
    middle = total_of(pieces) + own_row(table, bias, z, core)[None]
    kept[...] = middle
    state = mid_norm(middle, table, gain, shift, z, core, group, members)
    act[...] = (state[2] * state[3]).astype(act.dtype)


def mid_back_kernel(settings, where, *refs):
    group, members, gain, shift, chips = settings
    pieces, kept, table, inner, sums = refs[:chips], *refs[chips:]
    z, core = where[2], where[3]
    state = mid_norm(kept[...], table, gain, shift, z, core, group, members)
    back, rows = mid_back(total_of(pieces), state, group, members)
    inner[...] = back.astype(inner.dtype)
    sums[...] = rows


def mid_both_kernel(settings, where, *refs):
    group, members, gain, shift, bias, chips = settings
    ahead, behind = refs[:chips], refs[chips : chips + 1]
    table, act, inner, sums = refs[chips + 1 :]
    z, core = where[2], where[3]
    middle = total_of(ahead) + own_row(table, bias, z, core)[None]
    state = mid_norm(middle, table, gain, shift, z, core, group, members)
    act[...] = (state[2] * state[3]).astype(act.dtype)
    back, rows = mid_back(total_of(behind), state, group, members)
    inner[...] = back.astype(inner.dtype)
    sums[...] = rows


def last_back_kernel(settings, where, *refs):
    group, members, gain, shift, chips = settings
    pieces = refs[:chips]
    inputs, cotangent, stats, table, out, sums = refs[chips:]
    z, core = where[2], where[3]
    average, spread = own_row(stats, 0, z, core), own_row(stats, 1, z, core)
    flat = (inputs[...].astype(F32) - average[None]) * spread[None]
    scale = own_row(table, gain, z, core)
    normal = flat * scale[None] + own_row(table, shift, z, core)[None]
    state = (flat, spread, normal, logistic_of(normal), scale)
    back, rows = mid_back(total_of(pieces), state, group, members)
    out[...] = (cotangent[...].astype(F32) + back).astype(out.dtype)
    sums[...] = rows


def share_rim(field, coming, where, wide, rim, across, keep, send):
    coming.ready()
    add_taps(field, wide, rim, where[0])
    fold_rim(rim, across)
    share_blocks(of_rim(rim), keep, send, where[3])


def back_kernel(across, index, where, field, weights, keep, send, wide, rim, sem):
    coming = Rows(weights, index, where[1], wide, sem)
    share_rim(field, coming, where, wide, rim, across, keep, send)


def back_stacked_kernel(across, index, where, own, other, weights, keep, send, field, *work):
    wide, rim, sem = work
    coming = Rows(weights, index, where[1], wide, sem)
    unpack_stacks(own, other, field, where[2], where[3], True)
    share_rim(field, coming, where, wide, rim, across, keep, send)


def back_signs_kernel(settings, where, tiny, maps, weights, keep, send, field, mine, *work):
    across, bits, index = settings
    wide, rim, sem = work
    coming = Rows(weights, index, where[1], wide, sem)
    rows, channels = field.shape[1:]
    signs = tiny[0:rows, 0:bits].astype(BF16)
    parts, slabs = maps.shape[:2]
    size = field.shape[0] // (slabs * parts)

    def slab(s, carry):
        for p in range(parts):
            wave = jnp.dot(signs, maps[p, s], preferred_element_type=F32)
            for j in range(size):
                cube = (s * parts + p) * size + j
                field[cube] = wave[:, j * channels : (j + 1) * channels].astype(BF16)
        return carry

    lax.fori_loop(0, slabs, slab, 0)
    share_rim(field, coming, where, wide, rim, across, keep, send)
    pack_own(field, mine, where[2], where[3])


def back_whole_kernel(settings, where, *refs):
    across, group, members, gain, shift, bits, index = settings
    own, other, weights, inputs, stats, table, cotangent, maps = refs[:8]
    keep, send, tiny, field = refs[8:12]
    wide, rim, sem, pre_ref, low, sums = refs[12:]
    z, core = where[2], where[3]
    tiles, rows, channels = rim.shape[0], rim.shape[4], field.shape[2]
    size = CUBE * CUBE
    coming = Rows(weights, index, where[1], wide, sem)
    unpack_stacks(own, other, field, z, core, True)
    coming.ready()
    add_taps(field, wide, rim, where[0])
    fold_rim(rim, across)
    sums[...] = jnp.zeros(sums.shape, F32)
    block = of_rim(rim)

    def at(f, q):
        lanes = slice(q * LANES, (q + 1) * LANES)
        values = inputs[pl.ds(f * size, size), :, lanes].astype(F32)
        flat = (values - stats[0:1, lanes][None]) * stats[1:2, lanes][None]
        return flat, lanes

    def ahead(f, carry):
        for q in range(tiles):
            flat, lanes = at(f, q)
            normal = flat * table[gain : gain + 1, lanes][None] + table[shift : shift + 1, lanes][None]
            logistic = logistic_of(normal)
            pre = block(f, q) * (logistic * (1.0 + normal * (1.0 - logistic)))
            pre_ref[q, pl.ds(f * size, size)] = pre
            sums[0:1, lanes] += row_sum(pre)
            sums[1:2, lanes] += row_sum(pre * flat)
        return carry

    lax.fori_loop(0, CUBE, ahead, 0)
    means = group_totals(sums[0:2, :] * table[gain : gain + 1, :], group) / members
    lead_slab = (2 * z + core == 0).astype(F32)
    half = size // 2

    def behind(f, carry):
        for q in range(tiles):
            flat, lanes = at(f, q)
            scaled = pre_ref[q, pl.ds(f * size, size)] * table[gain : gain + 1, lanes][None]
            back = stats[1:2, lanes][None] * (
                scaled - means[0:1, lanes][None] - flat * means[1:2, lanes][None]
            )
            back = back + cotangent[pl.ds(f * size, size), :, lanes].astype(F32) * lead_slab
            low[pl.ds(f * size, size), :, lanes] = back.astype(BF16)
            lead = lax.broadcasted_iota(jnp.int32, (half, rows, LANES), 2) * 0 + core == 0
            keep[f, :, :, lanes] = jnp.where(lead, back[:half], back[half:])
            send[f, :, :, lanes] = jnp.where(lead, back[half:], back[:half]).astype(BF16)
        return carry

    lax.fori_loop(0, CUBE, behind, 0)
    parts, slabs = maps.shape[:2]
    size = field.shape[0] // (slabs * parts)

    def slab(s, total):
        for p in range(parts):
            cube = (s * parts + p) * size
            wave = jnp.concatenate([low[cube + j] for j in range(size)], axis=1)
            total = total + lax.dot_general(
                wave, maps[p, s], (((1,), (1,)), ((), ())), preferred_element_type=F32
            )
        return total

    signs = lax.fori_loop(0, slabs, slab, jnp.zeros((rows, bits), F32))
    tiny[...] = jnp.zeros(tiny.shape, F32)
    tiny[0:rows, 0:bits] = signs
    for q in range(tiles):
        lanes = slice(q * LANES, (q + 1) * LANES)
        tiny[rows + q : rows + q + 1, :] = sums[0:1, lanes]
        tiny[rows + tiles + q : rows + tiles + q + 1, :] = sums[1:2, lanes]


def fast_body(
    video_clips,
    code_bits,
    recon_grad,
    enc_convs,
    enc_gains,
    enc_shifts,
    down_weight,
    down_bias,
    down_proj,
    up_proj,
    up_bias,
    up_weight,
    upsample_bias,
    dec_convs,
    dec_gains,
    dec_shifts,
):
    section = lax.axis_index("section")
    space = lax.axis_index("space")
    z, core = here()
    sections = lax.axis_size("section")
    spaces = lax.axis_size("space")
    chips = chips_of()
    clips, frames, height, width, channels = video_clips.shape
    across = width // CUBE
    bits = code_bits.shape[-1]
    rows = spaces * across
    cubes = CUBE**3
    own_cubes = cubes // spaces
    half = cubes // 2
    group = channels // GROUPS
    members = float(cubes * rows * group)
    lanes = down_bias.shape[0]
    row_count = enc_convs.shape[1]
    total_rows = block_count(row_count) * LANES
    tiles = channels // LANES
    first, offset = rows_here(enc_convs)
    where = jnp.stack([first, offset, z, core]).astype(jnp.int32)

    def arr(shape, dtype):
        return jax.ShapeDtypeStruct(shape, dtype)

    full = arr((cubes, rows, channels), BF16)
    piece_b, piece_f = arr((half, rows, LANES), BF16), arr((half, rows, LANES), F32)
    blocks_f, blocks_b = arr((tiles, half, rows, LANES), F32), arr((tiles, half, rows, LANES), BF16)
    cubes_f = arr((CUBE, half // CUBE, rows, channels), F32)
    cubes_b = arr((CUBE, half // CUBE, rows, channels), BF16)
    stats_f = arr((8, channels), F32)
    sums_f = arr((2, LANES), F32)
    grad_b = arr((row_count, channels), BF16)
    rim_shape = (tiles, CUBE + 2, CUBE + 2, CUBE + 2, rows, LANES)
    rim_b, rim_f = pltpu.VMEM(rim_shape, BF16), pltpu.VMEM(rim_shape, F32)
    patch = pltpu.VMEM((cubes * rows, total_rows), BF16)
    wide = pltpu.VMEM((total_rows, channels), BF16)
    grad_s = pltpu.VMEM((total_rows, channels), F32)
    product = pltpu.VMEM((CUBE, cubes * rows // CUBE, channels), F32)
    spec = pl.BlockSpec(memory_space=pltpu.VMEM)
    conv_flops = 2 * cubes * rows * channels * total_rows

    hbm = pl.BlockSpec(memory_space=pltpu.HBM)
    enc_convs, dec_convs = (
        pltpu.with_memory_space_constraint(w, pltpu.HBM) for w in (enc_convs, dec_convs)
    )
    arrival = pltpu.SemaphoreType.DMA

    def piece_spec(index):
        return pl.BlockSpec((chips, None, half, rows, LANES), lambda i: (0, index, 0, 0, 0))

    order = [where]

    def call(kernel, name, out_shape, scratch, specs, args, flops=conv_flops, mib=28, held=(), after=()):
        place, anywhere = pl.BlockSpec(memory_space=pltpu.SMEM), pl.BlockSpec(memory_space=pl.ANY)
        inner, outer = len(args), len(out_shape)

        def ordered(*refs):
            skip = inner + len(held) + len(after)
            given, handed = refs[0], refs[1 + skip]
            for i in range(given.shape[0]):
                handed[i] = given[i]
            outs = 2 + skip
            scratch_refs = refs[outs + outer + len(held) :]
            kernel(given, *refs[1 : 1 + inner], *refs[outs : outs + outer], *scratch_refs)

        made = pl.pallas_call(
            ordered,
            grid=(1,),
            out_shape=(arr(where.shape, jnp.int32),)
            + tuple(out_shape)
            + tuple(arr(h.shape, h.dtype) for h in held),
            in_specs=[place] + specs + [anywhere] * (len(held) + len(after)),
            out_specs=(place,) + tuple(spec for _ in out_shape) + (anywhere,) * len(held),
            scratch_shapes=scratch,
            input_output_aliases={1 + inner + i: 1 + outer + i for i in range(len(held))},
            compiler_params=pltpu.CompilerParams(vmem_limit_bytes=mib << 20),
            cost_estimate=pl.CostEstimate(flops=flops, bytes_accessed=6 << 20, transcendentals=0),
            name=name,
        )(order[0], *args, *held, *after)
        order[0] = made[0]
        return made[1:]

    def z_hops(value):
        return [along_chips(value, step) for step in range(1, chips)]

    def gather_stacks(piece, hops=None):
        stack = jnp.stack([piece] + (hops or z_hops(piece)))
        return stack, to_twin(stack)

    def scatter_pieces(shares, held=(), after=()):
        keep, received = shares
        shape = keep.shape[1:]
        outs = (arr(shape, F32),) + tuple(arr(shape, BF16) for _ in range(chips - 1))
        made = call(
            twin_add_kernel, "twin_add", outs, [], [spec, spec], shares, 1, 8, held, after
        )
        hops = [along_chips(s, step) for step, s in zip(range(1, chips), made[1:chips])]
        return [made[0]] + hops, made[chips:]

    line = [[2 * chip + c for chip in range(chips)] for c in range(2)]

    def swap_chips(value):
        return lax.all_to_all(value, "space", 0, 0, axis_index_groups=line, tiled=True)

    def scatter_swap(shares, held=(), after=()):
        flat = [v for pair in shares for v in pair]
        out = arr((chips, len(shares), half, rows, LANES), BF16)
        made = call(
            partial(twin_sums_kernel, len(shares)),
            "twin_sums",
            (out,),
            [],
            [spec] * len(flat),
            flat,
            1,
            16,
            held,
            after,
        )
        return swap_chips(made[0]), made[1:]

    def tiny_gather(value):
        chain = z_hops(value)[::-1] + [value]
        stack = jnp.stack(chain)
        twin = to_twin(stack)
        pair = jnp.where(core == 0, jnp.stack([stack, twin], 1), jnp.stack([twin, stack], 1))
        return lax.dynamic_slice_in_dim(jnp.concatenate([pair, pair]), chips - 1 - z, chips, 0)

    def to_output(pieces):
        count, split = pieces.shape[0], LANES // 2
        parts = pieces.reshape(count, half, spaces, across, LANES).transpose(2, 0, 1, 3, 4)
        got = lax.all_to_all(parts, "space", 0, 0, tiled=True)
        got = got.reshape(spaces, count, half, across, 2, split).transpose(1, 4, 2, 3, 0, 5)
        slab = got.reshape(count, cubes, across, channels)
        slab = jax.vmap(lambda v: slab_of(v, (frames, height, width, channels)))(slab)
        slab = slab.reshape(count, frames, height, width, sections, channels // sections)
        slab = lax.all_to_all(slab.transpose(4, 0, 1, 2, 3, 5), "section", 0, 0, tiled=True)
        return tuple(slab[:, i] for i in range(count))

    def own_channels(row):
        return lax.dynamic_slice_in_dim(row, space * lanes, lanes, row.ndim - 1)

    code = code_bits.reshape(-1).astype(BF16)
    code = jnp.pad(code, (0, -code.shape[0] % lanes)).reshape(-1, lanes)
    small = jnp.concatenate(
        [enc_gains, dec_gains, enc_shifts, dec_shifts, up_bias[None], down_bias[None]]
        + [up_proj.T, down_proj.T, code],
        axis=0,
    )
    recon_slab = cubes_of(picked(recon_grad, section))
    (small,) = call(lambda where: None, "first", (), [], [], (), 1, 8, (small,), (recon_slab,))
    small = tiny_gather(small).reshape(spaces, small.shape[0], lanes)
    heads = 14 + 2 * bits
    heading = small[:, :heads].transpose(1, 0, 2).reshape(heads, channels)
    table = jnp.pad(heading[:14].astype(F32), ((0, 2), (0, 0)))
    up_cols, down_cols = heading[14 : 14 + bits], heading[14 + bits :]
    count = clips * across * bits
    code_all = small[:, heads:].reshape(spaces, -1)[:, :count].reshape(spaces, clips, across, bits)
    signs = (2 * code_all - 1).transpose(1, 0, 2, 3).reshape(clips * rows, bits)

    def cube_map(columns, weight):
        size = weight.shape[0] // sections
        part = lax.dynamic_slice_in_dim(weight, section * size, size, 0)
        made = lax.dot_general(
            columns, part, (((1,), (1,)), ((), ())), preferred_element_type=F32
        )
        return made.astype(BF16).reshape(bits, -1, channels)

    def field_from(every):
        return every.transpose(1, 0, 2, 3).reshape(cubes, rows, channels)

    recon_cot = field_from(lax.all_gather(recon_slab, "space", axis=0))
    hidden = (jnp.dot(signs, up_cols, preferred_element_type=F32) + table[12]).astype(BF16)
    hidden_own = lax.dynamic_slice_in_dim(hidden, section * rows, rows, 0)
    grown = lax.dot_general(
        hidden_own, up_weight, (((1,), (1,)), ((), ())), preferred_element_type=F32
    )
    grown = (grown + upsample_bias.astype(F32)).astype(BF16)
    grown = grown.reshape(rows, own_cubes, channels).transpose(1, 0, 2)
    grown_own, grown_twin = gather_stacks(grown)

    def map_spec(index):
        shape = (sections, spaces, None, bits, own_cubes * channels // sections)
        return pl.BlockSpec(shape, lambda i: (0, 0, index, 0, 0))

    def with_twin(keep, send, *rest):
        return ((keep, to_twin(send)),) + rest

    slabs = cubes_of(picked(video_clips, section))
    slabs, up_cols, down_cols = call(
        lambda where: None,
        "begin",
        (),
        [],
        [],
        (),
        1,
        8,
        (slabs, up_cols, down_cols),
        (grown_own, recon_cot),
    )
    slabs = jnp.concatenate([slabs, cube_map(up_cols, up_weight), cube_map(down_cols, down_weight)])
    slabs = lax.all_gather(slabs, "space", axis=0)
    video = field_from(slabs[:, :cubes])
    maps = slabs[:, cubes:].reshape(spaces, 2, bits, -1)
    (shares,) = with_twin(
        *call(
            partial(back_kernel, across, 1),
            "dec_back_two",
            (blocks_f, blocks_b),
            [wide, rim_f, arrival],
            [spec, hbm],
            (recon_cot, dec_convs),
        )
    )
    behind, _ = scatter_swap([shares])
    shares, dec_act, dec_stats, dec_mine, decoded_in = with_twin(
        *call(
            partial(first_conv_kernel, (True, across, group, members, 2, 8, 0)),
            "dec_conv_one",
            (blocks_f, blocks_b, full, stats_f, piece_b, full),
            [rim_b, patch, wide, product, arrival],
            [spec, spec, spec, hbm],
            (grown_own, grown_twin, table, dec_convs),
        )
    )
    ahead, _ = scatter_pieces(shares)
    enc_keep, enc_send, enc_act, enc_stats, enc_mine = call(
        partial(first_conv_kernel, (False, across, group, members, 0, 4, 0)),
        "enc_conv_one",
        (blocks_f, blocks_b, full, stats_f, piece_b),
        [rim_b, patch, wide, product, arrival],
        [spec, spec, hbm],
        (video, table, enc_convs),
    )
    dec_act_two, dec_inner, dec_sums_two, enc_send, maps = call(
        partial(mid_both_kernel, (group, members, 3, 9, 10, chips)),
        "dec_mid",
        (piece_b, piece_b, sums_f),
        [],
        [spec] * (chips + 2),
        (*ahead, behind[:, 0], table),
        1,
        8,
        (enc_send, maps),
    )
    maps = lax.all_gather(maps, "section", axis=0)
    inner_hops = z_hops(dec_inner)
    enc_pieces, _ = scatter_swap([(enc_keep, to_twin(enc_send))])
    enc_act_two, enc_kept, dec_inner = call(
        partial(mid_ahead_kernel, (group, members, 1, 5, 6, 1)),
        "enc_mid",
        (piece_b, piece_f),
        [],
        [spec] * 2,
        (enc_pieces[:, 0], table),
        1,
        8,
        (dec_inner,),
    )
    inner_own, inner_twin = gather_stacks(dec_inner, inner_hops)
    acts = jnp.broadcast_to(jnp.stack([dec_act_two, enc_act_two])[None], (chips, 2) + piece_b.shape)
    acts = swap_chips(acts)
    tiny_f = arr((rows + 2 * tiles, LANES), F32)
    grad_shares, tiny, dec_inner_full = with_twin(
        *call(
            partial(back_whole_kernel, (across, group, members, 2, 8, bits, 0)),
            "dec_back_one",
            (cubes_f, cubes_b, tiny_f, full),
            [
                wide,
                rim_f,
                arrival,
                pltpu.VMEM((tiles, cubes, rows, LANES), F32),
                pltpu.VMEM((cubes, rows, channels), BF16),
                pltpu.VMEM((8, channels), F32),
            ],
            [spec, spec, hbm, spec, spec, spec, spec, map_spec(0)],
            (inner_own, inner_twin, dec_convs, decoded_in, dec_stats, table, recon_cot, maps),
            mib=34,
        )
    )
    for hop in z_hops(tiny):
        tiny = tiny + hop
    tiny = tiny + to_twin(tiny)
    sign_grad = tiny[:rows, :bits].astype(BF16)

    def kernel_grad_of(act, cot, name, held=(), after=()):
        return call(
            partial(grad_only_kernel, across),
            name,
            (grad_b,),
            [rim_b, patch, grad_s],
            [spec, spec],
            (act, cot),
            held=held,
            after=after,
        )

    (dec_grad_one,) = kernel_grad_of(dec_act, dec_inner_full, "dec_grad_one")

    def parts_of(grad):
        parts = grad.reshape(sections, row_count // sections, channels)
        parts = lax.all_to_all(parts, "section", 0, 0, tiled=True)
        return jnp.sum(parts.astype(F32), axis=0).astype(BF16)

    shares, enc_cot, cot_mine, acts, dec_grad_one = with_twin(
        *call(
            partial(back_signs_kernel, (across, bits, 1)),
            "enc_back_two",
            (blocks_f, blocks_b, full, piece_b),
            [wide, rim_f, arrival],
            [spec, map_spec(1), hbm],
            (tiny, maps, enc_convs),
            held=(acts, dec_grad_one),
        )
    )
    acts_twin = to_twin(acts)
    enc_pieces, (dec_grad_one,) = scatter_pieces(shares, (dec_grad_one,))
    dec_one = parts_of(dec_grad_one)
    recon_keep, recon_send, dec_grad_two, _ = call(
        partial(second_conv_kernel, across, True, 1),
        "dec_conv_two",
        (blocks_f, blocks_b, grad_b, full),
        [rim_b, patch, wide, product, arrival, grad_s],
        [piece_spec(0), piece_spec(0), hbm, spec],
        (acts, acts_twin, dec_convs, recon_cot),
        mib=36,
    )
    enc_inner, enc_sums_two, recon_send, dec_grad_two = call(
        partial(mid_back_kernel, (group, members, 1, 5, chips)),
        "enc_mid_back",
        (piece_b, sums_f),
        [],
        [spec] * (chips + 2),
        (*enc_pieces, enc_kept, table),
        1,
        8,
        (recon_send, dec_grad_two),
    )
    einner_hops = z_hops(enc_inner)

    recon_shares = (recon_keep, to_twin(recon_send))
    encoded_keep, encoded_send, enc_act_two_full, enc_inner, dec_grad_two, dec_one = call(
        partial(second_conv_kernel, across, False, 1),
        "enc_conv_two",
        (cubes_f, cubes_b, full),
        [rim_b, patch, wide, product, arrival],
        [piece_spec(1), piece_spec(1), hbm],
        (acts, acts_twin, enc_convs),
        held=(enc_inner, dec_grad_two, dec_one),
    )
    dec_one = lax.all_gather(dec_one, "section", axis=0, tiled=True)
    dec_two = parts_of(dec_grad_two)
    einner_own, einner_twin = gather_stacks(enc_inner, einner_hops)
    encoded_shares = (encoded_keep, to_twin(encoded_send))
    shares, enc_inner_full = with_twin(
        *call(
            partial(back_stacked_kernel, across, 0),
            "enc_back_one",
            (blocks_f, blocks_b, full),
            [wide, rim_f, arrival],
            [spec, spec, hbm],
            (einner_own, einner_twin, enc_convs),
        )
    )
    enc_pieces, _ = scatter_pieces(shares)
    (enc_grad_two,) = kernel_grad_of(enc_act_two_full, enc_cot, "enc_grad_two")
    (enc_grad_one,) = kernel_grad_of(enc_act, enc_inner_full, "enc_grad_one")
    video_back, enc_sums_one, enc_grad_one, enc_grad_two = call(
        partial(last_back_kernel, (group, members, 0, 4, chips)),
        "enc_last",
        (piece_b, sums_f),
        [],
        [spec] * (chips + 4),
        (*enc_pieces, enc_mine, cot_mine, enc_stats, table),
        1,
        8,
        (enc_grad_one, enc_grad_two),
        (dec_two,),
    )
    dec_two = lax.all_gather(dec_two, "section", axis=0, tiled=True)
    swapped, _ = scatter_swap([grad_shares, recon_shares, encoded_shares])
    totals = jnp.sum(swapped.astype(F32), axis=0)
    own_bias = own_channels(table[11])
    recon = totals[1] + jnp.concatenate([own_bias, own_bias]) + dec_mine.astype(F32)
    pieces = jnp.stack([recon.astype(BF16), video_back])

    def as_cubes(part):
        split = part.reshape(own_cubes, tiles, rows, LANES).transpose(0, 2, 1, 3)
        return split.reshape(own_cubes, rows, channels)

    swaps = range(1, sections)

    def section_swap(value, step):
        return lax.ppermute(value, "section", [(i, i ^ step) for i in range(sections)])

    def quarter_sum(grad):
        size = row_count // sections

        def part(step):
            return lax.dynamic_slice_in_dim(grad, (section ^ step) * size, size, 0)

        got = [section_swap(part(step), step) for step in swaps]
        total = part(0).astype(F32)
        for value in got:
            total = total + value.astype(F32)
        return total.astype(BF16)

    def by_section(value):
        every = jnp.stack([value] + [section_swap(value, step) for step in swaps])
        every = every.reshape((sections // 2, 2) + value.shape)
        every = jnp.where(section % 2 == 1, every[:, ::-1], every)
        every = jnp.where(section // 2 == 1, every[::-1], every)
        return every.reshape((sections,) + value.shape)

    enc_one_sum = quarter_sum(enc_grad_one)
    enc_two = lax.all_gather(parts_of(enc_grad_two), "section", axis=0, tiled=True)

    own = lax.dynamic_slice_in_dim(video, space * own_cubes, own_cubes, 0).astype(F32)
    encoded = as_cubes(totals[2]) + table[7] + own
    decoded_grad = as_cubes(totals[0])
    sign_wide = jnp.pad(sign_grad, ((0, 0), (0, channels - bits)))[None]
    encoded, decoded_grad = encoded.astype(BF16), decoded_grad.astype(BF16)
    both = jnp.concatenate([encoded, decoded_grad, sign_wide])

    signs_own = lax.dynamic_slice_in_dim(signs, section * rows, rows, 0)
    signs_own = jnp.concatenate([signs_own, jnp.ones((rows, 1), BF16)], axis=1)

    def through(bit_rows, field, weight):
        wave = jnp.einsum("rk,orc->koc", bit_rows, field, preferred_element_type=F32)
        wave = wave.astype(BF16).reshape(wave.shape[0], -1)
        return jnp.dot(wave, weight, preferred_element_type=F32)

    projected = jnp.concatenate(
        [through(sign_grad, encoded, down_weight), through(signs_own, decoded_grad, up_weight)]
    )
    both, projected, pieces, enc_one_sum = call(
        lambda where: None,
        "latent",
        (),
        [],
        [],
        (),
        1,
        8,
        (both, projected, pieces, enc_one_sum),
    )
    enc_one = by_section(enc_one_sum).reshape(row_count, channels)
    both = by_section(both)
    recon_out, video_out = to_output(pieces)
    for hop in z_hops(projected):
        projected = projected + hop
    projected = own_channels(projected + to_twin(projected))
    sign_total = jnp.sum(sign_grad.astype(F32), axis=0)
    biased = sign_total[:, None] * down_bias.astype(F32)[None]
    projected = jnp.concatenate([projected[:bits] + biased, projected[bits:]])
    sign_all = both[:, 2 * own_cubes, :, :bits].reshape(clips * rows, bits)

    def latent_rows(part):
        return part.transpose(0, 2, 1, 3).reshape(clips * rows, own_cubes * channels)

    enc_rows = latent_rows(both[:, :own_cubes])
    dec_rows = latent_rows(both[:, own_cubes : 2 * own_cubes])
    inner_grad = jnp.dot(sign_all, down_cols, preferred_element_type=F32).astype(BF16)

    def outer(left, right):
        return lax.dot_general(left, right, (((0,), (0,)), ((), ())), preferred_element_type=F32)

    down_weight_grad = outer(enc_rows, inner_grad)
    up_weight_grad = outer(dec_rows, hidden)
    upsample_grad = jnp.sum(dec_rows.astype(F32), axis=0)
    down_bias_grad = jnp.sum(own_channels(inner_grad).astype(F32), axis=0)

    def own_sum(field):
        return own_channels(channel_sums(field.astype(F32)))[None]

    dec_sums_one = own_channels(tiny[rows:].reshape(2, channels))
    enc_sums_one, enc_sums_two, dec_sums_two = (
        s[:, :lanes] for s in (enc_sums_one, enc_sums_two, dec_sums_two)
    )
    small_grads = jnp.concatenate(
        [
            enc_sums_one[1:],
            enc_sums_two[1:],
            enc_sums_one[:1],
            enc_sums_two[:1],
            own_sum(enc_inner_full),
            own_sum(enc_cot),
            dec_sums_one[1:],
            dec_sums_two[1:],
            dec_sums_one[:1],
            dec_sums_two[:1],
            own_sum(dec_inner_full),
            own_sum(recon_cot),
            projected,
        ]
    )
    step = 1
    while step < sections:
        route = [(i, i ^ step) for i in range(sections)]
        small_grads = small_grads + lax.ppermute(small_grads, "section", route)
        step *= 2

    return (
        recon_out,
        video_out,
        jnp.stack([enc_one, enc_two]).astype(F32),
        small_grads[0:2],
        small_grads[2:6],
        down_weight_grad,
        down_bias_grad,
        small_grads[12 : 12 + bits].T,
        small_grads[12 + bits : 12 + 2 * bits].T,
        small_grads[12 + 2 * bits],
        up_weight_grad,
        upsample_grad,
        jnp.stack([dec_one, dec_two]).astype(F32),
        small_grads[6:8],
        small_grads[8:12],
    )


def general_body(
    video_clips,
    code_bits,
    recon_grad,
    enc_convs,
    enc_gains,
    enc_shifts,
    down_weight,
    down_bias,
    down_proj,
    up_proj,
    up_bias,
    up_weight,
    upsample_bias,
    dec_convs,
    dec_gains,
    dec_shifts,
):
    section = lax.axis_index("section")
    space = lax.axis_index("space")
    sections = lax.axis_size("section")
    spaces = lax.axis_size("space")
    chips = chips_of()
    clips, frames, height, width, channels = video_clips.shape
    extent = (frames, height, width, channels)
    across = width // CUBE
    bits = code_bits.shape[-1]
    rows = spaces * across
    cubes = CUBE**3
    own_cubes = cubes // spaces
    members = float(cubes * rows * (channels // GROUPS))
    group = channels // GROUPS
    first_space = (space == 0).astype(F32)

    lanes = down_bias.shape[0]
    code = code_bits.reshape(-1).astype(BF16)
    code = jnp.pad(code, (0, -code.shape[0] % lanes)).reshape(-1, lanes)
    small = jnp.concatenate(
        [
            enc_gains,
            dec_gains,
            enc_shifts,
            dec_shifts,
            up_bias[None],
            down_bias[None],
            up_proj.T,
            down_proj.T,
            code,
        ],
        axis=0,
    )
    small = gathered(small).reshape(spaces, small.shape[0], lanes)
    heads = 14 + 2 * bits
    table = small[:, :heads].transpose(1, 0, 2).reshape(heads, channels)
    wide_table = table.astype(F32)
    e_gains, d_gains = wide_table[0:2], wide_table[2:4]
    e_shifts, d_shifts = wide_table[4:8], wide_table[8:12]
    up_row, down_row = wide_table[12], wide_table[13]
    up_cols, down_cols = table[14 : 14 + bits], table[14 + bits :]
    count = clips * across * bits
    code_all = small[:, heads:].reshape(spaces, -1)[:, :count].reshape(spaces, clips, across, bits)
    signs = (2 * code_all - 1).transpose(1, 0, 2, 3).reshape(clips * rows, bits)

    slabs = jnp.stack(
        [cubes_of(picked(video_clips, section)), cubes_of(picked(recon_grad, section))]
    )
    hidden = (jnp.dot(signs, up_cols, preferred_element_type=F32) + up_row).astype(BF16)
    hidden_own = lax.dynamic_slice_in_dim(hidden, section * rows, rows, 0)
    grown = lax.dot_general(
        hidden_own, up_weight, (((1,), (1,)), ((), ())), preferred_element_type=F32
    )
    grown = (grown + upsample_bias.astype(F32)).astype(BF16)
    grown = grown.reshape(rows, own_cubes, channels).transpose(1, 0, 2)
    decoded_in = gathered(grown).reshape(cubes, rows, channels)
    both = gathered(slabs)
    video = field_of(both[:, :, 0])
    recon_cot = field_of(both[:, :, 1])

    maps = jnp.stack(
        [
            lax.dot_general(
                up_cols, up_weight, (((1,), (1,)), ((), ())), preferred_element_type=F32
            ),
            lax.dot_general(
                down_cols, down_weight, (((1,), (1,)), ((), ())), preferred_element_type=F32
            ),
        ]
    ).astype(BF16)
    maps = gathered(maps).reshape(spaces, 2, bits, own_cubes, channels)
    up_map, down_map = maps[:, 0], maps[:, 1]

    first, offset = rows_here(enc_convs)
    enc_w, dec_w = aligned(enc_convs), aligned(dec_convs)
    half_members = members

    def ahead(inputs, weights, gains, shifts):
        wide = inputs.astype(F32)
        flat_one, spread_one = normed(
            wide, channel_sums(wide), channel_sums(wide * wide), group, members
        )
        norm_one = flat_one * gains[0] + shifts[0]
        logistic = jax.nn.sigmoid(norm_one)
        act_one = (norm_one * logistic).astype(BF16)
        part, patch_one = conv_part(act_one, weights[0], first, across)
        middle = scattered(to_blocks(part)) + own_lanes(shifts[2])
        sums = pair_summed(jnp.stack([channel_sums(middle), channel_sums(middle * middle)]))
        flat_two, spread_two = normed(middle, sums[0], sums[1], group, half_members)
        norm_two = flat_two * own_lanes(gains[1]) + own_lanes(shifts[1])
        act_two = (norm_two * jax.nn.sigmoid(norm_two)).astype(BF16)
        act_two = from_blocks(gathered(act_two))
        branch, patch_two = conv_part(act_two, weights[1], first, across)
        return (
            branch,
            (flat_one, spread_one, norm_one, patch_one),
            (flat_two, spread_two, norm_two, patch_two),
        )

    def grads_two(spread_back, state, gains):
        flat, spread, norm, _ = state
        raw = scattered(to_blocks(spread_back))
        pre = raw * swish_slope(norm, jax.nn.sigmoid(norm))
        sums = pair_summed(jnp.stack([channel_sums(pre), channel_sums(pre * flat)]))
        gain = own_lanes(gains[1])
        total = group_means(sums[0] * gain, group, members)
        lined = group_means(sums[1] * gain, group, members)
        inner = (spread * (pre * gain - total - flat * lined)).astype(BF16)
        return inner, sums

    z, core = here()

    def spread_lanes(block_row):
        full = jnp.zeros(block_row.shape[:-1] + (channels,), F32)
        placed = lax.dynamic_update_slice_in_dim(
            full, block_row, z * block_row.shape[-1], full.ndim - 1
        )
        return jnp.where(core == 0, placed, 0.0)

    dec_branch, dec_one, dec_two = ahead(decoded_in, dec_w, d_gains, d_shifts)
    dec_inner, dec_sums_two = grads_two(
        convt_part(recon_cot, dec_w[1], first, across), dec_two, d_gains
    )
    dec_inner = from_blocks(gathered(dec_inner))
    back = convt_part(dec_inner, dec_w[0], first, across)
    flat_one, spread_one, norm_one, _ = dec_one
    pre = back * swish_slope(norm_one, jax.nn.sigmoid(norm_one))
    dec_sums_one = jnp.stack([channel_sums(pre), channel_sums(pre * flat_one)])
    total = group_means(dec_sums_one[0] * d_gains[0], group, members)
    lined = group_means(dec_sums_one[1] * d_gains[0], group, members)
    grad_part = spread_one * (pre * d_gains[0] - total - flat_one * lined)
    grad_part = grad_part + recon_cot.astype(F32) * first_space
    sign_part = jnp.einsum(
        "sorc,skoc->rk",
        grad_part.reshape(spaces, own_cubes, rows, channels).astype(BF16),
        up_map,
        preferred_element_type=F32,
    )
    sign_grad = summed(sign_part).astype(BF16)
    enc_cot = jnp.einsum("rk,skoc->sorc", sign_grad, down_map, preferred_element_type=F32)
    enc_cot = enc_cot.astype(BF16).reshape(cubes, rows, channels)

    enc_branch, enc_one, enc_two = ahead(video, enc_w, e_gains, e_shifts)
    enc_inner, enc_sums_two = grads_two(
        convt_part(enc_cot, enc_w[1], first, across), enc_two, e_gains
    )
    enc_inner = from_blocks(gathered(enc_inner))
    back = scattered(to_blocks(convt_part(enc_inner, enc_w[0], first, across)))
    flat, norm = own_block(enc_one[0]), own_block(enc_one[2])
    pre = back * swish_slope(norm, jax.nn.sigmoid(norm))
    enc_sums_one = pair_summed(jnp.stack([channel_sums(pre), channel_sums(pre * flat)]))
    gain = own_lanes(e_gains[0])
    total = group_means(enc_sums_one[0] * gain, group, members)
    lined = group_means(enc_sums_one[1] * gain, group, members)
    video_back = own_lanes(enc_one[1]) * (pre * gain - total - flat * lined)
    video_back = (own_block(enc_cot).astype(F32) + video_back).astype(BF16)
    recon = scattered(to_blocks(dec_branch)) + own_lanes(d_shifts[3])
    recon = (recon + own_block(decoded_in).astype(F32)).astype(BF16)

    def to_output(block):
        half, _, lane_count = block.shape
        pieces = block.reshape(half, spaces, across, lane_count).transpose(1, 0, 2, 3)
        swapped = lax.all_to_all(pieces, "space", 0, 0, tiled=True)
        slab = swapped.reshape(chips, 2, half, across, lane_count).transpose(1, 2, 3, 0, 4)
        slab = slab_of(slab.reshape(cubes, across, channels), extent)
        parted = slab.reshape(frames, height, width, sections, channels // sections)
        return lax.all_to_all(parted.transpose(3, 0, 1, 2, 4), "section", 0, 0, tiled=True)

    grads = [
        kernel_grad(enc_one[3], enc_inner),
        kernel_grad(enc_two[3], enc_cot),
        kernel_grad(dec_one[3], dec_inner),
        kernel_grad(dec_two[3], recon_cot),
    ]
    row_count = enc_convs.shape[1]
    grads = [
        lax.psum(lax.dynamic_slice_in_dim(g, offset, row_count, 0).astype(BF16), "section").astype(
            F32
        )
        for g in grads
    ]

    encoded = scattered(enc_branch.reshape(chips, 2, own_cubes, rows, channels))
    own = lambda v: lax.dynamic_slice_in_dim(v, space * own_cubes, own_cubes, 0).astype(F32)
    encoded = (encoded + e_shifts[3] + own(video)).astype(BF16)
    decoded_grad = scattered(grad_part.reshape(chips, 2, own_cubes, rows, channels)).astype(BF16)
    both = lax.all_gather(jnp.stack([encoded, decoded_grad]), "section", axis=0)
    both = both.transpose(1, 0, 3, 2, 4).reshape(2, clips * rows, own_cubes * channels)
    enc_rows, dec_rows = both[0], both[1]
    sign_all = lax.all_gather(sign_grad, "section", axis=0, tiled=True)
    inner_grad = jnp.dot(sign_all, down_cols, preferred_element_type=F32).astype(BF16)

    def outer(left, right):
        return lax.dot_general(left, right, (((0,), (0,)), ((), ())), preferred_element_type=F32)

    down_weight_grad = outer(enc_rows, inner_grad)
    up_weight_grad = outer(dec_rows, hidden)
    upsample_grad = jnp.sum(dec_rows.astype(F32), axis=0)
    parts = jnp.stack(
        [
            jnp.dot(enc_rows, down_weight, preferred_element_type=F32),
            jnp.dot(dec_rows, up_weight, preferred_element_type=F32),
        ]
    )
    shares = lax.psum_scatter(parts, "space", scatter_dimension=2, tiled=True)
    inner_low = (shares[0] + down_bias.astype(F32)).astype(BF16)
    hidden_grad = shares[1].astype(BF16)
    down_proj_grad = outer(inner_low, sign_all)
    up_proj_grad = outer(hidden_grad, signs)
    up_bias_grad = jnp.sum(hidden_grad.astype(F32), axis=0)
    inner_share = lax.dynamic_slice_in_dim(inner_grad, space * lanes, lanes, 1)
    down_bias_grad = jnp.sum(inner_share.astype(F32), axis=0)

    one = lambda v: channel_sums(v.astype(F32))[None] * first_space
    small_grads = jnp.concatenate(
        [
            spread_lanes(enc_sums_one[1:]),
            spread_lanes(enc_sums_two[1:]),
            spread_lanes(enc_sums_one[:1]),
            spread_lanes(enc_sums_two[:1]),
            one(enc_inner),
            one(enc_cot),
            dec_sums_one[1:],
            spread_lanes(dec_sums_two[1:]),
            dec_sums_one[:1],
            spread_lanes(dec_sums_two[:1]),
            one(dec_inner),
            one(recon_cot),
        ],
        axis=0,
    )
    small_grads = lax.psum(small_grads, ("section", "space"))
    small_grads = lax.dynamic_slice_in_dim(small_grads, space * lanes, lanes, 1)

    return (
        to_output(recon),
        to_output(video_back),
        jnp.stack(grads[:2]),
        small_grads[0:2],
        small_grads[2:6],
        down_weight_grad,
        down_bias_grad,
        down_proj_grad,
        up_proj_grad,
        up_bias_grad,
        up_weight_grad,
        upsample_grad,
        jnp.stack(grads[2:]),
        small_grads[6:8],
        small_grads[8:12],
    )


def solution(mesh):
    lead, second, third = P("space"), P(None, "space"), P(None, None, "space")
    field = P(None, None, "space", None, "section")
    short = mesh.shape["space"] == 8 and mesh.shape["section"] == 4
    return jax.shard_map(
        fast_body if short else general_body,
        mesh=mesh,
        in_specs=(
            third,
            third,
            third,
            second,
            second,
            second,
            lead,
            lead,
            lead,
            lead,
            lead,
            lead,
            lead,
            second,
            second,
            second,
        ),
        out_specs=(
            field,
            field,
            second,
            second,
            second,
            lead,
            lead,
            lead,
            lead,
            lead,
            lead,
            lead,
            second,
            second,
            second,
        ),
        check_vma=False,
    )
```
